128 devices in a mesh: ops: 32 (over x, z, core), sec: 4 (over y).
Axes of the slice: x: 4, y: 4, z: 4, core: 2. Of those that a mesh axis runs over, the one named last changes fastest.
Arguments:
- wave_in: bfloat16 [4096, 4096], P('sec', 'ops'), may hold values from -16 to 16
- row_energy: float32 [4096], P('sec'), may hold values from 1 to 4
- row_operators: bfloat16 [128, 4096, 512], P('ops', 'sec'), may hold values from -0.25 to 0.25
- column_operators: bfloat16 [128, 512, 512], P('ops'), may hold values from -0.52734375 to 0.52734375
- term_count: int32 [32], P('ops'), may hold values from 1 to 4, 48 in all
- source: int32 [128], P('ops'), may hold values from 0 to 7
- target: int32 [128], P('ops'), may hold values from 0 to 7
Outputs:
- wave_next: float32 [4096, 4096], P('sec', 'ops')
- renormalized: float32 [128, 4096, 512], P('ops', 'sec')
- energy: float32 [], replicated
The draws below stay inside these ranges and needn't reach their ends.
Inputs may be any that keep to these rules, and one draw needn't show every extreme that they name: `term_count`: the counts sum to 48, and some index of ops holds exactly 4 terms.
All inputs are finite; a program needn't handle non-finite values. No bound on the sum of `term_count` on one device may be relied on, other than what follows from the above.
Results may differ from the reference program's by a relative error of at most 0.0095.
Values may be sent and summed in bfloat16 or wider, within the bound.
A program may use at most 128 MiB of HBM per device.

```python
import math
import jax
import jax.numpy as jnp
import numpy as np
from jax import lax

SEC = 512
SECTORS = 8
COL_SECTORS = 8
SLOTS = 4
NS_STEPS = 2
ROWS = 4096
COLS = 4096
TERMS = 48
N_OPS = 32


def draw_wave_in(key, part):
    noise_key = jax.random.fold_in(key, 11)
    scale_key = jax.random.fold_in(key, 12)
    row_key = jax.random.fold_in(key, 13)
    col_key = jax.random.fold_in(key, 14)
    mixing_key = jax.random.fold_in(key, 15)
    signal_key = jax.random.fold_in(key, 16)
    weight_key = jax.random.fold_in(key, 17)
    order_key = jax.random.fold_in(key, 18)
    mode_count = SEC // 8
    order = jax.random.permutation(order_key, COL_SECTORS).astype(jnp.int32)
    column = jnp.arange(COLS, dtype=jnp.int32)
    ranked = order[column // SEC] * SEC + column % SEC
    position = ranked.astype(jnp.float32) / COLS
    rough = jax.random.uniform(scale_key, (COLS,), jnp.float32, jnp.log(0.75), jnp.log(1.33))
    row_common = jax.random.normal(row_key, (ROWS, 1), jnp.float32)
    col_common = jax.random.normal(col_key, (1, COLS), jnp.float32)
    mixing = jax.random.normal(mixing_key, (SECTORS, SEC, mode_count), jnp.float32)
    signal = jax.random.normal(signal_key, (SECTORS, mode_count, COLS), jnp.float32)
    weights = jnp.exp(jax.random.uniform(weight_key, (SECTORS, 1, mode_count), jnp.float32, jnp.log(0.3), jnp.log(0.5)))
    modal = jnp.einsum('sik,skc->sic', mixing * weights, signal)
    total = 1.0 + jnp.sum(weights * weights, axis=(1, 2))
    noise = jax.random.normal(noise_key, (SECTORS, SEC, COLS), jnp.float32)
    col_scale = jnp.exp(jnp.log(3.0) * position + rough)
    strength = position
    mixed = ((noise + modal) / jnp.sqrt(total)[:, None, None]).reshape(ROWS, COLS)
    values = col_scale[None, :] * (mixed + strength[None, :] * row_common * col_common)
    return jnp.clip(values, -16.0, 16.0).astype(jnp.bfloat16)


def place_ends(entries, rng, smallest, high):
    longest = entries.shape.index(max(entries.shape))
    spots = []
    for shift in (0, 1):
        where = [jax.random.randint(jax.random.fold_in(rng, axis), (), 0, length) for axis, length in enumerate(entries.shape)]
        where[longest] = (where[longest] + shift) % entries.shape[longest]
        spots.append(tuple(where))
    return entries.at[spots[0]].set(smallest).at[spots[1]].set(high)


def block_scale(key, dims, pieces, least, high):
    loudness, own = 1.0, jax.random.fold_in(key, 6)
    for axis_at, parts in pieces:
        heights = jnp.exp(jax.random.uniform(jax.random.fold_in(own, axis_at), (parts,), jnp.float32, least / len(pieces), high / len(pieces)))
        loudness = loudness * jnp.repeat(heights, dims[axis_at] // parts).reshape([-1 if axis == axis_at else 1 for axis in range(len(dims))])
    return loudness


def split_up(count, total, limit, lean):
    loads = [(1 << 20) // math.isqrt(rank ** lean) + 1 for rank in range(2, count + 1)]
    spare, holding = total - limit - (count - 1), [1] * (count - 1)
    while spare > 0:
        free = [i for i in range(count - 1) if holding[i] < limit]
        whole, budget = sum([loads[i] for i in free]), spare
        for i in free:
            more = min(limit - holding[i], max(1, budget * loads[i] // whole), spare)
            holding[i] = holding[i] + more
            spare = spare - more
    return np.array([limit] + holding)


def uneven_parts(own_key, amount, total, reach, skew):
    if amount == 2:
        one = jax.random.randint(own_key, (), max(1, total - reach), min(reach, total - 1) + 1)
        return jnp.stack([one, total - one])
    lengths = jnp.asarray(split_up(amount, total, reach, skew), jnp.int32)
    twos = (amount - 1) // 2
    giver, receiver = lengths[1:1 + 2 * twos:2], lengths[2:2 + 2 * twos:2]
    room = jnp.minimum(giver - 1, reach - receiver)
    shifted = jax.random.randint(jax.random.fold_in(own_key, 1), (twos,), 0, 1 << 20) % (room + 1)
    lengths = lengths.at[1:1 + 2 * twos:2].set(giver - shifted).at[2:2 + 2 * twos:2].set(receiver + shifted)
    return lengths[jax.random.permutation(jax.random.fold_in(own_key, 2), amount)]


def normal_values(own_key, shape, width, most, cuts=(), kind=jnp.bfloat16):
    factor_of = block_scale(own_key, shape, cuts, -0.22, 0.18) if cuts else 1.0
    values = jax.random.normal(own_key, shape, jnp.float32) * width * factor_of
    return jnp.minimum(jnp.maximum(values, -most), most).astype(kind)


def setup_inputs(seed: int = 0) -> dict:
    streams_of = jax.random.split(jax.random.key(seed), 8)
    wave_in = draw_wave_in(jax.random.fold_in(streams_of[7], 71), 0)
    row_energy = jnp.clip(1.0 + 3.0 * jax.random.uniform(streams_of[1], (ROWS,), jnp.float32) ** block_scale(streams_of[1], (ROWS,), ((0, 4),), -0.2, 0.2), 1.0, 4.0)
    row_operators = normal_values(streams_of[2], (SLOTS * N_OPS, ROWS, SEC), SEC ** -0.5, 0.25, ((0, 32), (1, 4)))
    column_operators = normal_values(streams_of[3], (SLOTS * N_OPS, SEC, SEC), (2.0 / SEC ** 0.5), 0.52734375, ((0, 32),))
    term_count = uneven_parts(streams_of[4], N_OPS, TERMS, SLOTS, 2).astype(jnp.int32)
    source = place_ends(jax.random.randint(streams_of[5], (SLOTS * N_OPS,), 0, COL_SECTORS), jax.random.fold_in(streams_of[5], 1), 0, COL_SECTORS - 1).astype(jnp.int32)
    target = place_ends(jax.random.randint(streams_of[6], (SLOTS * N_OPS,), 0, COL_SECTORS), jax.random.fold_in(streams_of[6], 1), 0, COL_SECTORS - 1).astype(jnp.int32)
    return {"wave_in": wave_in, "row_energy": row_energy, "row_operators": row_operators, "column_operators": column_operators, "term_count": term_count, "source": source, "target": target}


def precise(spec, first, second):
    return jnp.einsum(spec, first, second, precision=lax.Precision.HIGHEST)

def gram_of(first, second):
    return precise('sic,sjc->sij', first, second) / COLS

def inverse_root(gram_matrix):
    scaling = jnp.sqrt(lax.optimization_barrier(jnp.sum(gram_matrix * gram_matrix, axis=(1, 2), keepdims=True)) + 1e-06)
    identity = jnp.broadcast_to(jnp.eye(gram_matrix.shape[-1], dtype=jnp.float32), gram_matrix.shape)
    iterate = gram_matrix / scaling
    inverse = identity
    for repeat in range(NS_STEPS):
        middle = 1.5 * identity - 0.5 * precise('sij,sjk->sik', inverse, iterate)
        iterate = precise('sij,sjk->sik', iterate, middle)
        inverse = precise('sij,sjk->sik', middle, inverse)
    return (inverse, scaling)

def reference(wave_in, row_energy, row_operators, column_operators, term_count, source, target):
    amplitude = wave_in.astype(jnp.float32)

    def add_term(partial_value, term_slot):
        source_col = source[term_slot] * SEC
        target_col = target[term_slot] * SEC
        sector_cols = lax.dynamic_slice_in_dim(wave_in, source_col, SEC, 1).reshape(SECTORS, SEC, SEC).astype(jnp.float32)
        row_blocks = row_operators[term_slot].reshape(SECTORS, SEC, SEC).astype(jnp.float32)
        inner_prod = precise('sij,sjk->sik', row_blocks, sector_cols).astype(jnp.bfloat16)
        contribution = jnp.dot(inner_prod.reshape(ROWS, SEC), column_operators[term_slot], preferred_element_type=jnp.float32)
        existing = lax.dynamic_slice_in_dim(partial_value, target_col, SEC, 1)
        return lax.dynamic_update_slice_in_dim(partial_value, existing + contribution, target_col, 1)

    def per_device(running, device):

        def per_slot(partial_value, offset):
            term_slot = device * SLOTS + offset
            active = offset < term_count[device]
            updated = lax.cond(active, lambda carried: add_term(carried, term_slot), lambda carried: carried, partial_value)
            return (updated, None)
        partial_value, unused = lax.scan(per_slot, jnp.zeros((ROWS, COLS), jnp.float32), jnp.arange(SLOTS, dtype=jnp.int32))
        rounded = lax.optimization_barrier(partial_value.astype(jnp.bfloat16))
        return (running + rounded.astype(jnp.float32), None)
    summed, unused = lax.scan(per_device, jnp.zeros((ROWS, COLS), jnp.float32), jnp.arange(N_OPS, dtype=jnp.int32))
    applied = row_energy[:, None] * amplitude + summed
    energy = jnp.sum(amplitude * applied) / (ROWS * COLS)
    stepped = amplitude + 0.5 * (energy * amplitude - applied)
    stepped3 = stepped.reshape(SECTORS, SEC, COLS)
    gram_one = gram_of(stepped3, stepped3)
    root_one, scale_one = inverse_root(gram_one)
    basis_one = precise('sij,sjc->sic', root_one, stepped3) / jnp.sqrt(scale_one)
    gram_two = gram_of(basis_one, basis_one)
    root_two, scale_two = inverse_root(gram_two)
    wave_next = (precise('sij,sjc->sic', root_two, basis_one) / jnp.sqrt(scale_two)).reshape(ROWS, COLS)
    wave_half = wave_next.astype(jnp.bfloat16)

    def renorm(term_slot):
        active = term_slot % SLOTS < term_count[term_slot // SLOTS]

        def build_block(unused_arg):
            source_block = lax.dynamic_slice_in_dim(wave_half, source[term_slot] * SEC, SEC, 1).reshape(SECTORS, SEC, SEC).astype(jnp.float32)
            target_block = lax.dynamic_slice_in_dim(wave_half, target[term_slot] * SEC, SEC, 1).reshape(SECTORS, SEC, SEC).astype(jnp.float32)
            product = precise('sij,jk->sik', source_block, column_operators[term_slot].astype(jnp.float32)).astype(jnp.bfloat16)
            result = precise('sik,slk->sil', product.astype(jnp.float32), target_block) * SEC ** (-0.5)
            return result.reshape(ROWS, SEC)
        return lax.cond(active, build_block, lambda unused_arg: jnp.zeros((ROWS, SEC), jnp.float32), 0)
    renormalized = lax.map(renorm, jnp.arange(SLOTS * N_OPS, dtype=jnp.int32))
    return (wave_next, renormalized, energy)
```

```python
import functools

import jax
import jax.numpy as jnp
from jax import lax
from jax.experimental import pallas as pl
from jax.experimental.pallas import tpu as pltpu
from jax.sharding import Mesh
from jax.sharding import PartitionSpec as P

SEC = 512
COLS = 4096
ENTRIES = 4096 * 4096
CHIPS = 16
WIDE = 256
HALF = 256
QUARTER = 128
MIB = 1 << 20
MESH = pl.DeviceIdType.MESH
OPS = ("x", "z", "core")
F32 = jnp.float32
BF16 = jnp.bfloat16


def turn(place, by):
    return lax.rem(place + (by + 4), 4)


def push(src, dst, send, recv, to):
    return pltpu.make_async_remote_copy(
        src_ref=src, dst_ref=dst, send_sem=send, recv_sem=recv, device_id=to, device_id_type=MESH
    )


def greet(peers):
    barrier = pltpu.get_barrier_semaphore()
    for peer in peers:
        pl.semaphore_signal(barrier, inc=1, device_id=peer, device_id_type=MESH)
    pl.semaphore_wait(barrier, len(peers))


def all_blocks(buf, x, z, send, recv):
    names = (("x", "z"), ("z", "x"))
    places = ((x, z), (z, x))

    def block(h, pa, pb):
        return pa * 4 + pb if h == 0 else pb * 4 + pa

    def view(h, pa, pb, part):
        rows = pl.ds(h * HALF, HALF) if part is None else pl.ds(h * HALF + part * QUARTER, QUARTER)
        return buf.at[block(h, pa, pb), rows, :]

    def copy(h, j, pa, pb, part, axis, by):
        ref = view(h, pa, pb, part)
        to = {names[h][axis]: turn(places[h][axis], by)}
        return push(ref, ref, send.at[h, j], recv.at[h, j], to)

    def order(h):
        p = places[h][0]
        return (p, turn(p, -1), turn(p, 1), turn(p, 2))

    sent = []

    def go(*what):
        one = copy(*what)
        one.start()
        sent.append(one)

    def arrived(h, j, pa, pb, part):
        copy(h, j, pa, pb, part, 0, 1).wait_recv()

    for h in (0, 1):
        p, q = places[h]
        go(h, 0, p, q, None, 0, 1)
        go(h, 1, p, q, None, 0, -1)
    for h in (0, 1):
        p, q = places[h]
        go(h, 4, p, q, None, 1, 1)
        go(h, 8, p, q, None, 1, -1)
    yield
    for h in (0, 1):
        p, q = places[h]
        left, right = turn(p, -1), turn(p, 1)
        arrived(h, 0, left, q, None)
        go(h, 2, left, q, 0, 0, 1)
        go(h, 5, left, q, None, 1, 1)
        go(h, 9, left, q, None, 1, -1)
        arrived(h, 1, right, q, None)
        go(h, 3, right, q, 1, 0, -1)
        go(h, 6, right, q, None, 1, 1)
        go(h, 10, right, q, None, 1, -1)
    yield

    def onward(h, i):
        pa, q = order(h)[i], places[h][1]
        arrived(h, 4 + i, pa, turn(q, -1), None)
        go(h, 12 + i, pa, turn(q, -1), 0, 1, 1)
        arrived(h, 8 + i, pa, turn(q, 1), None)
        go(h, 16 + i, pa, turn(q, 1), 1, 1, -1)

    for h in (0, 1):
        onward(h, 0)
    yield
    for h in (0, 1):
        p, q = places[h]
        far = turn(p, 2)
        arrived(h, 2, far, q, 0)
        arrived(h, 3, far, q, 1)
        go(h, 7, far, q, None, 1, 1)
        go(h, 11, far, q, None, 1, -1)
    yield
    for i in (1, 2, 3):
        for h in (0, 1):
            onward(h, i)
        yield
    for i in range(4):
        for h in (0, 1):
            pa, far = order(h)[i], turn(places[h][1], 2)
            arrived(h, 12 + i, pa, far, 0)
            arrived(h, 16 + i, pa, far, 1)
    for one in sent:
        one.wait_send()


def ring_peers(x, z):
    return [{"x": turn(x, 1)}, {"x": turn(x, -1)}, {"z": turn(z, 1)}, {"z": turn(z, -1)}]


def gather_kernel(
    wave, row_ops, col_ops, table, wide, row_sib, col_sib, table_sib, send, recv, swap_send, swap_recv, own_sem
):
    x, z, c = lax.axis_index("x"), lax.axis_index("z"), lax.axis_index("core")
    sib = {"core": 1 - c}
    greet(ring_peers(x, z) + [sib])
    b = x * 4 + z
    mine = pl.ds(pl.multiple_of(c * SEC, SEC), SEC)
    other = pl.ds(pl.multiple_of((1 - c) * SEC, SEC), SEC)
    columns = pl.ds(pl.multiple_of(c * 128, 128), 128)
    other_columns = pl.ds(pl.multiple_of((1 - c) * 128, 128), 128)
    own = pltpu.make_async_copy(wave.at[mine, :], wide.at[b, :, columns], own_sem)
    swaps = [
        push(wave.at[other, :], wide.at[b, :, columns], swap_send.at[0], swap_recv.at[0], sib),
        push(table, table_sib, swap_send.at[1], swap_recv.at[1], sib),
        push(row_ops.at[:, other, :], row_sib, swap_send.at[2], swap_recv.at[2], sib),
        push(col_ops, col_sib, swap_send.at[3], swap_recv.at[3], sib),
    ]
    swaps[0].start()
    own.start()
    own.wait()
    push(wave.at[other, :], wide.at[b, :, other_columns], swap_send.at[0], swap_recv.at[0], sib).wait_recv()
    steps = all_blocks(wide, x, z, send, recv)
    next(steps)
    for swap in swaps[1:]:
        swap.start()
    for step in steps:
        del step
    swaps[0].wait_send()
    for swap in swaps[1:]:
        swap.wait()


def gather(wave, row_ops, col_ops, table):
    hbm = pl.BlockSpec(memory_space=pl.ANY)
    return pl.pallas_call(
        gather_kernel,
        out_shape=(
            jax.ShapeDtypeStruct((CHIPS, SEC, WIDE), BF16),
            jax.ShapeDtypeStruct((4, SEC, SEC), BF16),
            jax.ShapeDtypeStruct((4, SEC, SEC), BF16),
            jax.ShapeDtypeStruct((8, 128), jnp.int32),
        ),
        in_specs=[hbm] * 4,
        out_specs=(hbm,) * 4,
        scratch_shapes=[
            pltpu.SemaphoreType.DMA((2, 20)),
            pltpu.SemaphoreType.DMA((2, 20)),
            pltpu.SemaphoreType.DMA((4,)),
            pltpu.SemaphoreType.DMA((4,)),
            pltpu.SemaphoreType.DMA(()),
        ],
        compiler_params=pltpu.CompilerParams(collective_id=0, has_side_effects=True),
        name="gather",
    )(wave, row_ops, col_ops, table)


def dot(a, b):
    return jnp.dot(a, b, preferred_element_type=F32)


def dot_t(a, b):
    return lax.dot_general(a, b, (((1,), (1,)), ((), ())), preferred_element_type=F32)


def terms_kernel(
    table, table_sib, row_ops, row_sib, col_ops, col_sib, wide, out, wide_v, row_v, col_v, total, wide_sem, row_sem, col_sem
):
    c = table[0, 9]
    mine = pl.ds(pl.multiple_of(c * SEC, SEC), SEC)
    counts = (table[0, 0], table_sib[0, 0])
    load = pltpu.make_async_copy(wide, wide_v, wide_sem)
    load.start()

    def copies(side, k):
        slot = side * 4 + k
        rows = (row_ops.at[k, mine, :], row_sib.at[k])[side]
        cols = (col_ops.at[k], col_sib.at[k])[side]
        return (
            pltpu.make_async_copy(rows, row_v.at[slot], row_sem.at[slot]),
            pltpu.make_async_copy(cols, col_v.at[slot], col_sem.at[slot]),
        )

    for k in range(4):
        for side in (0, 1):

            @pl.when(k < counts[side])
            def start(side=side, k=k):
                for one in copies(side, k):
                    one.start()

    def clear(i, carry):
        total[i] = jnp.zeros((SEC, WIDE), F32)
        return carry

    lax.fori_loop(0, CHIPS, clear, 0)
    load.wait()
    for side in (0, 1):
        this = (table, table_sib)[side]

        def term(k, carry, side=side, this=this):
            slot = side * 4 + k
            src = this[0, 1 + k] * 2
            tgt = this[0, 5 + k] * 2
            for one in copies(side, k):
                one.wait()
            rows = row_v[slot]
            first = dot(rows, wide_v[src]).astype(BF16)
            second = dot(rows, wide_v[src + 1]).astype(BF16)
            for part in (0, 1):
                where = pl.ds(part * WIDE, WIDE)
                total[tgt + part] += dot(first, col_v[slot, :WIDE, where]) + dot(second, col_v[slot, WIDE:, where])
            return carry

        lax.fori_loop(0, counts[side], term, 0)

    def finish(i, carry):
        out[i] = total[i].astype(BF16)
        return carry

    lax.fori_loop(0, CHIPS, finish, 0)


def terms(table, table_sib, row_ops, row_sib, col_ops, col_sib, wide):
    hbm = pl.BlockSpec(memory_space=pl.ANY)
    smem = pl.BlockSpec(memory_space=pltpu.SMEM)
    return pl.pallas_call(
        terms_kernel,
        out_shape=jax.ShapeDtypeStruct((CHIPS, SEC, WIDE), BF16),
        in_specs=[smem, smem] + [hbm] * 5,
        out_specs=pl.BlockSpec(memory_space=pltpu.VMEM),
        scratch_shapes=[
            pltpu.VMEM((CHIPS, SEC, WIDE), BF16),
            pltpu.VMEM((8, SEC, SEC), BF16),
            pltpu.VMEM((8, SEC, SEC), BF16),
            pltpu.VMEM((CHIPS, SEC, WIDE), F32),
            pltpu.SemaphoreType.DMA(()),
            pltpu.SemaphoreType.DMA((8,)),
            pltpu.SemaphoreType.DMA((8,)),
        ],
        compiler_params=pltpu.CompilerParams(vmem_limit_bytes=48 * MIB),
        name="terms",
    )(table, table_sib, row_ops, row_sib, col_ops, col_sib, wide)


def rough(a, b):
    return dot(a.astype(BF16), b.astype(BF16))


def reduce_blocks(part, near, whole, near2, whole2, total, x, z, send, recv, send2, recv2):
    names = (("z", "x"), ("x", "z"))
    places = ((z, x), (x, z))

    def block(h, pa, pb):
        return pb * 4 + pa if h == 0 else pa * 4 + pb

    def rows(h, half):
        return pl.ds(h * HALF + half * QUARTER, QUARTER)

    def local(half):
        return pl.ds(half * QUARTER, QUARTER)

    def order(h):
        q = places[h][1]
        return (turn(q, 2), turn(q, 1), turn(q, -1), q)

    sent = []

    def go(one):
        one.start()
        sent.append(one)

    def near_copy(h, d, i):
        p = places[h][0]
        src = part.at[block(h, turn(p, 2), order(h)[i]), rows(h, d), :]
        to = {names[h][0]: turn(p, 1 - 2 * d)}
        return push(src, near.at[h, d, i], send.at[h, d, i], recv.at[h, d, i], to)

    def whole_copy(h, d, i, half):
        p = places[h][0]
        src = part.at[block(h, turn(p, 1 - 2 * d), order(h)[i]), rows(h, half), :]
        to = {names[h][0]: turn(p, 1 - 2 * d)}
        j = 2 + 2 * d + half
        return push(src, whole.at[h, d, i, local(half), :], send.at[h, j, i], recv.at[h, j, i], to)

    def near2_copy(h, d):
        p, q = places[h]
        src = part.at[block(h, p, turn(q, 2)), rows(h, d), :]
        return push(src, near2.at[h, d], send2.at[h, d], recv2.at[h, d], {names[h][1]: turn(q, 1 - 2 * d)})

    def whole2_copy(h, d, half):
        p, q = places[h]
        j = 2 + 2 * d + half
        src = part.at[block(h, p, turn(q, 1 - 2 * d)), rows(h, half), :]
        to = {names[h][1]: turn(q, 1 - 2 * d)}
        return push(src, whole2.at[h, d, local(half), :], send2.at[h, j], recv2.at[h, j], to)

    for i in range(4):
        for h in (0, 1):
            for d in (0, 1):
                go(near_copy(h, d, i))
    for i in range(4):
        for h in (0, 1):
            for d in (0, 1):
                go(whole_copy(h, d, i, 1 - d))
    for i in range(4):
        for h in (0, 1):
            p = places[h][0]
            for d in (0, 1):
                near_copy(h, d, i).wait_recv()
                at = block(h, turn(p, 1 - 2 * d), order(h)[i])
                both = part[at, rows(h, d), :].astype(F32) + near[h, d, i].astype(F32)
                part[at, rows(h, d), :] = both.astype(BF16)
                go(whole_copy(h, d, i, d))
    for i in range(4):
        for h in (0, 1):
            p, q = places[h]
            for d in (0, 1):
                for half in (0, 1):
                    whole_copy(h, d, i, half).wait_recv()
            at = block(h, p, order(h)[i])
            here = pl.ds(h * HALF, HALF)
            done = part[at, here, :].astype(F32) + whole[h, 0, i].astype(F32) + whole[h, 1, i].astype(F32)
            if i == 3:
                total[here, :] = done
            else:
                part[at, here, :] = done.astype(BF16)
            if i == 0:
                go(near2_copy(h, 0))
                go(near2_copy(h, 1))
            if i == 1:
                go(whole2_copy(h, 0, 1))
            if i == 2:
                go(whole2_copy(h, 1, 0))
    for h in (0, 1):
        p, q = places[h]
        for d in (0, 1):
            near2_copy(h, d).wait_recv()
            at = block(h, p, turn(q, 1 - 2 * d))
            both = part[at, rows(h, d), :].astype(F32) + near2[h, d].astype(F32)
            part[at, rows(h, d), :] = both.astype(BF16)
            go(whole2_copy(h, d, d))
    for h in (0, 1):
        for d in (0, 1):
            for half in (0, 1):
                whole2_copy(h, d, half).wait_recv()
        here = pl.ds(h * HALF, HALF)
        total[here, :] += whole2[h, 0].astype(F32) + whole2[h, 1].astype(F32)
    for one in sent:
        one.wait_send()


def frobenius(a):
    return jnp.sqrt(jnp.sum(a * a, axis=(0, 1), keepdims=True) + 1e-06)


def step_kernel(
    part_h, wide_h, energy_col,
    stepped_o, root_o, level_o, exact_o, energy_o,
    part, near, whole, near2, whole2, total, wide, summed, stepped, gram, my, mm, mu, mz, roots, level_two, exact, scalars,
    rs_send, rs_recv, rs2_send, rs2_recv, ag_send, ag_recv, en_send, en_recv, st_send, st_recv, st_own,
    end_send, end_recv, own_sem,
):
    x, z, c, y = lax.axis_index("x"), lax.axis_index("z"), lax.axis_index("core"), lax.axis_index("sec")
    b = x * 4 + z
    sib = {"core": 1 - c}
    load = pltpu.make_async_copy(part_h, part, own_sem.at[0])
    load_wide = pltpu.make_async_copy(wide_h, wide, own_sem.at[1])
    load.start()
    greet(
        ring_peers(x, z)
        + [{"x": turn(x, 2)}, {"z": turn(z, 2)}, sib, {"sec": turn(y, 1)}, {"sec": turn(y, 2)}, {"sec": turn(y, -1)}]
    )
    load.wait()
    load_wide.start()
    reduce_blocks(part, near, whole, near2, whole2, total, x, z, rs_send, rs_recv, rs2_send, rs2_recv)
    summed[b] = total[...].astype(BF16)
    steps = all_blocks(summed, x, z, ag_send, ag_recv)
    next(steps)
    load_wide.wait()
    level = energy_col[pl.ds(pl.multiple_of(c * SEC, SEC), SEC), :]
    amplitude = wide[b].astype(F32)
    applied = level * amplitude + total[...]
    share = jnp.sum(amplitude * applied, axis=(0, 1), keepdims=True)

    stages = (("sec", y, 4), ("x", x, 4), ("z", z, 4), ("core", c, 2))

    def energy_copies(s):
        name, place, size = stages[s]
        for hop in range(1, size):
            to = {name: lax.rem(place + hop, size)}
            src = lax.rem(place + (size - hop), size)
            yield (
                push(scalars.at[s, place], scalars.at[s, place], en_send.at[s, hop], en_recv.at[s, hop], to),
                push(scalars.at[s, src], scalars.at[s, src], en_send.at[s, hop], en_recv.at[s, hop], to),
            )

    for s in range(4):
        place, size = stages[s][1:]
        scalars[s, place] = jnp.broadcast_to(share, (8, 128))
        for out, unused in energy_copies(s):
            out.start()
        next(steps, None)
        for out, arriving in energy_copies(s):
            arriving.wait_recv()
            out.wait_send()
        share = scalars[s, 0] + scalars[s, 1]
        if size == 4:
            share = (share + scalars[s, 2]) + scalars[s, 3]
        share = share[0:1, 0:1]
    energy = share * (1.0 / ENTRIES)
    energy_o[...] = jnp.broadcast_to(energy, (8, 128))
    for step in steps:
        del step

    own = amplitude + 0.5 * (energy * amplitude - applied)
    exact[0] = own[:, :128]
    exact[1] = own[:, 128:]
    mine = pl.ds(pl.multiple_of(c * SEC, SEC), SEC)
    exact_send = push(exact.at[1 - c], exact_o.at[mine, :], end_send.at[0], end_recv.at[0], sib)
    exact_own = pltpu.make_async_copy(exact.at[c], exact_o.at[mine, :], own_sem.at[2])
    exact_send.start()
    exact_own.start()

    def out_block(i):
        return (
            push(stepped.at[i], stepped_o.at[c, i], st_send.at[i], st_recv.at[i], sib),
            pltpu.make_async_copy(stepped.at[i], stepped_o.at[c, i], st_own.at[i]),
        )

    gram[...] = jnp.zeros((SEC, SEC), F32)

    def one_block(i, carry):
        part_of = wide[i].astype(F32)
        value = part_of + 0.5 * (energy * part_of - (level * part_of + summed[i].astype(F32)))
        value = value.astype(BF16)
        stepped[i] = value
        for one in out_block(i):
            one.start()
        gram[...] += dot_t(value, value)
        return carry

    lax.fori_loop(0, CHIPS, one_block, 0)

    def root(y_ref, d_ref, again):
        my[...] = 1.5 * y_ref[...] - 0.5 * rough(y_ref[...], y_ref[...])
        mu[...] = 1.5 * my[...] - 0.5 * rough(y_ref[...], my[...])
        d_ref[...] = 0.25 * rough(mu[...], y_ref[...]) - 0.75 * (y_ref[...] + mu[...])
        if again:
            y_ref[...] = 1.5 * my[...] - 0.5 * rough(my[...], mu[...])

    gram_one = gram[...] * (1.0 / COLS)
    scale_one = frobenius(gram_one)
    gram[...] = gram_one / scale_one
    root(gram, mz, True)
    gram_two = 2.25 * gram[...] + rough(mz[...], gram[...])
    scale_two = frobenius(gram_two)
    gram[...] = gram_two / scale_two
    root(gram, mm, False)
    size = jnp.sqrt(scale_one) * jnp.sqrt(scale_two)
    roots[...] = ((2.25 * (mz[...] + mm[...]) + rough(mm[...], mz[...])) / size).astype(BF16)
    level_two[...] = jnp.broadcast_to(2.25 * 2.25 / size, (8, 128))
    root_send = push(roots, root_o.at[c], end_send.at[1], end_recv.at[1], sib)
    root_own = pltpu.make_async_copy(roots, root_o.at[c], own_sem.at[3])
    level_send = push(level_two, level_o.at[c], end_send.at[2], end_recv.at[2], sib)
    level_own = pltpu.make_async_copy(level_two, level_o.at[c], own_sem.at[4])
    level_send.start()
    level_own.start()
    root_send.start()
    root_own.start()

    def block_done(i, carry):
        going, staying = out_block(i)
        going.wait_send()
        staying.wait()
        push(stepped.at[i], stepped_o.at[1 - c, i], st_send.at[i], st_recv.at[i], sib).wait_recv()
        return carry

    lax.fori_loop(0, CHIPS, block_done, 0)
    other = pl.ds(pl.multiple_of((1 - c) * SEC, SEC), SEC)
    exact_send.wait_send()
    exact_own.wait()
    push(exact.at[1 - c], exact_o.at[other, :], end_send.at[0], end_recv.at[0], sib).wait_recv()
    root_send.wait_send()
    root_own.wait()
    push(roots, root_o.at[1 - c], end_send.at[1], end_recv.at[1], sib).wait_recv()
    level_send.wait_send()
    level_own.wait()
    push(level_two, level_o.at[1 - c], end_send.at[2], end_recv.at[2], sib).wait_recv()


def step(part, wide, energy_col):
    hbm = pl.BlockSpec(memory_space=pl.ANY)
    vmem = pl.BlockSpec(memory_space=pltpu.VMEM)
    square = pltpu.VMEM((SEC, SEC), F32)
    blocks = pltpu.VMEM((CHIPS, SEC, WIDE), BF16)
    dma = pltpu.SemaphoreType.DMA
    return pl.pallas_call(
        step_kernel,
        out_shape=(
            jax.ShapeDtypeStruct((2, CHIPS, SEC, WIDE), BF16),
            jax.ShapeDtypeStruct((2, SEC, SEC), BF16),
            jax.ShapeDtypeStruct((2, 8, 128), F32),
            jax.ShapeDtypeStruct((2 * SEC, 128), F32),
            jax.ShapeDtypeStruct((8, 128), F32),
        ),
        in_specs=[hbm, hbm, vmem],
        out_specs=(hbm, hbm, hbm, hbm, vmem),
        scratch_shapes=[
            blocks,
            pltpu.VMEM((2, 2, 4, QUARTER, WIDE), BF16),
            pltpu.VMEM((2, 2, 4, HALF, WIDE), BF16),
            pltpu.VMEM((2, 2, QUARTER, WIDE), BF16),
            pltpu.VMEM((2, 2, HALF, WIDE), BF16),
            pltpu.VMEM((SEC, WIDE), F32),
            blocks,
            blocks,
            blocks,
            square,
            square,
            square,
            square,
            square,
            pltpu.VMEM((SEC, SEC), BF16),
            pltpu.VMEM((8, 128), F32),
            pltpu.VMEM((2, SEC, 128), F32),
            pltpu.VMEM((4, 4, 8, 128), F32),
            dma((2, 6, 4)),
            dma((2, 6, 4)),
            dma((2, 6)),
            dma((2, 6)),
            dma((2, 20)),
            dma((2, 20)),
            dma((4, 4)),
            dma((4, 4)),
            dma((CHIPS,)),
            dma((CHIPS,)),
            dma((CHIPS,)),
            dma((3,)),
            dma((3,)),
            dma((5,)),
        ],
        compiler_params=pltpu.CompilerParams(
            collective_id=1, has_side_effects=True, vmem_limit_bytes=56 * MIB
        ),
        name="step",
    )(part, wide, energy_col)


def renorm_kernel(table, src_block, tgt_block, cols, root, level, exact, out, wave_o):
    k = pl.program_id(0)
    scale = level[0, 0:1, 0:1]

    @pl.when(k == 0)
    def first():
        wave_o[...] = scale * exact[...] + dot(root[0], exact[...].astype(BF16))

    @pl.when(k < table[0])
    def live():
        product = None
        for part in (0, 1):
            block = src_block[0, part]
            half = (scale * block.astype(F32) + dot(root[0], block)).astype(BF16)
            added = dot(half, cols[0, part * WIDE : (part + 1) * WIDE, :])
            product = added if product is None else product + added
        product = product.astype(BF16)
        total = None
        for part in (0, 1):
            block = tgt_block[0, part]
            half = (scale * block.astype(F32) + dot(root[0], block)).astype(BF16)
            added = dot_t(product[:, part * WIDE : (part + 1) * WIDE], half)
            total = added if total is None else total + added
        out[0] = total * SEC ** (-0.5)

    @pl.when(k >= table[0])
    def empty():
        out[...] = jnp.zeros_like(out)


def renorm(table, stepped, cols, root, level, exact):
    def slot(k, table):
        return jnp.minimum(k, table[0] - 1)

    def sector(k, s, table):
        return jnp.where(k < table[0], s, 1)

    def src_at(k, s, table):
        return (sector(k, s, table), table[1 + slot(k, table)], 0, 0)

    def tgt_at(k, s, table):
        return (sector(k, s, table), table[5 + slot(k, table)], 0, 0)

    return pl.pallas_call(
        renorm_kernel,
        out_shape=(
            jax.ShapeDtypeStruct((4, 2 * SEC, SEC), F32),
            jax.ShapeDtypeStruct((2 * SEC, 128), F32),
        ),
        grid_spec=pltpu.PrefetchScalarGridSpec(
            num_scalar_prefetch=1,
            grid=(4, 2),
            in_specs=[
                pl.BlockSpec((1, 2, SEC, WIDE), src_at),
                pl.BlockSpec((1, 2, SEC, WIDE), tgt_at),
                pl.BlockSpec((1, SEC, SEC), lambda k, s, table: (slot(k, table), 0, 0)),
                pl.BlockSpec((1, SEC, SEC), lambda k, s, table: (sector(k, s, table), 0, 0)),
                pl.BlockSpec((1, 8, 128), lambda k, s, table: (sector(k, s, table), 0, 0)),
                pl.BlockSpec((SEC, 128), lambda k, s, table: (jnp.where(k == 0, s, 1), 0)),
            ],
            out_specs=[
                pl.BlockSpec((1, SEC, SEC), lambda k, s, table: (k, s, 0)),
                pl.BlockSpec((SEC, 128), lambda k, s, table: (jnp.where(k == 0, s, 1), 0)),
            ],
        ),
        compiler_params=pltpu.CompilerParams(vmem_limit_bytes=32 * MIB),
        name="renorm",
    )(table, stepped, stepped, cols, root, level, exact)


def on_device(wave_in, row_energy, row_operators, column_operators, term_count, source, target):
    core = lax.axis_index("core").astype(jnp.int32).reshape(1)
    numbers = jnp.concatenate([term_count, source, target, core])
    table = jnp.pad(numbers.reshape(1, 10), ((0, 7), (0, 118)))
    wide, row_sib, col_sib, table_sib = gather(wave_in, row_operators, column_operators, table)
    part = terms(table, table_sib, row_operators, row_sib, column_operators, col_sib, wide)
    stepped, root, level, exact, energy = step(part, wide, row_energy.reshape(-1, 1))
    renormalized, wave_next = renorm(numbers, stepped, column_operators, root, level, exact)
    return (wave_next, renormalized, energy[0, 0])


def solution(mesh):
    torus = Mesh(mesh.devices.reshape(4, 4, 2, mesh.shape["sec"]), ("x", "z", "core", "sec"))
    return jax.shard_map(
        on_device,
        mesh=torus,
        in_specs=(
            P("sec", OPS),
            P("sec"),
            P(OPS, "sec", None),
            P(OPS, None, None),
            P(OPS),
            P(OPS),
            P(OPS),
        ),
        out_specs=(P("sec", OPS), P(OPS, "sec", None), P()),
        check_vma=False,
    )
```

```python
import functools

import jax
import jax.numpy as jnp
from jax import lax
from jax.experimental import pallas as pl
from jax.experimental.pallas import tpu as pltpu
from jax.sharding import Mesh
from jax.sharding import PartitionSpec as P

SEC = 512
COLS = 4096
ENTRIES = 4096 * 4096
CHIPS = 16
WIDE = 256
HALF = 256
QUARTER = 128
MIB = 1 << 20
MESH = pl.DeviceIdType.MESH
OPS = ("x", "z", "core")
F32 = jnp.float32
BF16 = jnp.bfloat16


def turn(place, by):
    return lax.rem(place + (by + 4), 4)


def push(src, dst, send, recv, to):
    return pltpu.make_async_remote_copy(
        src_ref=src, dst_ref=dst, send_sem=send, recv_sem=recv, device_id=to, device_id_type=MESH
    )


def greet(peers):
    barrier = pltpu.get_barrier_semaphore()
    for peer in peers:
        pl.semaphore_signal(barrier, inc=1, device_id=peer, device_id_type=MESH)
    pl.semaphore_wait(barrier, len(peers))


def all_blocks(buf, x, z, send, recv):
    names = (("x", "z"), ("z", "x"))
    places = ((x, z), (z, x))

    def block(h, pa, pb):
        return pa * 4 + pb if h == 0 else pb * 4 + pa

    def view(h, pa, pb, part):
        rows = pl.ds(h * HALF, HALF) if part is None else pl.ds(h * HALF + part * QUARTER, QUARTER)
        return buf.at[block(h, pa, pb), rows, :]

    def copy(h, j, pa, pb, part, axis, by):
        ref = view(h, pa, pb, part)
        to = {names[h][axis]: turn(places[h][axis], by)}
        return push(ref, ref, send.at[h, j], recv.at[h, j], to)

    def order(h):
        p = places[h][0]
        return (p, turn(p, -1), turn(p, 1), turn(p, 2))

    sent = []

    def go(*what):
        one = copy(*what)
        one.start()
        sent.append(one)

    def arrived(h, j, pa, pb, part):
        copy(h, j, pa, pb, part, 0, 1).wait_recv()

    for h in (0, 1):
        p, q = places[h]
        go(h, 0, p, q, None, 0, 1)
        go(h, 1, p, q, None, 0, -1)
    for h in (0, 1):
        p, q = places[h]
        go(h, 4, p, q, None, 1, 1)
        go(h, 8, p, q, None, 1, -1)
    yield
    for h in (0, 1):
        p, q = places[h]
        left, right = turn(p, -1), turn(p, 1)
        arrived(h, 0, left, q, None)
        go(h, 2, left, q, 0, 0, 1)
        go(h, 5, left, q, None, 1, 1)
        go(h, 9, left, q, None, 1, -1)
        arrived(h, 1, right, q, None)
        go(h, 3, right, q, 1, 0, -1)
        go(h, 6, right, q, None, 1, 1)
        go(h, 10, right, q, None, 1, -1)
    yield

    def onward(h, i):
        pa, q = order(h)[i], places[h][1]
        arrived(h, 4 + i, pa, turn(q, -1), None)
        go(h, 12 + i, pa, turn(q, -1), 0, 1, 1)
        arrived(h, 8 + i, pa, turn(q, 1), None)
        go(h, 16 + i, pa, turn(q, 1), 1, 1, -1)

    for h in (0, 1):
        onward(h, 0)
    yield
    for h in (0, 1):
        p, q = places[h]
        far = turn(p, 2)
        arrived(h, 2, far, q, 0)
        arrived(h, 3, far, q, 1)
        go(h, 7, far, q, None, 1, 1)
        go(h, 11, far, q, None, 1, -1)
    yield
    for i in (1, 2, 3):
        for h in (0, 1):
            onward(h, i)
        yield
    for i in range(4):
        for h in (0, 1):
            pa, far = order(h)[i], turn(places[h][1], 2)
            arrived(h, 12 + i, pa, far, 0)
            arrived(h, 16 + i, pa, far, 1)
    for one in sent:
        one.wait_send()


def ring_peers(x, z):
    return [{"x": turn(x, 1)}, {"x": turn(x, -1)}, {"z": turn(z, 1)}, {"z": turn(z, -1)}]


def gather_kernel(
    wave, row_ops, col_ops, count, source, target, wide, row_sib, col_sib, table_sib,
    table, send, recv, swap_send, swap_recv, own_sem,
):
    x, z, c = lax.axis_index("x"), lax.axis_index("z"), lax.axis_index("core")
    sib = {"core": 1 - c}
    greet(ring_peers(x, z) + [sib])
    b = x * 4 + z
    mine = pl.ds(pl.multiple_of(c * SEC, SEC), SEC)
    other = pl.ds(pl.multiple_of((1 - c) * SEC, SEC), SEC)
    columns = pl.ds(pl.multiple_of(c * 128, 128), 128)
    other_columns = pl.ds(pl.multiple_of((1 - c) * 128, 128), 128)
    own = pltpu.make_async_copy(wave.at[mine, :], wide.at[b, :, columns], own_sem)
    swaps = [
        push(wave.at[other, :], wide.at[b, :, columns], swap_send.at[0], swap_recv.at[0], sib),
        push(table, table_sib, swap_send.at[1], swap_recv.at[1], sib),
        push(row_ops.at[:, other, :], row_sib, swap_send.at[2], swap_recv.at[2], sib),
        push(col_ops, col_sib, swap_send.at[3], swap_recv.at[3], sib),
    ]
    swaps[0].start()
    own.start()
    lane = lax.broadcasted_iota(jnp.int32, (8, 128), 1)
    numbers = jnp.where(lane == 0, count[0], 0)
    for k in range(4):
        numbers = jnp.where(lane == 1 + k, source[k], numbers)
        numbers = jnp.where(lane == 5 + k, target[k], numbers)
    table[...] = numbers
    own.wait()
    push(wave.at[other, :], wide.at[b, :, other_columns], swap_send.at[0], swap_recv.at[0], sib).wait_recv()
    steps = all_blocks(wide, x, z, send, recv)
    next(steps)
    for swap in swaps[1:]:
        swap.start()
    for step in steps:
        del step
    swaps[0].wait_send()
    for swap in swaps[1:]:
        swap.wait()


def gather(wave, row_ops, col_ops, count, source, target):
    hbm = pl.BlockSpec(memory_space=pltpu.HBM)
    smem = pl.BlockSpec(memory_space=pltpu.SMEM)
    return pl.pallas_call(
        gather_kernel,
        out_shape=(
            jax.ShapeDtypeStruct((CHIPS, SEC, WIDE), BF16),
            jax.ShapeDtypeStruct((4, SEC, SEC), BF16),
            jax.ShapeDtypeStruct((4, SEC, SEC), BF16),
            jax.ShapeDtypeStruct((8, 128), jnp.int32),
        ),
        in_specs=[hbm] * 3 + [smem] * 3,
        out_specs=(hbm,) * 4,
        scratch_shapes=[
            pltpu.VMEM((8, 128), jnp.int32),
            pltpu.SemaphoreType.DMA((2, 20)),
            pltpu.SemaphoreType.DMA((2, 20)),
            pltpu.SemaphoreType.DMA((4,)),
            pltpu.SemaphoreType.DMA((4,)),
            pltpu.SemaphoreType.DMA(()),
        ],
        compiler_params=pltpu.CompilerParams(collective_id=0, has_side_effects=True),
        name="gather",
    )(wave, row_ops, col_ops, count, source, target)


def dot(a, b):
    return jnp.dot(a, b, preferred_element_type=F32)


def dot_t(a, b):
    return lax.dot_general(a, b, (((1,), (1,)), ((), ())), preferred_element_type=F32)


def terms_kernel(
    count, source, target, table_sib, row_ops, row_sib, col_ops, col_sib, wide,
    out, wide_v, row_v, col_v, total, wide_sem, row_sem, col_sem,
):
    c = lax.axis_index("core")
    mine = pl.ds(pl.multiple_of(c * SEC, SEC), SEC)
    counts = (count[0], table_sib[0, 0])
    load = pltpu.make_async_copy(wide, wide_v, wide_sem)
    load.start()

    def copies(side, k):
        slot = side * 4 + k
        rows = (row_ops.at[k, mine, :], row_sib.at[k])[side]
        cols = (col_ops.at[k], col_sib.at[k])[side]
        return (
            pltpu.make_async_copy(rows, row_v.at[slot], row_sem.at[slot]),
            pltpu.make_async_copy(cols, col_v.at[slot], col_sem.at[slot]),
        )

    for k in range(4):
        for side in (0, 1):

            @pl.when(k < counts[side])
            def start(side=side, k=k):
                for one in copies(side, k):
                    one.start()

    def clear(i, carry):
        total[i] = jnp.zeros((SEC, WIDE), F32)
        return carry

    lax.fori_loop(0, CHIPS, clear, 0)
    load.wait()
    for side in (0, 1):

        def term(k, carry, side=side):
            slot = side * 4 + k
            src = (table_sib[0, 1 + k] if side else source[k]) * 2
            tgt = (table_sib[0, 5 + k] if side else target[k]) * 2
            for one in copies(side, k):
                one.wait()
            rows = row_v[slot]
            first = dot(rows, wide_v[src]).astype(BF16)
            second = dot(rows, wide_v[src + 1]).astype(BF16)
            for part in (0, 1):
                where = pl.ds(part * WIDE, WIDE)
                total[tgt + part] += dot(first, col_v[slot, :WIDE, where]) + dot(second, col_v[slot, WIDE:, where])
            return carry

        lax.fori_loop(0, counts[side], term, 0)

    def finish(i, carry):
        out[i] = total[i].astype(BF16)
        return carry

    lax.fori_loop(0, CHIPS, finish, 0)


def terms(count, source, target, table_sib, row_ops, row_sib, col_ops, col_sib, wide):
    hbm = pl.BlockSpec(memory_space=pltpu.HBM)
    smem = pl.BlockSpec(memory_space=pltpu.SMEM)
    return pl.pallas_call(
        terms_kernel,
        out_shape=jax.ShapeDtypeStruct((CHIPS, SEC, WIDE), BF16),
        in_specs=[smem] * 4 + [hbm] * 5,
        out_specs=pl.BlockSpec(memory_space=pltpu.VMEM),
        scratch_shapes=[
            pltpu.VMEM((CHIPS, SEC, WIDE), BF16),
            pltpu.VMEM((8, SEC, SEC), BF16),
            pltpu.VMEM((8, SEC, SEC), BF16),
            pltpu.VMEM((CHIPS, SEC, WIDE), F32),
            pltpu.SemaphoreType.DMA(()),
            pltpu.SemaphoreType.DMA((8,)),
            pltpu.SemaphoreType.DMA((8,)),
        ],
        compiler_params=pltpu.CompilerParams(vmem_limit_bytes=60 * MIB),
        name="terms",
    )(count, source, target, table_sib, row_ops, row_sib, col_ops, col_sib, wide)


def rough(a, b):
    return dot(a.astype(BF16), b.astype(BF16))


def reduce_blocks(part, near, whole, near2, whole2, total, x, z, send, recv, send2, recv2):
    names = (("z", "x"), ("x", "z"))
    places = ((z, x), (x, z))

    def block(h, pa, pb):
        return pb * 4 + pa if h == 0 else pa * 4 + pb

    def rows(h, half):
        return pl.ds(h * HALF + half * QUARTER, QUARTER)

    def local(half):
        return pl.ds(half * QUARTER, QUARTER)

    def order(h):
        q = places[h][1]
        return (turn(q, 2), turn(q, 1), turn(q, -1), q)

    sent = []

    def go(one):
        one.start()
        sent.append(one)

    def near_copy(h, d, i):
        p = places[h][0]
        src = part.at[block(h, turn(p, 2), order(h)[i]), rows(h, d), :]
        to = {names[h][0]: turn(p, 1 - 2 * d)}
        return push(src, near.at[h, d, i], send.at[h, d, i], recv.at[h, d, i], to)

    def whole_copy(h, d, i, half):
        p = places[h][0]
        src = part.at[block(h, turn(p, 1 - 2 * d), order(h)[i]), rows(h, half), :]
        to = {names[h][0]: turn(p, 1 - 2 * d)}
        j = 2 + 2 * d + half
        return push(src, whole.at[h, d, i, local(half), :], send.at[h, j, i], recv.at[h, j, i], to)

    def near2_copy(h, d):
        p, q = places[h]
        src = part.at[block(h, p, turn(q, 2)), rows(h, d), :]
        return push(src, near2.at[h, d], send2.at[h, d], recv2.at[h, d], {names[h][1]: turn(q, 1 - 2 * d)})

    def whole2_copy(h, d, half):
        p, q = places[h]
        j = 2 + 2 * d + half
        src = part.at[block(h, p, turn(q, 1 - 2 * d)), rows(h, half), :]
        to = {names[h][1]: turn(q, 1 - 2 * d)}
        return push(src, whole2.at[h, d, local(half), :], send2.at[h, j], recv2.at[h, j], to)

    for i in range(4):
        for h in (0, 1):
            for d in (0, 1):
                go(near_copy(h, d, i))
    for i in range(4):
        for h in (0, 1):
            for d in (0, 1):
                go(whole_copy(h, d, i, 1 - d))
    for i in range(4):
        for h in (0, 1):
            p = places[h][0]
            for d in (0, 1):
                near_copy(h, d, i).wait_recv()
                at = block(h, turn(p, 1 - 2 * d), order(h)[i])
                both = part[at, rows(h, d), :].astype(F32) + near[h, d, i].astype(F32)
                part[at, rows(h, d), :] = both.astype(BF16)
                go(whole_copy(h, d, i, d))
    for i in range(4):
        for h in (0, 1):
            p, q = places[h]
            for d in (0, 1):
                for half in (0, 1):
                    whole_copy(h, d, i, half).wait_recv()
            at = block(h, p, order(h)[i])
            here = pl.ds(h * HALF, HALF)
            done = part[at, here, :].astype(F32) + whole[h, 0, i].astype(F32) + whole[h, 1, i].astype(F32)
            if i == 3:
                total[here, :] = done
            else:
                part[at, here, :] = done.astype(BF16)
            if i == 0:
                go(near2_copy(h, 0))
                go(near2_copy(h, 1))
            if i == 1:
                go(whole2_copy(h, 0, 1))
            if i == 2:
                go(whole2_copy(h, 1, 0))
    for h in (0, 1):
        p, q = places[h]
        for d in (0, 1):
            near2_copy(h, d).wait_recv()
            at = block(h, p, turn(q, 1 - 2 * d))
            both = part[at, rows(h, d), :].astype(F32) + near2[h, d].astype(F32)
            part[at, rows(h, d), :] = both.astype(BF16)
            go(whole2_copy(h, d, d))
    for h in (0, 1):
        for d in (0, 1):
            for half in (0, 1):
                whole2_copy(h, d, half).wait_recv()
        here = pl.ds(h * HALF, HALF)
        total[here, :] += whole2[h, 0].astype(F32) + whole2[h, 1].astype(F32)
    for one in sent:
        one.wait_send()


def frobenius(a):
    return jnp.sqrt(jnp.sum(a * a, axis=(0, 1), keepdims=True) + 1e-06)


def step_kernel(
    part_h, wide_h, energy_row,
    stepped_o, root_o, level_o, exact_o, energy_o,
    part, near, whole, near2, whole2, total, wide, summed, stepped, gram, my, mm, mu, mz, roots, level_two, exact, scalars, energy_col,
    rs_send, rs_recv, rs2_send, rs2_recv, ag_send, ag_recv, en_send, en_recv, st_send, st_recv, st_own,
    end_send, end_recv, own_sem,
):
    x, z, c, y = lax.axis_index("x"), lax.axis_index("z"), lax.axis_index("core"), lax.axis_index("sec")
    b = x * 4 + z
    sib = {"core": 1 - c}
    load = pltpu.make_async_copy(part_h, part, own_sem.at[0])
    load_wide = pltpu.make_async_copy(wide_h, wide, own_sem.at[1])
    load.start()
    greet(
        ring_peers(x, z)
        + [{"x": turn(x, 2)}, {"z": turn(z, 2)}, sib, {"sec": turn(y, 1)}, {"sec": turn(y, 2)}, {"sec": turn(y, -1)}]
    )
    same = lax.broadcasted_iota(jnp.int32, (128, 128), 0) == lax.broadcasted_iota(jnp.int32, (128, 128), 1)
    for i in range(4):
        spread = jnp.where(same, jnp.broadcast_to(energy_row[pl.ds(c * 4 + i, 1), :], (128, 128)), 0.0)
        energy_col[pl.ds(i * 128, 128), :] = jnp.sum(spread, axis=1, keepdims=True)
    load.wait()
    load_wide.start()
    reduce_blocks(part, near, whole, near2, whole2, total, x, z, rs_send, rs_recv, rs2_send, rs2_recv)
    summed[b] = total[...].astype(BF16)
    steps = all_blocks(summed, x, z, ag_send, ag_recv)
    next(steps)
    load_wide.wait()
    level = energy_col[...]
    amplitude = wide[b].astype(F32)
    applied = level * amplitude + total[...]
    share = jnp.sum(amplitude * applied, axis=(0, 1), keepdims=True)

    stages = (("sec", y, 4), ("x", x, 4), ("z", z, 4), ("core", c, 2))

    def energy_copies(s):
        name, place, size = stages[s]
        for hop in range(1, size):
            to = {name: lax.rem(place + hop, size)}
            src = lax.rem(place + (size - hop), size)
            yield (
                push(scalars.at[s, place], scalars.at[s, place], en_send.at[s, hop], en_recv.at[s, hop], to),
                push(scalars.at[s, src], scalars.at[s, src], en_send.at[s, hop], en_recv.at[s, hop], to),
            )

    for s in range(4):
        place, size = stages[s][1:]
        scalars[s, place] = jnp.broadcast_to(share, (8, 128))
        for out, unused in energy_copies(s):
            out.start()
        next(steps, None)
        for out, arriving in energy_copies(s):
            arriving.wait_recv()
            out.wait_send()
        share = scalars[s, 0] + scalars[s, 1]
        if size == 4:
            share = (share + scalars[s, 2]) + scalars[s, 3]
        share = share[0:1, 0:1]
    energy = share * (1.0 / ENTRIES)
    energy_o[...] = jnp.broadcast_to(energy, (8, 128))
    for step in steps:
        del step

    own = amplitude + 0.5 * (energy * amplitude - applied)
    exact[0] = own[:, :128]
    exact[1] = own[:, 128:]
    mine = pl.ds(pl.multiple_of(c * SEC, SEC), SEC)
    exact_send = push(exact.at[1 - c], exact_o.at[mine, :], end_send.at[0], end_recv.at[0], sib)
    exact_own = pltpu.make_async_copy(exact.at[c], exact_o.at[mine, :], own_sem.at[2])
    exact_send.start()
    exact_own.start()

    def out_block(i):
        return (
            push(stepped.at[i], stepped_o.at[c, i], st_send.at[i], st_recv.at[i], sib),
            pltpu.make_async_copy(stepped.at[i], stepped_o.at[c, i], st_own.at[i]),
        )

    gram[...] = jnp.zeros((SEC, SEC), F32)

    def one_block(i, carry):
        part_of = wide[i].astype(F32)
        value = part_of + 0.5 * (energy * part_of - (level * part_of + summed[i].astype(F32)))
        value = value.astype(BF16)
        stepped[i] = value
        for one in out_block(i):
            one.start()
        gram[...] += dot_t(value, value)
        return carry

    lax.fori_loop(0, CHIPS, one_block, 0)

    def root(y_ref, d_ref, again):
        my[...] = 1.5 * y_ref[...] - 0.5 * rough(y_ref[...], y_ref[...])
        mu[...] = 1.5 * my[...] - 0.5 * rough(y_ref[...], my[...])
        d_ref[...] = 0.25 * rough(mu[...], y_ref[...]) - 0.75 * (y_ref[...] + mu[...])
        if again:
            y_ref[...] = 1.5 * my[...] - 0.5 * rough(my[...], mu[...])

    gram_one = gram[...] * (1.0 / COLS)
    scale_one = frobenius(gram_one)
    gram[...] = gram_one / scale_one
    root(gram, mz, True)
    gram_two = 2.25 * gram[...] + rough(mz[...], gram[...])
    scale_two = frobenius(gram_two)
    gram[...] = gram_two / scale_two
    root(gram, mm, False)
    size = jnp.sqrt(scale_one) * jnp.sqrt(scale_two)
    roots[...] = ((2.25 * (mz[...] + mm[...]) + rough(mm[...], mz[...])) / size).astype(BF16)
    level_two[...] = jnp.broadcast_to(2.25 * 2.25 / size, (8, 128))
    root_send = push(roots, root_o.at[c], end_send.at[1], end_recv.at[1], sib)
    root_own = pltpu.make_async_copy(roots, root_o.at[c], own_sem.at[3])
    level_send = push(level_two, level_o.at[c], end_send.at[2], end_recv.at[2], sib)
    level_own = pltpu.make_async_copy(level_two, level_o.at[c], own_sem.at[4])
    level_send.start()
    level_own.start()
    root_send.start()
    root_own.start()

    def block_done(i, carry):
        going, staying = out_block(i)
        going.wait_send()
        staying.wait()
        push(stepped.at[i], stepped_o.at[1 - c, i], st_send.at[i], st_recv.at[i], sib).wait_recv()
        return carry

    lax.fori_loop(0, CHIPS, block_done, 0)
    other = pl.ds(pl.multiple_of((1 - c) * SEC, SEC), SEC)
    exact_send.wait_send()
    exact_own.wait()
    push(exact.at[1 - c], exact_o.at[other, :], end_send.at[0], end_recv.at[0], sib).wait_recv()
    root_send.wait_send()
    root_own.wait()
    push(roots, root_o.at[1 - c], end_send.at[1], end_recv.at[1], sib).wait_recv()
    level_send.wait_send()
    level_own.wait()
    push(level_two, level_o.at[1 - c], end_send.at[2], end_recv.at[2], sib).wait_recv()


def step(part, wide, energy_row):
    hbm = pl.BlockSpec(memory_space=pltpu.HBM)
    vmem = pl.BlockSpec(memory_space=pltpu.VMEM)
    square = pltpu.VMEM((SEC, SEC), F32)
    blocks = pltpu.VMEM((CHIPS, SEC, WIDE), BF16)
    dma = pltpu.SemaphoreType.DMA
    return pl.pallas_call(
        step_kernel,
        out_shape=(
            jax.ShapeDtypeStruct((2, CHIPS, SEC, WIDE), BF16),
            jax.ShapeDtypeStruct((2, SEC, SEC), BF16),
            jax.ShapeDtypeStruct((2, 8, 128), F32),
            jax.ShapeDtypeStruct((2 * SEC, 128), F32),
            jax.ShapeDtypeStruct((8, 128), F32),
        ),
        in_specs=[hbm, hbm, vmem],
        out_specs=(hbm, hbm, hbm, hbm, vmem),
        scratch_shapes=[
            blocks,
            pltpu.VMEM((2, 2, 4, QUARTER, WIDE), BF16),
            pltpu.VMEM((2, 2, 4, HALF, WIDE), BF16),
            pltpu.VMEM((2, 2, QUARTER, WIDE), BF16),
            pltpu.VMEM((2, 2, HALF, WIDE), BF16),
            pltpu.VMEM((SEC, WIDE), F32),
            blocks,
            blocks,
            blocks,
            square,
            square,
            square,
            square,
            square,
            pltpu.VMEM((SEC, SEC), BF16),
            pltpu.VMEM((8, 128), F32),
            pltpu.VMEM((2, SEC, 128), F32),
            pltpu.VMEM((4, 4, 8, 128), F32),
            pltpu.VMEM((SEC, 1), F32),
            dma((2, 6, 4)),
            dma((2, 6, 4)),
            dma((2, 6)),
            dma((2, 6)),
            dma((2, 20)),
            dma((2, 20)),
            dma((4, 4)),
            dma((4, 4)),
            dma((CHIPS,)),
            dma((CHIPS,)),
            dma((CHIPS,)),
            dma((3,)),
            dma((3,)),
            dma((5,)),
        ],
        compiler_params=pltpu.CompilerParams(
            collective_id=1, has_side_effects=True, vmem_limit_bytes=60 * MIB
        ),
        name="step",
    )(part, wide, energy_row)


def renorm_kernel(count, source, target, src_block, tgt_block, cols, root, level, exact, energy, out, wave_o, energy_o):
    k = pl.program_id(0)
    scale = level[0, 0:1, 0:1]

    @pl.when(k == 0)
    def first():
        energy_o[0] = energy[0, 0]
        wave_o[...] = scale * exact[...] + dot(root[0], exact[...].astype(BF16))

    @pl.when(k < count[0])
    def live():
        product = None
        for part in (0, 1):
            block = src_block[0, part]
            half = (scale * block.astype(F32) + dot(root[0], block)).astype(BF16)
            added = dot(half, cols[0, part * WIDE : (part + 1) * WIDE, :])
            product = added if product is None else product + added
        product = product.astype(BF16)
        total = None
        for part in (0, 1):
            block = tgt_block[0, part]
            half = (scale * block.astype(F32) + dot(root[0], block)).astype(BF16)
            added = dot_t(product[:, part * WIDE : (part + 1) * WIDE], half)
            total = added if total is None else total + added
        out[0] = total * SEC ** (-0.5)

    @pl.when(k >= count[0])
    def empty():
        out[...] = jnp.zeros_like(out)


def renorm(count, source, target, stepped, cols, root, level, exact, energy):
    def slot(k, count):
        return jnp.minimum(k, count[0] - 1)

    def sector(k, s, count):
        return jnp.where(k < count[0], s, 1)

    def src_at(k, s, count, source, target):
        return (sector(k, s, count), source[slot(k, count)], 0, 0)

    def tgt_at(k, s, count, source, target):
        return (sector(k, s, count), target[slot(k, count)], 0, 0)

    def root_at(k, s, count, source, target):
        return (sector(k, s, count), 0, 0)

    def once_at(k, s, count, source, target):
        return (jnp.where(k == 0, s, 1), 0)

    return pl.pallas_call(
        renorm_kernel,
        out_shape=(
            jax.ShapeDtypeStruct((4, 2 * SEC, SEC), F32),
            jax.ShapeDtypeStruct((2 * SEC, 128), F32),
            jax.ShapeDtypeStruct((1,), F32),
        ),
        grid_spec=pltpu.PrefetchScalarGridSpec(
            num_scalar_prefetch=3,
            grid=(4, 2),
            in_specs=[
                pl.BlockSpec((1, 2, SEC, WIDE), src_at),
                pl.BlockSpec((1, 2, SEC, WIDE), tgt_at),
                pl.BlockSpec((1, SEC, SEC), lambda k, s, count, source, target: (slot(k, count), 0, 0)),
                pl.BlockSpec((1, SEC, SEC), root_at),
                pl.BlockSpec((1, 8, 128), root_at),
                pl.BlockSpec((SEC, 128), once_at),
                pl.BlockSpec(memory_space=pltpu.SMEM),
            ],
            out_specs=[
                pl.BlockSpec((1, SEC, SEC), lambda k, s, count, source, target: (k, s, 0)),
                pl.BlockSpec((SEC, 128), once_at),
                pl.BlockSpec(memory_space=pltpu.SMEM),
            ],
        ),
        compiler_params=pltpu.CompilerParams(vmem_limit_bytes=60 * MIB),
        name="renorm",
    )(count, source, target, stepped, stepped, cols, root, level, exact, energy)


def on_device(wave_in, row_energy, row_operators, column_operators, term_count, source, target):
    wide, row_sib, col_sib, table_sib = gather(
        wave_in, row_operators, column_operators, term_count, source, target
    )
    part = terms(
        term_count, source, target, table_sib, row_operators, row_sib, column_operators, col_sib, wide
    )
    stepped, root, level, exact, energy = step(part, wide, row_energy.reshape(8, 128))
    renormalized, wave_next, energy = renorm(
        term_count, source, target, stepped, column_operators, root, level, exact, energy
    )
    return (wave_next, renormalized, energy.reshape(()))


def solution(mesh):
    torus = Mesh(mesh.devices.reshape(4, 4, 2, mesh.shape["sec"]), ("x", "z", "core", "sec"))
    return jax.shard_map(
        on_device,
        mesh=torus,
        in_specs=(
            P("sec", OPS),
            P("sec"),
            P(OPS, "sec", None),
            P(OPS, None, None),
            P(OPS),
            P(OPS),
            P(OPS),
        ),
        out_specs=(P("sec", OPS), P(OPS, "sec", None), P()),
        check_vma=False,
    )
```

```python
import functools

import jax
import jax.numpy as jnp
from jax import lax
from jax.experimental import pallas as pl
from jax.experimental.pallas import tpu as pltpu
from jax.sharding import Mesh
from jax.sharding import PartitionSpec as P

SEC = 512
COLS = 4096
ENTRIES = 4096 * 4096
CHIPS = 16
WIDE = 256
HALF = 256
QUARTER = 128
MIB = 1 << 20
MESH = pl.DeviceIdType.MESH
OPS = ("x", "z", "core")
F32 = jnp.float32
BF16 = jnp.bfloat16


def turn(place, by):
    return lax.rem(place + (by + 4), 4)


def push(src, dst, send, recv, to):
    return pltpu.make_async_remote_copy(
        src_ref=src, dst_ref=dst, send_sem=send, recv_sem=recv, device_id=to, device_id_type=MESH
    )


def greet(peers):
    barrier = pltpu.get_barrier_semaphore()
    for peer in peers:
        pl.semaphore_signal(barrier, inc=1, device_id=peer, device_id_type=MESH)
    pl.semaphore_wait(barrier, len(peers))


def all_blocks(buf, x, z, send, recv):
    names = (("x", "z"), ("z", "x"))
    places = ((x, z), (z, x))

    def block(h, pa, pb):
        return pa * 4 + pb if h == 0 else pb * 4 + pa

    def view(h, pa, pb, part):
        rows = pl.ds(h * HALF, HALF) if part is None else pl.ds(h * HALF + part * QUARTER, QUARTER)
        return buf.at[block(h, pa, pb), rows, :]

    def copy(h, j, pa, pb, part, axis, by):
        ref = view(h, pa, pb, part)
        to = {names[h][axis]: turn(places[h][axis], by)}
        return push(ref, ref, send.at[h, j], recv.at[h, j], to)

    def order(h):
        p = places[h][0]
        return (p, turn(p, -1), turn(p, 1), turn(p, 2))

    sent = []

    def go(*what):
        one = copy(*what)
        one.start()
        sent.append(one)

    def arrived(h, j, pa, pb, part):
        copy(h, j, pa, pb, part, 0, 1).wait_recv()

    for h in (0, 1):
        p, q = places[h]
        go(h, 0, p, q, None, 0, 1)
        go(h, 1, p, q, None, 0, -1)
    for h in (0, 1):
        p, q = places[h]
        go(h, 4, p, q, None, 1, 1)
        go(h, 8, p, q, None, 1, -1)
    yield
    for h in (0, 1):
        p, q = places[h]
        left, right = turn(p, -1), turn(p, 1)
        arrived(h, 0, left, q, None)
        go(h, 2, left, q, 0, 0, 1)
        go(h, 5, left, q, None, 1, 1)
        go(h, 9, left, q, None, 1, -1)
        arrived(h, 1, right, q, None)
        go(h, 3, right, q, 1, 0, -1)
        go(h, 6, right, q, None, 1, 1)
        go(h, 10, right, q, None, 1, -1)
    yield

    def onward(h, i):
        pa, q = order(h)[i], places[h][1]
        arrived(h, 4 + i, pa, turn(q, -1), None)
        go(h, 12 + i, pa, turn(q, -1), 0, 1, 1)
        arrived(h, 8 + i, pa, turn(q, 1), None)
        go(h, 16 + i, pa, turn(q, 1), 1, 1, -1)

    for h in (0, 1):
        onward(h, 0)
    yield 1
    for h in (0, 1):
        p, q = places[h]
        far = turn(p, 2)
        arrived(h, 2, far, q, 0)
        arrived(h, 3, far, q, 1)
        go(h, 7, far, q, None, 1, 1)
        go(h, 11, far, q, None, 1, -1)
    yield
    for h in (0, 1):
        onward(h, 1)
    yield
    for h in (0, 1):
        onward(h, 2)
    yield 2

    def last(i):
        for h in (0, 1):
            pa, far = order(h)[i], turn(places[h][1], 2)
            arrived(h, 12 + i, pa, far, 0)
            arrived(h, 16 + i, pa, far, 1)

    last(0)
    yield 3
    for h in (0, 1):
        onward(h, 3)
    last(1)
    last(2)
    yield 4
    last(3)
    yield 5
    for one in sent:
        one.wait_send()


def ring_peers(x, z):
    return [{"x": turn(x, 1)}, {"x": turn(x, -1)}, {"z": turn(z, 1)}, {"z": turn(z, -1)}]


def dot(a, b):
    return jnp.dot(a, b, preferred_element_type=F32)


def dot_t(a, b):
    return lax.dot_general(a, b, (((1,), (1,)), ((), ())), preferred_element_type=F32)


def rough(a, b):
    return dot(a.astype(BF16), b.astype(BF16))


def reduce_blocks(part, near, whole, near2, whole2, total, x, z, send, recv, send2, recv2):
    names = (("z", "x"), ("x", "z"))
    places = ((z, x), (x, z))

    def block(h, pa, pb):
        return pb * 4 + pa if h == 0 else pa * 4 + pb

    def rows(h, half):
        return pl.ds(h * HALF + half * QUARTER, QUARTER)

    def local(half):
        return pl.ds(half * QUARTER, QUARTER)

    def order(h):
        q = places[h][1]
        return (turn(q, 2), turn(q, 1), turn(q, -1), q)

    sent = []

    def go(one):
        one.start()
        sent.append(one)

    def near_copy(h, d, i):
        p = places[h][0]
        src = part.at[block(h, turn(p, 2), order(h)[i]), rows(h, d), :]
        to = {names[h][0]: turn(p, 1 - 2 * d)}
        return push(src, near.at[h, d, i], send.at[h, d, i], recv.at[h, d, i], to)

    def whole_copy(h, d, i, half):
        p = places[h][0]
        src = part.at[block(h, turn(p, 1 - 2 * d), order(h)[i]), rows(h, half), :]
        to = {names[h][0]: turn(p, 1 - 2 * d)}
        j = 2 + 2 * d + half
        return push(src, whole.at[h, d, i, local(half), :], send.at[h, j, i], recv.at[h, j, i], to)

    def near2_copy(h, d):
        p, q = places[h]
        src = part.at[block(h, p, turn(q, 2)), rows(h, d), :]
        return push(src, near2.at[h, d], send2.at[h, d], recv2.at[h, d], {names[h][1]: turn(q, 1 - 2 * d)})

    def whole2_copy(h, d, half):
        p, q = places[h]
        j = 2 + 2 * d + half
        src = part.at[block(h, p, turn(q, 1 - 2 * d)), rows(h, half), :]
        to = {names[h][1]: turn(q, 1 - 2 * d)}
        return push(src, whole2.at[h, d, local(half), :], send2.at[h, j], recv2.at[h, j], to)

    for i in range(4):
        for h in (0, 1):
            for d in (0, 1):
                go(near_copy(h, d, i))
    for i in range(4):
        for h in (0, 1):
            for d in (0, 1):
                go(whole_copy(h, d, i, 1 - d))
    for i in range(4):
        for h in (0, 1):
            p = places[h][0]
            for d in (0, 1):
                near_copy(h, d, i).wait_recv()
                at = block(h, turn(p, 1 - 2 * d), order(h)[i])
                both = part[at, rows(h, d), :].astype(F32) + near[h, d, i].astype(F32)
                part[at, rows(h, d), :] = both.astype(BF16)
                go(whole_copy(h, d, i, d))
    for i in range(4):
        for h in (0, 1):
            p, q = places[h]
            for d in (0, 1):
                for half in (0, 1):
                    whole_copy(h, d, i, half).wait_recv()
            at = block(h, p, order(h)[i])
            here = pl.ds(h * HALF, HALF)
            done = part[at, here, :].astype(F32) + whole[h, 0, i].astype(F32) + whole[h, 1, i].astype(F32)
            if i == 3:
                total[here, :] = done
            else:
                part[at, here, :] = done.astype(BF16)
            if i == 0:
                go(near2_copy(h, 0))
                go(near2_copy(h, 1))
            if i == 1:
                go(whole2_copy(h, 0, 1))
            if i == 2:
                go(whole2_copy(h, 1, 0))
    for h in (0, 1):
        p, q = places[h]
        for d in (0, 1):
            near2_copy(h, d).wait_recv()
            at = block(h, p, turn(q, 1 - 2 * d))
            both = part[at, rows(h, d), :].astype(F32) + near2[h, d].astype(F32)
            part[at, rows(h, d), :] = both.astype(BF16)
            go(whole2_copy(h, d, d))
    for h in (0, 1):
        for d in (0, 1):
            for half in (0, 1):
                whole2_copy(h, d, half).wait_recv()
        here = pl.ds(h * HALF, HALF)
        total[here, :] += whole2[h, 0].astype(F32) + whole2[h, 1].astype(F32)
    for one in sent:
        one.wait_send()


def frobenius(a):
    return jnp.sqrt(jnp.sum(a * a, axis=(0, 1), keepdims=True) + 1e-06)


def group_block(group, t, x, z):
    if group == 1:
        dx = (t == 1).astype(jnp.int32) - (t == 2).astype(jnp.int32)
        dz = (t == 3).astype(jnp.int32) - (t == 4).astype(jnp.int32)
    elif group == 2:
        dx, dz = 1 - 2 * lax.rem(t, 2), 1 - 2 * lax.div(t, 2)
    elif group == 3:
        dx, dz = 2 - 2 * t, 2 * t
    elif group == 4:
        dx, dz = jnp.where(t < 2, 1 - 2 * t, 2), jnp.where(t < 2, 2, 5 - 2 * t)
    else:
        dx = dz = 2
    return turn(x, dx) * 4 + turn(z, dz)


GROUP_SIZE = {1: 5, 2: 4, 3: 2, 4: 4, 5: 1}


def site_kernel(
    wave, row_ops, col_ops, count, source, target, energy_row,
    stepped_o, root_o, level_o, exact_o, energy_o,
    wide, row_v, col_v, table, table_in, table_s, order_s, source_s, prefix,
    part, near, whole, near2, whole2, total, summed, stepped, gram, my, mm, mu, mz, roots, level_two, exact, scalars, energy_col,
    wv_send, wv_recv, swap_send, swap_recv,
    rs_send, rs_recv, rs2_send, rs2_recv, ag_send, ag_recv, en_send, en_recv, st_send, st_recv, st_own,
    end_send, end_recv, own_sem,
):
    x, z, c, y = lax.axis_index("x"), lax.axis_index("z"), lax.axis_index("core"), lax.axis_index("sec")
    b = x * 4 + z
    sib = {"core": 1 - c}
    mine = pl.ds(pl.multiple_of(c * SEC, SEC), SEC)
    other = pl.ds(pl.multiple_of((1 - c) * SEC, SEC), SEC)
    columns = pl.ds(pl.multiple_of(c * 128, 128), 128)
    other_columns = pl.ds(pl.multiple_of((1 - c) * 128, 128), 128)
    own_slots, sib_slots = pl.ds(0, 4), pl.ds(4, 4)
    own_wave = pltpu.make_async_copy(wave.at[mine, :], wide.at[b, :, columns], own_sem.at[0])
    own_wave.start()
    lane = lax.broadcasted_iota(jnp.int32, (8, 128), 1)
    numbers = jnp.where(lane == 0, count[0], 0)
    for k in range(4):
        numbers = jnp.where(lane == 1 + k, source[k], numbers)
        numbers = jnp.where(lane == 5 + k, target[k], numbers)
    table[...] = numbers
    greet(
        ring_peers(x, z)
        + [sib, {"x": turn(x, 2)}, {"z": turn(z, 2)}, {"sec": turn(y, 1)}, {"sec": turn(y, 2)}, {"sec": turn(y, -1)}]
    )
    swaps = [
        push(wave.at[other, :], wide.at[b, :, columns], swap_send.at[0], swap_recv.at[0], sib),
        push(table, table_in, swap_send.at[1], swap_recv.at[1], sib),
        push(row_ops.at[:, other, :], row_v.at[sib_slots], swap_send.at[2], swap_recv.at[2], sib),
        push(col_ops, col_v.at[sib_slots], swap_send.at[3], swap_recv.at[3], sib),
    ]
    swaps[0].start()
    own_wave.wait()
    push(wave.at[other, :], wide.at[b, :, other_columns], swap_send.at[0], swap_recv.at[0], sib).wait_recv()
    steps = all_blocks(wide, x, z, wv_send, wv_recv)
    next(steps)
    for swap in swaps[1:]:
        swap.start()
    own_rows = pltpu.make_async_copy(row_ops.at[:, mine, :], row_v.at[own_slots], own_sem.at[1])
    own_cols = pltpu.make_async_copy(col_ops, col_v.at[own_slots], own_sem.at[5])
    own_rows.start()
    own_cols.start()
    same = lax.broadcasted_iota(jnp.int32, (128, 128), 0) == lax.broadcasted_iota(jnp.int32, (128, 128), 1)
    for i in range(4):
        spread = jnp.where(same, jnp.broadcast_to(energy_row[pl.ds(c * 4 + i, 1), :], (128, 128)), 0.0)
        energy_col[pl.ds(i * 128, 128), :] = jnp.sum(spread, axis=1, keepdims=True)
    swaps[1].wait_recv()
    to_scalars = pltpu.make_async_copy(table_in, table_s, own_sem.at[6])
    to_scalars.start()
    to_scalars.wait()

    def flag(condition):
        return condition.astype(jnp.int32)

    keys, sources = [], []
    for side in (0, 1):
        live = table_s[0, 0] if side else count[0]
        for k in range(4):
            alive = flag(k < live)
            aim = table_s[0, 5 + k] if side else target[k]
            keys.append(aim * alive + 8 * (1 - alive))
            sources.append(table_s[0, 1 + k] if side else source[k])
    ranks = []
    for i in range(8):
        ahead = [flag(keys[j] <= keys[i]) if j < i else flag(keys[j] < keys[i]) for j in range(8) if j != i]
        ranks.append(sum(ahead))
    for j in range(8):
        order_s[j] = sum(i * flag(ranks[i] == j) for i in range(8))
        source_s[j] = sum(sources[i] * flag(ranks[i] == j) for i in range(8))
    starts = [sum(flag(key < t) for key in keys) for t in range(9)]

    for ready in steps:
        del ready
    swaps[0].wait_send()
    swaps[1].wait_send()
    own_rows.wait()
    own_cols.wait()
    swaps[2].wait()
    swaps[3].wait()

    prefix[0] = jnp.zeros((HALF, SEC), F32)
    for h in (0, 1):
        here = pl.ds(h * HALF, HALF)

        def term(j, carry, here=here):
            slot = order_s[j]
            src = source_s[j] * 2
            rows = row_v[slot, here, :]
            first = dot(rows, wide[src]).astype(BF16)
            second = dot(rows, wide[src + 1]).astype(BF16)
            prefix[j + 1] = prefix[j] + (dot(first, col_v[slot, :WIDE, :]) + dot(second, col_v[slot, WIDE:, :]))
            return carry

        lax.fori_loop(0, 8, term, 0)
        for t in range(8):
            added = (prefix[starts[t + 1]] - prefix[starts[t]]).astype(BF16)
            part[2 * t, here, :] = added[:, :WIDE]
            part[2 * t + 1, here, :] = added[:, WIDE:]

    reduce_blocks(part, near, whole, near2, whole2, total, x, z, rs_send, rs_recv, rs2_send, rs2_recv)
    summed[b] = total[...].astype(BF16)
    steps = all_blocks(summed, x, z, ag_send, ag_recv)
    next(steps)
    level = energy_col[...]
    amplitude = wide[b].astype(F32)
    applied = level * amplitude + total[...]
    share = jnp.sum(amplitude * applied, axis=(0, 1), keepdims=True)

    stages = (("sec", y, 4), ("x", x, 4), ("z", z, 4), ("core", c, 2))

    def energy_copies(s):
        name, place, size = stages[s]
        for hop in range(1, size):
            to = {name: lax.rem(place + hop, size)}
            src = lax.rem(place + (size - hop), size)
            yield (
                push(scalars.at[s, place], scalars.at[s, place], en_send.at[s, hop], en_recv.at[s, hop], to),
                push(scalars.at[s, src], scalars.at[s, src], en_send.at[s, hop], en_recv.at[s, hop], to),
            )

    groups = []
    for s in range(4):
        place, size = stages[s][1:]
        scalars[s, place] = jnp.broadcast_to(share, (8, 128))
        for out, unused in energy_copies(s):
            out.start()
        ready = next(steps)
        groups += [ready] if ready else []
        for out, arriving in energy_copies(s):
            arriving.wait_recv()
            out.wait_send()
        share = scalars[s, 0] + scalars[s, 1]
        if size == 4:
            share = (share + scalars[s, 2]) + scalars[s, 3]
        share = share[0:1, 0:1]
    energy = share * (1.0 / ENTRIES)
    energy_o[...] = jnp.broadcast_to(energy, (8, 128))
    own = amplitude + 0.5 * (energy * amplitude - applied)
    exact[0] = own[:, :128]
    exact[1] = own[:, 128:]
    exact_send = push(exact.at[1 - c], exact_o.at[mine, :], end_send.at[0], end_recv.at[0], sib)
    exact_own = pltpu.make_async_copy(exact.at[c], exact_o.at[mine, :], own_sem.at[2])
    exact_send.start()
    exact_own.start()

    def out_block(i):
        return (
            push(stepped.at[i], stepped_o.at[c, i], st_send.at[i], st_recv.at[i], sib),
            pltpu.make_async_copy(stepped.at[i], stepped_o.at[c, i], st_own.at[i]),
        )

    gram[...] = jnp.zeros((SEC, SEC), F32)

    def add_group(group):
        def one_block(t, carry):
            i = group_block(group, t, x, z)
            part_of = wide[i].astype(F32)
            value = part_of + 0.5 * (energy * part_of - (level * part_of + summed[i].astype(F32)))
            value = value.astype(BF16)
            stepped[i] = value
            for one in out_block(i):
                one.start()
            gram[...] += dot_t(value, value)
            return carry

        lax.fori_loop(0, GROUP_SIZE[group], one_block, 0)

    for group in groups:
        add_group(group)
    for ready in steps:
        if ready:
            add_group(ready)

    def root(y_ref, d_ref, again):
        my[...] = 1.5 * y_ref[...] - 0.5 * rough(y_ref[...], y_ref[...])
        mu[...] = 1.5 * my[...] - 0.5 * rough(y_ref[...], my[...])
        d_ref[...] = 0.25 * rough(mu[...], y_ref[...]) - 0.75 * (y_ref[...] + mu[...])
        if again:
            y_ref[...] = 1.5 * my[...] - 0.5 * rough(my[...], mu[...])

    gram_one = gram[...] * (1.0 / COLS)
    scale_one = frobenius(gram_one)
    gram[...] = gram_one / scale_one
    root(gram, mz, True)
    gram_two = 2.25 * gram[...] + rough(mz[...], gram[...])
    scale_two = frobenius(gram_two)
    gram[...] = gram_two / scale_two
    root(gram, mm, False)
    size = jnp.sqrt(scale_one) * jnp.sqrt(scale_two)
    roots[...] = ((2.25 * (mz[...] + mm[...]) + rough(mm[...], mz[...])) / size).astype(BF16)
    level_two[...] = jnp.broadcast_to(2.25 * 2.25 / size, (8, 128))
    root_send = push(roots, root_o.at[c], end_send.at[1], end_recv.at[1], sib)
    root_own = pltpu.make_async_copy(roots, root_o.at[c], own_sem.at[3])
    level_send = push(level_two, level_o.at[c], end_send.at[2], end_recv.at[2], sib)
    level_own = pltpu.make_async_copy(level_two, level_o.at[c], own_sem.at[4])
    level_send.start()
    level_own.start()
    root_send.start()
    root_own.start()

    def block_done(i, carry):
        going, staying = out_block(i)
        going.wait_send()
        staying.wait()
        push(stepped.at[i], stepped_o.at[1 - c, i], st_send.at[i], st_recv.at[i], sib).wait_recv()
        return carry

    lax.fori_loop(0, CHIPS, block_done, 0)
    exact_send.wait_send()
    exact_own.wait()
    push(exact.at[1 - c], exact_o.at[other, :], end_send.at[0], end_recv.at[0], sib).wait_recv()
    root_send.wait_send()
    root_own.wait()
    push(roots, root_o.at[1 - c], end_send.at[1], end_recv.at[1], sib).wait_recv()
    level_send.wait_send()
    level_own.wait()
    push(level_two, level_o.at[1 - c], end_send.at[2], end_recv.at[2], sib).wait_recv()


def site(wave, row_ops, col_ops, count, source, target, energy_row):
    hbm = pl.BlockSpec(memory_space=pltpu.HBM)
    smem = pl.BlockSpec(memory_space=pltpu.SMEM)
    vmem = pl.BlockSpec(memory_space=pltpu.VMEM)
    square = pltpu.VMEM((SEC, SEC), F32)
    blocks = pltpu.VMEM((CHIPS, SEC, WIDE), BF16)
    dma = pltpu.SemaphoreType.DMA
    return pl.pallas_call(
        site_kernel,
        out_shape=(
            jax.ShapeDtypeStruct((2, CHIPS, SEC, WIDE), BF16),
            jax.ShapeDtypeStruct((2, SEC, SEC), BF16),
            jax.ShapeDtypeStruct((2, 8, 128), F32),
            jax.ShapeDtypeStruct((2 * SEC, 128), F32),
            jax.ShapeDtypeStruct((8, 128), F32),
        ),
        in_specs=[hbm] * 3 + [smem] * 3 + [vmem],
        out_specs=(hbm, hbm, hbm, hbm, vmem),
        scratch_shapes=[
            blocks,
            pltpu.VMEM((8, SEC, SEC), BF16),
            pltpu.VMEM((8, SEC, SEC), BF16),
            pltpu.VMEM((8, 128), jnp.int32),
            pltpu.VMEM((8, 128), jnp.int32),
            pltpu.SMEM((8, 128), jnp.int32),
            pltpu.SMEM((8,), jnp.int32),
            pltpu.SMEM((8,), jnp.int32),
            pltpu.VMEM((9, HALF, SEC), F32),
            blocks,
            pltpu.VMEM((2, 2, 4, QUARTER, WIDE), BF16),
            pltpu.VMEM((2, 2, 4, HALF, WIDE), BF16),
            pltpu.VMEM((2, 2, QUARTER, WIDE), BF16),
            pltpu.VMEM((2, 2, HALF, WIDE), BF16),
            pltpu.VMEM((SEC, WIDE), F32),
            blocks,
            blocks,
            square,
            square,
            square,
            square,
            square,
            pltpu.VMEM((SEC, SEC), BF16),
            pltpu.VMEM((8, 128), F32),
            pltpu.VMEM((2, SEC, 128), F32),
            pltpu.VMEM((4, 4, 8, 128), F32),
            pltpu.VMEM((SEC, 1), F32),
            dma((2, 20)),
            dma((2, 20)),
            dma((4,)),
            dma((4,)),
            dma((2, 6, 4)),
            dma((2, 6, 4)),
            dma((2, 6)),
            dma((2, 6)),
            dma((2, 20)),
            dma((2, 20)),
            dma((4, 4)),
            dma((4, 4)),
            dma((CHIPS,)),
            dma((CHIPS,)),
            dma((CHIPS,)),
            dma((3,)),
            dma((3,)),
            dma((7,)),
        ],
        compiler_params=pltpu.CompilerParams(
            collective_id=0, has_side_effects=True, vmem_limit_bytes=60 * MIB
        ),
        name="site",
    )(wave, row_ops, col_ops, count, source, target, energy_row)


def renorm_kernel(count, source, target, src_block, tgt_block, cols, root, level, exact, energy, out, wave_o, energy_o):
    k = pl.program_id(0)
    scale = level[0, 0:1, 0:1]

    @pl.when(k == 0)
    def first():
        energy_o[0] = energy[0, 0]
        wave_o[...] = scale * exact[...] + dot(root[0], exact[...].astype(BF16))

    @pl.when(k < count[0])
    def live():
        product = None
        for part in (0, 1):
            block = src_block[0, part]
            half = (scale * block.astype(F32) + dot(root[0], block)).astype(BF16)
            added = dot(half, cols[0, part * WIDE : (part + 1) * WIDE, :])
            product = added if product is None else product + added
        product = product.astype(BF16)
        total = None
        for part in (0, 1):
            block = tgt_block[0, part]
            half = (scale * block.astype(F32) + dot(root[0], block)).astype(BF16)
            added = dot_t(product[:, part * WIDE : (part + 1) * WIDE], half)
            total = added if total is None else total + added
        out[0] = total * SEC ** (-0.5)

    @pl.when(k >= count[0])
    def empty():
        out[...] = jnp.zeros_like(out)


def renorm(count, source, target, stepped, cols, root, level, exact, energy):
    def slot(k, count):
        return jnp.minimum(k, count[0] - 1)

    def sector(k, s, count):
        return jnp.where(k < count[0], s, 1)

    def src_at(k, s, count, source, target):
        return (sector(k, s, count), source[slot(k, count)], 0, 0)

    def tgt_at(k, s, count, source, target):
        return (sector(k, s, count), target[slot(k, count)], 0, 0)

    def root_at(k, s, count, source, target):
        return (sector(k, s, count), 0, 0)

    def once_at(k, s, count, source, target):
        return (jnp.where(k == 0, s, 1), 0)

    return pl.pallas_call(
        renorm_kernel,
        out_shape=(
            jax.ShapeDtypeStruct((4, 2 * SEC, SEC), F32),
            jax.ShapeDtypeStruct((2 * SEC, 128), F32),
            jax.ShapeDtypeStruct((1,), F32),
        ),
        grid_spec=pltpu.PrefetchScalarGridSpec(
            num_scalar_prefetch=3,
            grid=(4, 2),
            in_specs=[
                pl.BlockSpec((1, 2, SEC, WIDE), src_at),
                pl.BlockSpec((1, 2, SEC, WIDE), tgt_at),
                pl.BlockSpec((1, SEC, SEC), lambda k, s, count, source, target: (slot(k, count), 0, 0)),
                pl.BlockSpec((1, SEC, SEC), root_at),
                pl.BlockSpec((1, 8, 128), root_at),
                pl.BlockSpec((SEC, 128), once_at),
                pl.BlockSpec(memory_space=pltpu.SMEM),
            ],
            out_specs=[
                pl.BlockSpec((1, SEC, SEC), lambda k, s, count, source, target: (k, s, 0)),
                pl.BlockSpec((SEC, 128), once_at),
                pl.BlockSpec(memory_space=pltpu.SMEM),
            ],
        ),
        compiler_params=pltpu.CompilerParams(vmem_limit_bytes=60 * MIB),
        name="renorm",
    )(count, source, target, stepped, stepped, cols, root, level, exact, energy)


def on_device(wave_in, row_energy, row_operators, column_operators, term_count, source, target):
    stepped, root, level, exact, energy = site(
        wave_in, row_operators, column_operators, term_count, source, target, row_energy.reshape(8, 128)
    )
    renormalized, wave_next, energy = renorm(
        term_count, source, target, stepped, column_operators, root, level, exact, energy
    )
    return (wave_next, renormalized, energy.reshape(()))


def solution(mesh):
    torus = Mesh(mesh.devices.reshape(4, 4, 2, mesh.shape["sec"]), ("x", "z", "core", "sec"))
    return jax.shard_map(
        on_device,
        mesh=torus,
        in_specs=(
            P("sec", OPS),
            P("sec"),
            P(OPS, "sec", None),
            P(OPS, None, None),
            P(OPS),
            P(OPS),
            P(OPS),
        ),
        out_specs=(P("sec", OPS), P(OPS, "sec", None), P()),
        check_vma=False,
    )
```

```python
import functools

import jax
import jax.numpy as jnp
from jax import lax
from jax.experimental import pallas as pl
from jax.experimental.pallas import tpu as pltpu
from jax.sharding import Mesh
from jax.sharding import PartitionSpec as P

SEC = 512
COLS = 4096
ENTRIES = 4096 * 4096
CHIPS = 16
WIDE = 256
HALF = 256
QUARTER = 128
EIGHTH = 64
MIB = 1 << 20
MESH = pl.DeviceIdType.MESH
OPS = ("x", "z", "core")
F32 = jnp.float32
BF16 = jnp.bfloat16


def turn(place, by):
    return lax.rem(place + (by + 4), 4)


def push(src, dst, send, recv, to):
    return pltpu.make_async_remote_copy(
        src_ref=src, dst_ref=dst, send_sem=send, recv_sem=recv, device_id=to, device_id_type=MESH
    )


def greet(peers):
    barrier = pltpu.get_barrier_semaphore()
    for peer in peers:
        pl.semaphore_signal(barrier, inc=1, device_id=peer, device_id_type=MESH)
    pl.semaphore_wait(barrier, len(peers))


def all_blocks(buf, x, z, send, recv):
    names = (("x", "z"), ("z", "x"))
    places = ((x, z), (z, x))

    def block(h, pa, pb):
        return pa * 4 + pb if h == 0 else pb * 4 + pa

    def view(h, pa, pb, part):
        rows = pl.ds(h * HALF, HALF) if part is None else pl.ds(h * HALF + part * QUARTER, QUARTER)
        return buf.at[block(h, pa, pb), rows, :]

    def copy(h, j, pa, pb, part, axis, by):
        ref = view(h, pa, pb, part)
        to = {names[h][axis]: turn(places[h][axis], by)}
        return push(ref, ref, send.at[h, j], recv.at[h, j], to)

    def order(h):
        p = places[h][0]
        return (p, turn(p, -1), turn(p, 1), turn(p, 2))

    sent = []

    def go(*what):
        one = copy(*what)
        one.start()
        sent.append(one)

    def arrived(h, j, pa, pb, part):
        copy(h, j, pa, pb, part, 0, 1).wait_recv()

    for h in (0, 1):
        p, q = places[h]
        go(h, 0, p, q, None, 0, 1)
        go(h, 1, p, q, None, 0, -1)
    for h in (0, 1):
        p, q = places[h]
        go(h, 4, p, q, None, 1, 1)
        go(h, 8, p, q, None, 1, -1)
    yield
    for h in (0, 1):
        p, q = places[h]
        left, right = turn(p, -1), turn(p, 1)
        arrived(h, 0, left, q, None)
        go(h, 2, left, q, 0, 0, 1)
        arrived(h, 1, right, q, None)
        go(h, 3, right, q, 1, 0, -1)
    for h in (0, 1):
        p, q = places[h]
        left, right = turn(p, -1), turn(p, 1)
        go(h, 5, left, q, None, 1, 1)
        go(h, 9, left, q, None, 1, -1)
        go(h, 6, right, q, None, 1, 1)
        go(h, 10, right, q, None, 1, -1)
    yield

    def onward(h, i):
        pa, q = order(h)[i], places[h][1]
        arrived(h, 4 + i, pa, turn(q, -1), None)
        go(h, 12 + i, pa, turn(q, -1), 0, 1, 1)
        arrived(h, 8 + i, pa, turn(q, 1), None)
        go(h, 16 + i, pa, turn(q, 1), 1, 1, -1)

    for h in (0, 1):
        onward(h, 0)
    yield 1
    for h in (0, 1):
        p, q = places[h]
        far = turn(p, 2)
        arrived(h, 2, far, q, 0)
        arrived(h, 3, far, q, 1)
        go(h, 7, far, q, None, 1, 1)
        go(h, 11, far, q, None, 1, -1)
    yield
    for h in (0, 1):
        onward(h, 1)
    yield
    for h in (0, 1):
        onward(h, 2)
    yield 2

    def last(i):
        for h in (0, 1):
            pa, far = order(h)[i], turn(places[h][1], 2)
            arrived(h, 12 + i, pa, far, 0)
            arrived(h, 16 + i, pa, far, 1)

    last(0)
    yield 3
    for h in (0, 1):
        onward(h, 3)
    last(1)
    last(2)
    yield 4
    last(3)
    yield 5
    for one in sent:
        one.wait_send()


def ring_peers(x, z):
    return [{"x": turn(x, 1)}, {"x": turn(x, -1)}, {"z": turn(z, 1)}, {"z": turn(z, -1)}]


def dot(a, b):
    return jnp.dot(a, b, preferred_element_type=F32)


def dot_t(a, b):
    return lax.dot_general(a, b, (((1,), (1,)), ((), ())), preferred_element_type=F32)


def rough(a, b):
    return dot(a.astype(BF16), b.astype(BF16))


class Reduction:
    def __init__(self, bufs, sems, x, z):
        self.part, self.near, self.whole, self.near2, self.whole2, self.total = bufs
        self.send, self.recv, self.mod_send, self.mod_recv, self.send2, self.recv2 = sems
        self.places = ((z, x), (x, z))
        self.sent = []

    def at(self, h, pa, pb):
        return (pb, pa) if h == 0 else (pa, pb)

    def rows(self, w, h, half):
        return pl.ds(w * HALF + h * QUARTER + half * EIGHTH, EIGHTH)

    def both_rows(self, w, h):
        return pl.ds(w * HALF + h * QUARTER, QUARTER)

    def line(self, w, h, pa, half):
        rows = self.rows(w, h, half)
        return self.part.at[:, pa, rows, :] if h == 0 else self.part.at[pa, :, rows, :]

    def order(self, h):
        q = self.places[h][1]
        return (turn(q, 2), turn(q, 1), turn(q, -1), q)

    def peer(self, h, axis, d):
        return {("zx", "xz")[h][axis]: turn(self.places[h][axis], 1 - 2 * d)}

    def go(self, one):
        one.start()
        self.sent.append(one)

    def near_copy(self, w, h, d):
        src = self.line(w, h, turn(self.places[h][0], 2), d)
        return push(src, self.near.at[w, h, d], self.send.at[w, h, d], self.recv.at[w, h, d], self.peer(h, 0, d))

    def plain_copy(self, w, h, d):
        src = self.line(w, h, turn(self.places[h][0], 1 - 2 * d), 1 - d)
        dst = self.whole.at[w, h, d, :, pl.ds((1 - d) * EIGHTH, EIGHTH), :]
        return push(src, dst, self.send.at[w, h, 2 + d], self.recv.at[w, h, 2 + d], self.peer(h, 0, d))

    def added_copy(self, w, h, d, i):
        to = self.order(h)[i]
        src = self.part.at[*self.at(h, turn(self.places[h][0], 1 - 2 * d), to), self.rows(w, h, d), :]
        dst = self.whole.at[w, h, d, to, pl.ds(d * EIGHTH, EIGHTH), :]
        return push(src, dst, self.mod_send.at[w, h, d, i], self.mod_recv.at[w, h, d, i], self.peer(h, 0, d))

    def near2_copy(self, w, h, d):
        p, q = self.places[h]
        src = self.part.at[*self.at(h, p, turn(q, 2)), self.rows(w, h, d), :]
        return push(src, self.near2.at[w, h, d], self.send2.at[w, h, d], self.recv2.at[w, h, d], self.peer(h, 1, d))

    def whole2_copy(self, w, h, d, half):
        p, q = self.places[h]
        j = 2 + 2 * d + half
        src = self.part.at[*self.at(h, p, turn(q, 1 - 2 * d)), self.rows(w, h, half), :]
        dst = self.whole2.at[w, h, d, pl.ds(half * EIGHTH, EIGHTH), :]
        return push(src, dst, self.send2.at[w, h, j], self.recv2.at[w, h, j], self.peer(h, 1, d))

    def begin(self, w):
        for h in (0, 1):
            for d in (0, 1):
                self.go(self.near_copy(w, h, d))
        for h in (0, 1):
            for d in (0, 1):
                self.go(self.plain_copy(w, h, d))

    def add(self, w):
        for h in (0, 1):
            p = self.places[h][0]
            for d in (0, 1):
                self.near_copy(w, h, d).wait_recv()
                for i in range(4):
                    to = self.order(h)[i]
                    spot = (*self.at(h, turn(p, 1 - 2 * d), to), self.rows(w, h, d), slice(None))
                    both = self.part[spot].astype(F32) + self.near[w, h, d, to].astype(F32)
                    self.part[spot] = both.astype(BF16)
                    self.go(self.added_copy(w, h, d, i))

    def second(self, w):
        for h in (0, 1):
            for d in (0, 1):
                self.plain_copy(w, h, d).wait_recv()
        for i in range(4):
            for h in (0, 1):
                p = self.places[h][0]
                for d in (0, 1):
                    self.added_copy(w, h, d, i).wait_recv()
                to = self.order(h)[i]
                spot = (*self.at(h, p, to), self.both_rows(w, h), slice(None))
                done = self.part[spot].astype(F32) + self.whole[w, h, 0, to].astype(F32) + self.whole[w, h, 1, to].astype(F32)
                if i == 3:
                    self.total[self.both_rows(w, h), :] = done
                else:
                    self.part[spot] = done.astype(BF16)
                if i == 0:
                    self.go(self.near2_copy(w, h, 0))
                    self.go(self.near2_copy(w, h, 1))
                if i == 1:
                    self.go(self.whole2_copy(w, h, 0, 1))
                if i == 2:
                    self.go(self.whole2_copy(w, h, 1, 0))

    def add2(self, w):
        for h in (0, 1):
            p, q = self.places[h]
            for d in (0, 1):
                self.near2_copy(w, h, d).wait_recv()
                spot = (*self.at(h, p, turn(q, 1 - 2 * d)), self.rows(w, h, d), slice(None))
                both = self.part[spot].astype(F32) + self.near2[w, h, d].astype(F32)
                self.part[spot] = both.astype(BF16)
                self.go(self.whole2_copy(w, h, d, d))

    def finish(self, w):
        for h in (0, 1):
            for d in (0, 1):
                for half in (0, 1):
                    self.whole2_copy(w, h, d, half).wait_recv()
            here = self.both_rows(w, h)
            self.total[here, :] += self.whole2[w, h, 0].astype(F32) + self.whole2[w, h, 1].astype(F32)

    def close(self):
        for one in self.sent:
            one.wait_send()


def frobenius(a):
    return jnp.sqrt(jnp.sum(a * a, axis=(0, 1), keepdims=True) + 1e-06)


def group_block(group, t, x, z):
    if group == 1:
        dx = (t == 1).astype(jnp.int32) - (t == 2).astype(jnp.int32)
        dz = (t == 3).astype(jnp.int32) - (t == 4).astype(jnp.int32)
    elif group == 2:
        dx, dz = 1 - 2 * lax.rem(t, 2), 1 - 2 * lax.div(t, 2)
    elif group == 3:
        dx, dz = 2 - 2 * t, 2 * t
    elif group == 4:
        dx, dz = jnp.where(t < 2, 1 - 2 * t, 2), jnp.where(t < 2, 2, 5 - 2 * t)
    else:
        dx = dz = 2
    return turn(x, dx) * 4 + turn(z, dz)


GROUP_SIZE = {1: 5, 2: 4, 3: 2, 4: 4, 5: 1}


def site_kernel(
    wave, row_ops, col_ops, count, source, target, energy_row,
    stepped_o, root_o, level_o, exact_o, energy_o,
    wide, row_v, col_v, table, table_in, table_s, order_s, source_s, prefix,
    part, near, whole, near2, whole2, total, summed, stepped, gram, my, mm, mu, mz, roots, level_two, exact, scalars, energy_col,
    wv_send, wv_recv, swap_send, swap_recv,
    rs_send, rs_recv, mod_send, mod_recv, rs2_send, rs2_recv, ag_send, ag_recv, en_send, en_recv, st_send, st_recv, st_own,
    end_send, end_recv, own_sem,
):
    x, z, c, y = lax.axis_index("x"), lax.axis_index("z"), lax.axis_index("core"), lax.axis_index("sec")
    b = x * 4 + z
    sib = {"core": 1 - c}
    mine = pl.ds(pl.multiple_of(c * SEC, SEC), SEC)
    other = pl.ds(pl.multiple_of((1 - c) * SEC, SEC), SEC)
    columns = pl.ds(pl.multiple_of(c * 128, 128), 128)
    other_columns = pl.ds(pl.multiple_of((1 - c) * 128, 128), 128)
    own_slots, sib_slots = pl.ds(0, 4), pl.ds(4, 4)
    own_wave = pltpu.make_async_copy(wave.at[mine, :], wide.at[b, :, columns], own_sem.at[0])
    own_wave.start()
    lane = lax.broadcasted_iota(jnp.int32, (8, 128), 1)
    numbers = jnp.where(lane == 0, count[0], 0)
    for k in range(4):
        numbers = jnp.where(lane == 1 + k, source[k], numbers)
        numbers = jnp.where(lane == 5 + k, target[k], numbers)
    table[...] = numbers
    greet(
        ring_peers(x, z)
        + [sib, {"x": turn(x, 2)}, {"z": turn(z, 2)}, {"sec": turn(y, 1)}, {"sec": turn(y, 2)}, {"sec": turn(y, -1)}]
    )
    swaps = [
        push(wave.at[other, :], wide.at[b, :, columns], swap_send.at[0], swap_recv.at[0], sib),
        push(table, table_in, swap_send.at[1], swap_recv.at[1], sib),
        push(row_ops.at[:, other, :], row_v.at[sib_slots], swap_send.at[2], swap_recv.at[2], sib),
        push(col_ops, col_v.at[sib_slots], swap_send.at[3], swap_recv.at[3], sib),
    ]
    swaps[0].start()
    own_wave.wait()
    push(wave.at[other, :], wide.at[b, :, other_columns], swap_send.at[0], swap_recv.at[0], sib).wait_recv()
    steps = all_blocks(wide, x, z, wv_send, wv_recv)
    next(steps)
    for swap in swaps[1:]:
        swap.start()
    own_rows = pltpu.make_async_copy(row_ops.at[:, mine, :], row_v.at[own_slots], own_sem.at[1])
    own_cols = pltpu.make_async_copy(col_ops, col_v.at[own_slots], own_sem.at[5])
    own_rows.start()
    own_cols.start()
    same = lax.broadcasted_iota(jnp.int32, (128, 128), 0) == lax.broadcasted_iota(jnp.int32, (128, 128), 1)
    for i in range(4):
        spread = jnp.where(same, jnp.broadcast_to(energy_row[pl.ds(c * 4 + i, 1), :], (128, 128)), 0.0)
        energy_col[pl.ds(i * 128, 128), :] = jnp.sum(spread, axis=1, keepdims=True)
    swaps[1].wait_recv()
    to_scalars = pltpu.make_async_copy(table_in, table_s, own_sem.at[6])
    to_scalars.start()
    to_scalars.wait()

    def flag(condition):
        return condition.astype(jnp.int32)

    keys, sources = [], []
    for side in (0, 1):
        live = table_s[0, 0] if side else count[0]
        for k in range(4):
            alive = flag(k < live)
            aim = table_s[0, 5 + k] if side else target[k]
            keys.append(aim * alive + 8 * (1 - alive))
            sources.append(table_s[0, 1 + k] if side else source[k])
    ranks = []
    for i in range(8):
        ahead = [flag(keys[j] <= keys[i]) if j < i else flag(keys[j] < keys[i]) for j in range(8) if j != i]
        ranks.append(sum(ahead))
    for j in range(8):
        order_s[j] = sum(i * flag(ranks[i] == j) for i in range(8))
        source_s[j] = sum(sources[i] * flag(ranks[i] == j) for i in range(8))
    starts = [sum(flag(key < t) for key in keys) for t in range(9)]

    for ready in steps:
        del ready
    swaps[0].wait_send()
    swaps[1].wait_send()
    own_rows.wait()
    own_cols.wait()
    swaps[2].wait()
    swaps[3].wait()

    reduction = Reduction(
        (part, near, whole, near2, whole2, total), (rs_send, rs_recv, mod_send, mod_recv, rs2_send, rs2_recv), x, z
    )
    prefix[0] = jnp.zeros((HALF, SEC), F32)
    for h in (0, 1):
        here = pl.ds(h * HALF, HALF)

        def term(j, carry, here=here):
            slot = order_s[j]
            src = source_s[j] * 2
            rows = row_v[slot, here, :]
            first = dot(rows, wide[src]).astype(BF16)
            second = dot(rows, wide[src + 1]).astype(BF16)
            prefix[j + 1] = prefix[j] + (dot(first, col_v[slot, :WIDE, :]) + dot(second, col_v[slot, WIDE:, :]))
            return carry

        lax.fori_loop(0, 8, term, 0)
        for t in range(8):
            added = (prefix[starts[t + 1]] - prefix[starts[t]]).astype(BF16)
            part[t // 2, 2 * (t % 2), here, :] = added[:, :WIDE]
            part[t // 2, 2 * (t % 2) + 1, here, :] = added[:, WIDE:]
        reduction.begin(h)

    for work in (reduction.add, reduction.second, reduction.add2, reduction.finish):
        work(0)
        work(1)
    reduction.close()
    summed[b] = total[...].astype(BF16)
    steps = all_blocks(summed, x, z, ag_send, ag_recv)
    next(steps)
    level = energy_col[...]
    amplitude = wide[b].astype(F32)
    applied = level * amplitude + total[...]
    share = jnp.sum(amplitude * applied, axis=(0, 1), keepdims=True)

    stages = (("sec", y, 4), ("x", x, 4), ("z", z, 4), ("core", c, 2))

    def energy_copies(s):
        name, place, size = stages[s]
        for hop in range(1, size):
            to = {name: lax.rem(place + hop, size)}
            src = lax.rem(place + (size - hop), size)
            yield (
                push(scalars.at[s, place], scalars.at[s, place], en_send.at[s, hop], en_recv.at[s, hop], to),
                push(scalars.at[s, src], scalars.at[s, src], en_send.at[s, hop], en_recv.at[s, hop], to),
            )

    groups = []
    for s in range(4):
        place, size = stages[s][1:]
        scalars[s, place] = jnp.broadcast_to(share, (8, 128))
        for out, unused in energy_copies(s):
            out.start()
        ready = next(steps)
        groups += [ready] if ready else []
        for out, arriving in energy_copies(s):
            arriving.wait_recv()
            out.wait_send()
        share = scalars[s, 0] + scalars[s, 1]
        if size == 4:
            share = (share + scalars[s, 2]) + scalars[s, 3]
        share = share[0:1, 0:1]
    energy = share * (1.0 / ENTRIES)
    energy_o[...] = jnp.broadcast_to(energy, (8, 128))
    own = amplitude + 0.5 * (energy * amplitude - applied)
    exact[0] = own[:, :128]
    exact[1] = own[:, 128:]
    exact_send = push(exact.at[1 - c], exact_o.at[mine, :], end_send.at[0], end_recv.at[0], sib)
    exact_own = pltpu.make_async_copy(exact.at[c], exact_o.at[mine, :], own_sem.at[2])
    exact_send.start()
    exact_own.start()

    def out_block(i):
        return (
            push(stepped.at[i], stepped_o.at[c, i], st_send.at[i], st_recv.at[i], sib),
            pltpu.make_async_copy(stepped.at[i], stepped_o.at[c, i], st_own.at[i]),
        )

    gram[...] = jnp.zeros((SEC, SEC), F32)

    def add_group(group):
        def one_block(t, carry):
            i = group_block(group, t, x, z)
            part_of = wide[i].astype(F32)
            value = part_of + 0.5 * (energy * part_of - (level * part_of + summed[i].astype(F32)))
            value = value.astype(BF16)
            stepped[i] = value
            for one in out_block(i):
                one.start()
            gram[...] += dot_t(value, value)
            return carry

        lax.fori_loop(0, GROUP_SIZE[group], one_block, 0)

    for group in groups:
        add_group(group)
    for ready in steps:
        if ready:
            add_group(ready)

    def root(y_ref, d_ref, again):
        my[...] = 1.5 * y_ref[...] - 0.5 * rough(y_ref[...], y_ref[...])
        mu[...] = 1.5 * my[...] - 0.5 * rough(y_ref[...], my[...])
        d_ref[...] = 0.25 * rough(mu[...], y_ref[...]) - 0.75 * (y_ref[...] + mu[...])
        if again:
            y_ref[...] = 1.5 * my[...] - 0.5 * rough(my[...], mu[...])

    gram_one = gram[...] * (1.0 / COLS)
    scale_one = frobenius(gram_one)
    gram[...] = gram_one / scale_one
    root(gram, mz, True)
    gram_two = 2.25 * gram[...] + rough(mz[...], gram[...])
    scale_two = frobenius(gram_two)
    gram[...] = gram_two / scale_two
    root(gram, mm, False)
    size = jnp.sqrt(scale_one) * jnp.sqrt(scale_two)
    roots[...] = ((2.25 * (mz[...] + mm[...]) + rough(mm[...], mz[...])) / size).astype(BF16)
    level_two[...] = jnp.broadcast_to(2.25 * 2.25 / size, (8, 128))
    root_send = push(roots, root_o.at[c], end_send.at[1], end_recv.at[1], sib)
    root_own = pltpu.make_async_copy(roots, root_o.at[c], own_sem.at[3])
    level_send = push(level_two, level_o.at[c], end_send.at[2], end_recv.at[2], sib)
    level_own = pltpu.make_async_copy(level_two, level_o.at[c], own_sem.at[4])
    level_send.start()
    level_own.start()
    root_send.start()
    root_own.start()

    def block_done(i, carry):
        going, staying = out_block(i)
        going.wait_send()
        staying.wait()
        push(stepped.at[i], stepped_o.at[1 - c, i], st_send.at[i], st_recv.at[i], sib).wait_recv()
        return carry

    lax.fori_loop(0, CHIPS, block_done, 0)
    exact_send.wait_send()
    exact_own.wait()
    push(exact.at[1 - c], exact_o.at[other, :], end_send.at[0], end_recv.at[0], sib).wait_recv()
    root_send.wait_send()
    root_own.wait()
    push(roots, root_o.at[1 - c], end_send.at[1], end_recv.at[1], sib).wait_recv()
    level_send.wait_send()
    level_own.wait()
    push(level_two, level_o.at[1 - c], end_send.at[2], end_recv.at[2], sib).wait_recv()


def site(wave, row_ops, col_ops, count, source, target, energy_row):
    hbm = pl.BlockSpec(memory_space=pltpu.HBM)
    smem = pl.BlockSpec(memory_space=pltpu.SMEM)
    vmem = pl.BlockSpec(memory_space=pltpu.VMEM)
    square = pltpu.VMEM((SEC, SEC), F32)
    blocks = pltpu.VMEM((CHIPS, SEC, WIDE), BF16)
    dma = pltpu.SemaphoreType.DMA
    return pl.pallas_call(
        site_kernel,
        out_shape=(
            jax.ShapeDtypeStruct((2, CHIPS, SEC, WIDE), BF16),
            jax.ShapeDtypeStruct((2, SEC, SEC), BF16),
            jax.ShapeDtypeStruct((2, 8, 128), F32),
            jax.ShapeDtypeStruct((2 * SEC, 128), F32),
            jax.ShapeDtypeStruct((8, 128), F32),
        ),
        in_specs=[hbm] * 3 + [smem] * 3 + [vmem],
        out_specs=(hbm, hbm, hbm, hbm, vmem),
        scratch_shapes=[
            blocks,
            pltpu.VMEM((8, SEC, SEC), BF16),
            pltpu.VMEM((8, SEC, SEC), BF16),
            pltpu.VMEM((8, 128), jnp.int32),
            pltpu.VMEM((8, 128), jnp.int32),
            pltpu.SMEM((8, 128), jnp.int32),
            pltpu.SMEM((8,), jnp.int32),
            pltpu.SMEM((8,), jnp.int32),
            pltpu.VMEM((9, HALF, SEC), F32),
            pltpu.VMEM((4, 4, SEC, WIDE), BF16),
            pltpu.VMEM((2, 2, 2, 4, EIGHTH, WIDE), BF16),
            pltpu.VMEM((2, 2, 2, 4, QUARTER, WIDE), BF16),
            pltpu.VMEM((2, 2, 2, EIGHTH, WIDE), BF16),
            pltpu.VMEM((2, 2, 2, QUARTER, WIDE), BF16),
            pltpu.VMEM((SEC, WIDE), F32),
            blocks,
            blocks,
            square,
            square,
            square,
            square,
            square,
            pltpu.VMEM((SEC, SEC), BF16),
            pltpu.VMEM((8, 128), F32),
            pltpu.VMEM((2, SEC, 128), F32),
            pltpu.VMEM((4, 4, 8, 128), F32),
            pltpu.VMEM((SEC, 1), F32),
            dma((2, 20)),
            dma((2, 20)),
            dma((4,)),
            dma((4,)),
            dma((2, 2, 4)),
            dma((2, 2, 4)),
            dma((2, 2, 2, 4)),
            dma((2, 2, 2, 4)),
            dma((2, 2, 6)),
            dma((2, 2, 6)),
            dma((2, 20)),
            dma((2, 20)),
            dma((4, 4)),
            dma((4, 4)),
            dma((CHIPS,)),
            dma((CHIPS,)),
            dma((CHIPS,)),
            dma((3,)),
            dma((3,)),
            dma((7,)),
        ],
        compiler_params=pltpu.CompilerParams(
            collective_id=0, has_side_effects=True, vmem_limit_bytes=60 * MIB
        ),
        name="site",
    )(wave, row_ops, col_ops, count, source, target, energy_row)


def renorm_kernel(
    count, source, target, stepped, cols, root, level, exact, energy,
    out, wave_o, energy_o,
    block_v, cols_v, root_v, out_v, zero_v, exact_v, wave_v, block_sem, cols_sem, root_sem, out_sem, exact_sem, wave_sem,
):
    energy_o[0] = energy[0, 0]

    def needs(k, s):
        pair = (source[k], target[k])
        return [
            pltpu.make_async_copy(
                stepped.at[s, pl.ds(2 * pair[e], 2)], block_v.at[k, s, e], block_sem.at[k, s, e]
            )
            for e in (0, 1)
        ]

    def column_op(k):
        return pltpu.make_async_copy(cols.at[k], cols_v.at[k], cols_sem.at[k])

    def result(k, s):
        return pltpu.make_async_copy(out_v.at[k, s], out.at[k, pl.ds(s * SEC, SEC), :], out_sem.at[k, s])

    def nothing(k, s):
        return pltpu.make_async_copy(zero_v, out.at[k, pl.ds(s * SEC, SEC), :], out_sem.at[k, s])

    roots = [pltpu.make_async_copy(root.at[s], root_v.at[s], root_sem.at[s]) for s in (0, 1)]
    roots[0].start()
    for k in range(4):

        @pl.when(k < count[0])
        def fetch(k=k):
            column_op(k).start()
            for s in (0, 1):
                for one in needs(k, s):
                    one.start()

        if k == 0:
            roots[1].start()
    zero_v[...] = jnp.zeros_like(zero_v)
    for k in range(1, 4):

        @pl.when(k >= count[0])
        def clear(k=k):
            nothing(k, 0).start()
            nothing(k, 1).start()

    load_exact = pltpu.make_async_copy(exact, exact_v, exact_sem)
    load_exact.start()
    for one in roots:
        one.wait()

    def one_term(k, carry):
        column_op(k).wait()
        for s in (0, 1):
            scale = level[s, 0:1, 0:1]
            for one in needs(k, s):
                one.wait()
            halves = []
            for e in (0, 1):
                block = jnp.concatenate([block_v[k, s, e, 0], block_v[k, s, e, 1]], axis=1)
                halves.append((scale * block.astype(F32) + dot(root_v[s], block)).astype(BF16))
            product = dot(halves[0], cols_v[k]).astype(BF16)
            out_v[k, s] = dot_t(product, halves[1]) * SEC ** (-0.5)
            result(k, s).start()
        return carry

    lax.fori_loop(0, count[0], one_term, 0)
    load_exact.wait()
    waves = []
    for s in (0, 1):
        rows = pl.ds(s * SEC, SEC)
        own = exact_v[rows, :]
        wave_v[rows, :] = level[s, 0:1, 0:1] * own + dot(root_v[s], own.astype(BF16))
        waves.append(pltpu.make_async_copy(wave_v.at[rows, :], wave_o.at[rows, :], wave_sem.at[s]))
        waves[s].start()
    for one in waves:
        one.wait()
    for k in range(4):
        for s in (0, 1):
            result(k, s).wait()


def renorm(count, source, target, stepped, cols, root, level, exact, energy):
    hbm = pl.BlockSpec(memory_space=pltpu.HBM)
    vmem = pl.BlockSpec(memory_space=pltpu.VMEM)
    smem = pl.BlockSpec(memory_space=pltpu.SMEM)
    return pl.pallas_call(
        renorm_kernel,
        out_shape=(
            jax.ShapeDtypeStruct((4, 2 * SEC, SEC), F32),
            jax.ShapeDtypeStruct((2 * SEC, 128), F32),
            jax.ShapeDtypeStruct((1,), F32),
        ),
        in_specs=[smem] * 3 + [hbm] * 3 + [vmem, hbm, smem],
        out_specs=(hbm, hbm, smem),
        scratch_shapes=[
            pltpu.VMEM((4, 2, 2, 2, SEC, WIDE), BF16),
            pltpu.VMEM((4, SEC, SEC), BF16),
            pltpu.VMEM((2, SEC, SEC), BF16),
            pltpu.VMEM((4, 2, SEC, SEC), F32),
            pltpu.VMEM((SEC, SEC), F32),
            pltpu.VMEM((2 * SEC, 128), F32),
            pltpu.VMEM((2 * SEC, 128), F32),
            pltpu.SemaphoreType.DMA((4, 2, 2)),
            pltpu.SemaphoreType.DMA((4,)),
            pltpu.SemaphoreType.DMA((2,)),
            pltpu.SemaphoreType.DMA((4, 2)),
            pltpu.SemaphoreType.DMA(()),
            pltpu.SemaphoreType.DMA((2,)),
        ],
        compiler_params=pltpu.CompilerParams(vmem_limit_bytes=60 * MIB),
        name="renorm",
    )(count, source, target, stepped, cols, root, level, exact, energy)


def on_device(wave_in, row_energy, row_operators, column_operators, term_count, source, target):
    stepped, root, level, exact, energy = site(
        wave_in, row_operators, column_operators, term_count, source, target, row_energy.reshape(8, 128)
    )
    renormalized, wave_next, energy = renorm(
        term_count, source, target, stepped, column_operators, root, level, exact, energy
    )
    return (wave_next, renormalized, energy.reshape(()))


def solution(mesh):
    torus = Mesh(mesh.devices.reshape(4, 4, 2, mesh.shape["sec"]), ("x", "z", "core", "sec"))
    return jax.shard_map(
        on_device,
        mesh=torus,
        in_specs=(
            P("sec", OPS),
            P("sec"),
            P(OPS, "sec", None),
            P(OPS, None, None),
            P(OPS),
            P(OPS),
            P(OPS),
        ),
        out_specs=(P("sec", OPS), P(OPS, "sec", None), P()),
        check_vma=False,
    )
```

```python
import functools

import jax
import jax.numpy as jnp
from jax import lax
from jax.experimental import pallas as pl
from jax.experimental.pallas import tpu as pltpu
from jax.sharding import Mesh
from jax.sharding import PartitionSpec as P

SEC = 512
COLS = 4096
ENTRIES = 4096 * 4096
CHIPS = 16
WIDE = 256
HALF = 256
QUARTER = 128
EIGHTH = 64
CUT = (3,)
MIB = 1 << 20
MESH = pl.DeviceIdType.MESH
OPS = ("x", "z", "core")
F32 = jnp.float32
BF16 = jnp.bfloat16


def turn(place, by):
    return lax.rem(place + (by + 4), 4)


def push(src, dst, send, recv, to):
    return pltpu.make_async_remote_copy(
        src_ref=src, dst_ref=dst, send_sem=send, recv_sem=recv, device_id=to, device_id_type=MESH
    )


def greet(peers):
    barrier = pltpu.get_barrier_semaphore()
    for peer in peers:
        pl.semaphore_signal(barrier, inc=1, device_id=peer, device_id_type=MESH)
    pl.semaphore_wait(barrier, len(peers))


def all_blocks(buf, x, z, send, recv, late=None, cut=(), apart=False):
    names = (("x", "z"), ("z", "x"))
    places = ((x, z), (z, x))
    every = slice(None)

    def block(h, pa, pb):
        return pa * 4 + pb if h == 0 else pb * 4 + pa

    def copy(h, j, pa, pb, part, axis, by, columns=every):
        rows = pl.ds(h * HALF, HALF) if part is None else pl.ds(h * HALF + part * QUARTER, QUARTER)
        ref = buf.at[block(h, pa, pb), rows, columns]
        to = {names[h][axis]: turn(places[h][axis], by)}
        return push(ref, ref, send.at[h, j], recv.at[h, j], to)

    def order(h):
        p = places[h][0]
        return (p, turn(p, -1), turn(p, 1), turn(p, 2))

    sent = []

    def go(*what):
        one = copy(*what)
        one.start()
        sent.append(one)

    def arrived(h, j, pa, pb, part, columns=every):
        copy(h, j, pa, pb, part, 0, 1, columns).wait_recv()

    def across(h, i):
        pa, q = order(h)[i], places[h][1]
        for d in (0, 1):
            for n in (0, 1) if i in cut else (0,):
                part = (d + n) % 2 if i in cut else None
                go(h, 8 + 4 * i + 2 * d + n, pa, q, part, 1, 1 - 2 * d)

    def across_arrived(h, i, d, n):
        part = (d + n) % 2 if i in cut else None
        arrived(h, 8 + 4 * i + 2 * d + n, order(h)[i], turn(places[h][1], 2 * d - 1), part)

    def onward(h, i):
        pa, q = order(h)[i], places[h][1]
        for d in (0, 1):
            across_arrived(h, i, d, 0)
            go(h, 24 + 2 * i + d, pa, turn(q, 2 * d - 1), d, 1, 1 - 2 * d)

    def rest(h, i):
        if i in cut:
            across_arrived(h, i, 0, 1)
            across_arrived(h, i, 1, 1)

    def first(h, columns, j):
        p, q = places[h]
        go(h, j, p, q, None, 0, 1, columns)
        go(h, j + 1, p, q, None, 0, -1, columns)

    if late is None:
        for h in (0, 1):
            first(h, every, 0)
            if apart:
                across(h, 0)
                yield
    else:
        for h in (0, 1):
            first(h, late[0], 0)
        late[2]()
        for h in (0, 1):
            first(h, late[1], 2)
    if not apart:
        for h in (0, 1):
            across(h, 0)
        yield
    for h in (0, 1):
        p, q = places[h]
        for d in (0, 1):
            side = turn(p, 2 * d - 1)
            if late is None:
                arrived(h, d, side, q, None)
            else:
                arrived(h, d, side, q, None, late[0])
                arrived(h, 2 + d, side, q, None, late[1])
            go(h, 4 + d, side, q, d, 0, 1 - 2 * d)
    for h in (0, 1):
        across(h, 1)
        across(h, 2)
    yield
    for h in (0, 1):
        onward(h, 0)
    for h in (0, 1):
        rest(h, 0)
    yield 1
    for h in (0, 1):
        p, q = places[h]
        arrived(h, 4, turn(p, 2), q, 0)
        arrived(h, 5, turn(p, 2), q, 1)
        across(h, 3)
    yield
    for h in (0, 1):
        onward(h, 1)
    yield
    for h in (0, 1):
        onward(h, 2)
    for h in (0, 1):
        rest(h, 1)
        rest(h, 2)
    yield 2

    def last(i):
        for h in (0, 1):
            pa, far = order(h)[i], turn(places[h][1], 2)
            arrived(h, 24 + 2 * i, pa, far, 0)
            arrived(h, 25 + 2 * i, pa, far, 1)

    last(0)
    yield 3
    for h in (0, 1):
        onward(h, 3)
    for h in (0, 1):
        rest(h, 3)
    last(1)
    last(2)
    yield 4
    last(3)
    yield 5
    for one in sent:
        one.wait_send()


def ring_peers(x, z):
    return [{"x": turn(x, 1)}, {"x": turn(x, -1)}, {"z": turn(z, 1)}, {"z": turn(z, -1)}]


def dot(a, b):
    return jnp.dot(a, b, preferred_element_type=F32)


def dot_t(a, b):
    return lax.dot_general(a, b, (((1,), (1,)), ((), ())), preferred_element_type=F32)


def rough(a, b):
    return dot(a.astype(BF16), b.astype(BF16))


class Reduction:
    def __init__(self, bufs, sems, x, z):
        self.part, self.near, self.whole, self.near2, self.whole2, self.total = bufs
        self.send, self.recv, self.mod_send, self.mod_recv, self.send2, self.recv2 = sems
        self.places = ((z, x), (x, z))
        self.sent = []

    def at(self, h, pa, pb):
        return (pb, pa) if h == 0 else (pa, pb)

    def rows(self, w, h, half):
        return pl.ds(w * HALF + h * QUARTER + half * EIGHTH, EIGHTH)

    def both_rows(self, w, h):
        return pl.ds(w * HALF + h * QUARTER, QUARTER)

    def line(self, w, h, pa, half):
        rows = self.rows(w, h, half)
        return self.part.at[:, pa, rows, :] if h == 0 else self.part.at[pa, :, rows, :]

    def order(self, h):
        q = self.places[h][1]
        return (turn(q, 2), turn(q, 1), turn(q, -1), q)

    def peer(self, h, axis, d):
        return {("zx", "xz")[h][axis]: turn(self.places[h][axis], 1 - 2 * d)}

    def go(self, one):
        one.start()
        self.sent.append(one)

    def near_copy(self, w, h, d):
        src = self.line(w, h, turn(self.places[h][0], 2), d)
        return push(src, self.near.at[w, h, d], self.send.at[w, h, d], self.recv.at[w, h, d], self.peer(h, 0, d))

    def plain_copy(self, w, h, d):
        src = self.line(w, h, turn(self.places[h][0], 1 - 2 * d), 1 - d)
        dst = self.whole.at[w, h, d, :, pl.ds((1 - d) * EIGHTH, EIGHTH), :]
        return push(src, dst, self.send.at[w, h, 2 + d], self.recv.at[w, h, 2 + d], self.peer(h, 0, d))

    def added_copy(self, w, h, d, i):
        to = self.order(h)[i]
        src = self.part.at[*self.at(h, turn(self.places[h][0], 1 - 2 * d), to), self.rows(w, h, d), :]
        dst = self.whole.at[w, h, d, to, pl.ds(d * EIGHTH, EIGHTH), :]
        return push(src, dst, self.mod_send.at[w, h, d, i], self.mod_recv.at[w, h, d, i], self.peer(h, 0, d))

    def near2_copy(self, w, h, d):
        p, q = self.places[h]
        src = self.part.at[*self.at(h, p, turn(q, 2)), self.rows(w, h, d), :]
        return push(src, self.near2.at[w, h, d], self.send2.at[w, h, d], self.recv2.at[w, h, d], self.peer(h, 1, d))

    def whole2_copy(self, w, h, d, half):
        p, q = self.places[h]
        j = 2 + 2 * d + half
        src = self.part.at[*self.at(h, p, turn(q, 1 - 2 * d)), self.rows(w, h, half), :]
        dst = self.whole2.at[w, h, d, pl.ds(half * EIGHTH, EIGHTH), :]
        return push(src, dst, self.send2.at[w, h, j], self.recv2.at[w, h, j], self.peer(h, 1, d))

    def begin(self, w):
        for h in (0, 1):
            for d in (0, 1):
                self.go(self.near_copy(w, h, d))
        for h in (0, 1):
            for d in (0, 1):
                self.go(self.plain_copy(w, h, d))

    def add(self, w):
        for h in (0, 1):
            p = self.places[h][0]
            for d in (0, 1):
                self.near_copy(w, h, d).wait_recv()
                for i in range(4):
                    to = self.order(h)[i]
                    spot = (*self.at(h, turn(p, 1 - 2 * d), to), self.rows(w, h, d), slice(None))
                    both = self.part[spot].astype(F32) + self.near[w, h, d, to].astype(F32)
                    self.part[spot] = both.astype(BF16)
                    self.go(self.added_copy(w, h, d, i))

    def second(self, w):
        for h in (0, 1):
            for d in (0, 1):
                self.plain_copy(w, h, d).wait_recv()
        for i in range(4):
            for h in (0, 1):
                p = self.places[h][0]
                for d in (0, 1):
                    self.added_copy(w, h, d, i).wait_recv()
                to = self.order(h)[i]
                spot = (*self.at(h, p, to), self.both_rows(w, h), slice(None))
                done = self.part[spot].astype(F32) + self.whole[w, h, 0, to].astype(F32) + self.whole[w, h, 1, to].astype(F32)
                if i == 3:
                    self.total[self.both_rows(w, h), :] = done
                else:
                    self.part[spot] = done.astype(BF16)
                if i == 0:
                    self.go(self.near2_copy(w, h, 0))
                    self.go(self.near2_copy(w, h, 1))
                if i == 1:
                    self.go(self.whole2_copy(w, h, 0, 1))
                if i == 2:
                    self.go(self.whole2_copy(w, h, 1, 0))

    def add2(self, w):
        for h in (0, 1):
            p, q = self.places[h]
            for d in (0, 1):
                self.near2_copy(w, h, d).wait_recv()
                spot = (*self.at(h, p, turn(q, 1 - 2 * d)), self.rows(w, h, d), slice(None))
                both = self.part[spot].astype(F32) + self.near2[w, h, d].astype(F32)
                self.part[spot] = both.astype(BF16)
                self.go(self.whole2_copy(w, h, d, d))

    def finish(self, w):
        for h in (0, 1):
            for d in (0, 1):
                for half in (0, 1):
                    self.whole2_copy(w, h, d, half).wait_recv()
            here = self.both_rows(w, h)
            self.total[here, :] += self.whole2[w, h, 0].astype(F32) + self.whole2[w, h, 1].astype(F32)

    def close(self):
        for one in self.sent:
            one.wait_send()


def frobenius(a):
    return jnp.sqrt(jnp.sum(a * a, axis=(0, 1), keepdims=True) + 1e-06)


def group_block(group, t, x, z):
    if group == 1:
        dx = (t == 1).astype(jnp.int32) - (t == 2).astype(jnp.int32)
        dz = (t == 3).astype(jnp.int32) - (t == 4).astype(jnp.int32)
    elif group == 2:
        dx, dz = 1 - 2 * lax.rem(t, 2), 1 - 2 * lax.div(t, 2)
    elif group == 3:
        dx, dz = 2 - 2 * t, 2 * t
    elif group == 4:
        dx, dz = jnp.where(t < 2, 1 - 2 * t, 2), jnp.where(t < 2, 2, 5 - 2 * t)
    else:
        dx = dz = 2
    return turn(x, dx) * 4 + turn(z, dz)


GROUP_SIZE = {1: 5, 2: 4, 3: 2, 4: 4, 5: 1}


def site_kernel(
    wave, row_ops, col_ops, count, source, target, energy_row,
    stepped_o, root_o, level_o, exact_o, energy_o,
    wide, row_v, col_v, table, table_in, table_s, order_s, source_s, prefix,
    part, near, whole, near2, whole2, total, summed, stepped, gram, my, mm, mu, mz, roots, level_two, exact, scalars, energy_col,
    wv_send, wv_recv, swap_send, swap_recv,
    rs_send, rs_recv, mod_send, mod_recv, rs2_send, rs2_recv, ag_send, ag_recv, en_send, en_recv, st_send, st_recv, st_own,
    end_send, end_recv, own_sem,
):
    x, z, c, y = lax.axis_index("x"), lax.axis_index("z"), lax.axis_index("core"), lax.axis_index("sec")
    b = x * 4 + z
    sib = {"core": 1 - c}
    mine = pl.ds(pl.multiple_of(c * SEC, SEC), SEC)
    other = pl.ds(pl.multiple_of((1 - c) * SEC, SEC), SEC)
    columns = pl.ds(pl.multiple_of(c * 128, 128), 128)
    other_columns = pl.ds(pl.multiple_of((1 - c) * 128, 128), 128)
    own_slots, sib_slots = pl.ds(0, 4), pl.ds(4, 4)
    own_wave = pltpu.make_async_copy(wave.at[mine, :], wide.at[b, :, columns], own_sem.at[0])
    own_wave.start()
    lane = lax.broadcasted_iota(jnp.int32, (8, 128), 1)
    numbers = jnp.where(lane == 0, count[0], 0)
    for k in range(4):
        numbers = jnp.where(lane == 1 + k, source[k], numbers)
        numbers = jnp.where(lane == 5 + k, target[k], numbers)
    table[...] = numbers
    greet(
        ring_peers(x, z)
        + [sib, {"x": turn(x, 2)}, {"z": turn(z, 2)}, {"sec": turn(y, 1)}, {"sec": turn(y, 2)}, {"sec": turn(y, -1)}]
    )
    swaps = [
        push(wave.at[other, :], wide.at[b, :, columns], swap_send.at[0], swap_recv.at[0], sib),
        push(table, table_in, swap_send.at[1], swap_recv.at[1], sib),
        push(row_ops.at[:, other, :], row_v.at[sib_slots], swap_send.at[2], swap_recv.at[2], sib),
        push(col_ops, col_v.at[sib_slots], swap_send.at[3], swap_recv.at[3], sib),
    ]
    swaps[0].start()
    own_wave.wait()

    def swapped():
        push(wave.at[other, :], wide.at[b, :, other_columns], swap_send.at[0], swap_recv.at[0], sib).wait_recv()

    steps = all_blocks(wide, x, z, wv_send, wv_recv, (columns, other_columns, swapped), CUT)
    next(steps)
    for swap in swaps[1:]:
        swap.start()
    own_rows = pltpu.make_async_copy(row_ops.at[:, mine, :], row_v.at[own_slots], own_sem.at[1])
    own_cols = pltpu.make_async_copy(col_ops, col_v.at[own_slots], own_sem.at[5])
    own_rows.start()
    own_cols.start()
    same = lax.broadcasted_iota(jnp.int32, (128, 128), 0) == lax.broadcasted_iota(jnp.int32, (128, 128), 1)
    for i in range(4):
        spread = jnp.where(same, jnp.broadcast_to(energy_row[pl.ds(c * 4 + i, 1), :], (128, 128)), 0.0)
        energy_col[pl.ds(i * 128, 128), :] = jnp.sum(spread, axis=1, keepdims=True)
    swaps[1].wait_recv()
    to_scalars = pltpu.make_async_copy(table_in, table_s, own_sem.at[6])
    to_scalars.start()
    to_scalars.wait()

    def flag(condition):
        return condition.astype(jnp.int32)

    keys, sources = [], []
    for side in (0, 1):
        live = table_s[0, 0] if side else count[0]
        for k in range(4):
            alive = flag(k < live)
            aim = table_s[0, 5 + k] if side else target[k]
            keys.append(aim * alive + 8 * (1 - alive))
            sources.append(table_s[0, 1 + k] if side else source[k])
    ranks = []
    for i in range(8):
        ahead = [flag(keys[j] <= keys[i]) if j < i else flag(keys[j] < keys[i]) for j in range(8) if j != i]
        ranks.append(sum(ahead))
    for j in range(8):
        order_s[j] = sum(i * flag(ranks[i] == j) for i in range(8))
        source_s[j] = sum(sources[i] * flag(ranks[i] == j) for i in range(8))
    starts = [sum(flag(key < t) for key in keys) for t in range(9)]

    for ready in steps:
        del ready
    swaps[0].wait_send()
    swaps[1].wait_send()
    own_rows.wait()
    own_cols.wait()
    swaps[2].wait()
    swaps[3].wait()

    reduction = Reduction(
        (part, near, whole, near2, whole2, total), (rs_send, rs_recv, mod_send, mod_recv, rs2_send, rs2_recv), x, z
    )
    prefix[0] = jnp.zeros((HALF, SEC), F32)
    for h in (0, 1):
        here = pl.ds(h * HALF, HALF)

        def term(j, carry, here=here):
            slot = order_s[j]
            src = source_s[j] * 2
            rows = row_v[slot, here, :]
            first = dot(rows, wide[src]).astype(BF16)
            second = dot(rows, wide[src + 1]).astype(BF16)
            prefix[j + 1] = prefix[j] + (dot(first, col_v[slot, :WIDE, :]) + dot(second, col_v[slot, WIDE:, :]))
            return carry

        lax.fori_loop(0, 8, term, 0)
        for t in range(8):
            added = (prefix[starts[t + 1]] - prefix[starts[t]]).astype(BF16)
            part[t // 2, 2 * (t % 2), here, :] = added[:, :WIDE]
            part[t // 2, 2 * (t % 2) + 1, here, :] = added[:, WIDE:]
        reduction.begin(h)

    for work in (reduction.add, reduction.second, reduction.add2):
        work(0)
        work(1)
    steps = all_blocks(summed, x, z, ag_send, ag_recv, None, CUT, True)
    for h in (0, 1):
        reduction.finish(h)
        here = pl.ds(h * HALF, HALF)
        summed[b, here, :] = total[here, :].astype(BF16)
        next(steps)
    reduction.close()
    level = energy_col[...]
    amplitude = wide[b].astype(F32)
    applied = level * amplitude + total[...]
    share = jnp.sum(amplitude * applied, axis=(0, 1), keepdims=True)

    stages = (("sec", y, 4), ("x", x, 4), ("z", z, 4), ("core", c, 2))

    def energy_copies(s):
        name, place, size = stages[s]
        for hop in range(1, size):
            to = {name: lax.rem(place + hop, size)}
            src = lax.rem(place + (size - hop), size)
            yield (
                push(scalars.at[s, place], scalars.at[s, place], en_send.at[s, hop], en_recv.at[s, hop], to),
                push(scalars.at[s, src], scalars.at[s, src], en_send.at[s, hop], en_recv.at[s, hop], to),
            )

    groups = []
    for s in range(4):
        place, size = stages[s][1:]
        scalars[s, place] = jnp.broadcast_to(share, (8, 128))
        for out, unused in energy_copies(s):
            out.start()
        ready = next(steps)
        groups += [ready] if ready else []
        for out, arriving in energy_copies(s):
            arriving.wait_recv()
            out.wait_send()
        share = scalars[s, 0] + scalars[s, 1]
        if size == 4:
            share = (share + scalars[s, 2]) + scalars[s, 3]
        share = share[0:1, 0:1]
    energy = share * (1.0 / ENTRIES)
    energy_o[...] = jnp.broadcast_to(energy, (8, 128))
    own = amplitude + 0.5 * (energy * amplitude - applied)
    exact[0] = own[:, :128]
    exact[1] = own[:, 128:]
    exact_send = push(exact.at[1 - c], exact_o.at[mine, :], end_send.at[0], end_recv.at[0], sib)
    exact_own = pltpu.make_async_copy(exact.at[c], exact_o.at[mine, :], own_sem.at[2])
    exact_send.start()
    exact_own.start()

    def out_block(i):
        return (
            push(stepped.at[i], stepped_o.at[c, i], st_send.at[i], st_recv.at[i], sib),
            pltpu.make_async_copy(stepped.at[i], stepped_o.at[c, i], st_own.at[i]),
        )

    gram[...] = jnp.zeros((SEC, SEC), F32)

    def add_group(group):
        def one_block(t, carry):
            i = group_block(group, t, x, z)
            part_of = wide[i].astype(F32)
            value = part_of + 0.5 * (energy * part_of - (level * part_of + summed[i].astype(F32)))
            value = value.astype(BF16)
            stepped[i] = value
            for one in out_block(i):
                one.start()
            gram[...] += dot_t(value, value)
            return carry

        lax.fori_loop(0, GROUP_SIZE[group], one_block, 0)

    for group in groups:
        add_group(group)
    for ready in steps:
        if ready:
            add_group(ready)

    def root(y_ref, d_ref, again):
        my[...] = 1.5 * y_ref[...] - 0.5 * rough(y_ref[...], y_ref[...])
        mu[...] = 1.5 * my[...] - 0.5 * rough(y_ref[...], my[...])
        d_ref[...] = 0.25 * rough(mu[...], y_ref[...]) - 0.75 * (y_ref[...] + mu[...])
        if again:
            y_ref[...] = 1.5 * my[...] - 0.5 * rough(my[...], mu[...])

    gram_one = gram[...] * (1.0 / COLS)
    scale_one = frobenius(gram_one)
    gram[...] = gram_one / scale_one
    root(gram, mz, True)
    gram_two = 2.25 * gram[...] + rough(mz[...], gram[...])
    scale_two = frobenius(gram_two)
    gram[...] = gram_two / scale_two
    root(gram, mm, False)
    size = jnp.sqrt(scale_one) * jnp.sqrt(scale_two)
    roots[...] = ((2.25 * (mz[...] + mm[...]) + rough(mm[...], mz[...])) / size).astype(BF16)
    level_two[...] = jnp.broadcast_to(2.25 * 2.25 / size, (8, 128))
    root_send = push(roots, root_o.at[c], end_send.at[1], end_recv.at[1], sib)
    root_own = pltpu.make_async_copy(roots, root_o.at[c], own_sem.at[3])
    level_send = push(level_two, level_o.at[c], end_send.at[2], end_recv.at[2], sib)
    level_own = pltpu.make_async_copy(level_two, level_o.at[c], own_sem.at[4])
    level_send.start()
    level_own.start()
    root_send.start()
    root_own.start()

    def block_done(i, carry):
        going, staying = out_block(i)
        going.wait_send()
        staying.wait()
        push(stepped.at[i], stepped_o.at[1 - c, i], st_send.at[i], st_recv.at[i], sib).wait_recv()
        return carry

    lax.fori_loop(0, CHIPS, block_done, 0)
    exact_send.wait_send()
    exact_own.wait()
    push(exact.at[1 - c], exact_o.at[other, :], end_send.at[0], end_recv.at[0], sib).wait_recv()
    root_send.wait_send()
    root_own.wait()
    push(roots, root_o.at[1 - c], end_send.at[1], end_recv.at[1], sib).wait_recv()
    level_send.wait_send()
    level_own.wait()
    push(level_two, level_o.at[1 - c], end_send.at[2], end_recv.at[2], sib).wait_recv()


def site(wave, row_ops, col_ops, count, source, target, energy_row):
    hbm = pl.BlockSpec(memory_space=pltpu.HBM)
    smem = pl.BlockSpec(memory_space=pltpu.SMEM)
    vmem = pl.BlockSpec(memory_space=pltpu.VMEM)
    square = pltpu.VMEM((SEC, SEC), F32)
    blocks = pltpu.VMEM((CHIPS, SEC, WIDE), BF16)
    dma = pltpu.SemaphoreType.DMA
    return pl.pallas_call(
        site_kernel,
        out_shape=(
            jax.ShapeDtypeStruct((2, CHIPS, SEC, WIDE), BF16),
            jax.ShapeDtypeStruct((2, SEC, SEC), BF16),
            jax.ShapeDtypeStruct((2, 8, 128), F32),
            jax.ShapeDtypeStruct((2 * SEC, 128), F32),
            jax.ShapeDtypeStruct((8, 128), F32),
        ),
        in_specs=[hbm] * 3 + [smem] * 3 + [vmem],
        out_specs=(hbm, hbm, hbm, hbm, vmem),
        scratch_shapes=[
            blocks,
            pltpu.VMEM((8, SEC, SEC), BF16),
            pltpu.VMEM((8, SEC, SEC), BF16),
            pltpu.VMEM((8, 128), jnp.int32),
            pltpu.VMEM((8, 128), jnp.int32),
            pltpu.SMEM((8, 128), jnp.int32),
            pltpu.SMEM((8,), jnp.int32),
            pltpu.SMEM((8,), jnp.int32),
            pltpu.VMEM((9, HALF, SEC), F32),
            pltpu.VMEM((4, 4, SEC, WIDE), BF16),
            pltpu.VMEM((2, 2, 2, 4, EIGHTH, WIDE), BF16),
            pltpu.VMEM((2, 2, 2, 4, QUARTER, WIDE), BF16),
            pltpu.VMEM((2, 2, 2, EIGHTH, WIDE), BF16),
            pltpu.VMEM((2, 2, 2, QUARTER, WIDE), BF16),
            pltpu.VMEM((SEC, WIDE), F32),
            blocks,
            blocks,
            square,
            square,
            square,
            square,
            square,
            pltpu.VMEM((SEC, SEC), BF16),
            pltpu.VMEM((8, 128), F32),
            pltpu.VMEM((2, SEC, 128), F32),
            pltpu.VMEM((4, 4, 8, 128), F32),
            pltpu.VMEM((SEC, 1), F32),
            dma((2, 32)),
            dma((2, 32)),
            dma((4,)),
            dma((4,)),
            dma((2, 2, 4)),
            dma((2, 2, 4)),
            dma((2, 2, 2, 4)),
            dma((2, 2, 2, 4)),
            dma((2, 2, 6)),
            dma((2, 2, 6)),
            dma((2, 32)),
            dma((2, 32)),
            dma((4, 4)),
            dma((4, 4)),
            dma((CHIPS,)),
            dma((CHIPS,)),
            dma((CHIPS,)),
            dma((3,)),
            dma((3,)),
            dma((7,)),
        ],
        compiler_params=pltpu.CompilerParams(
            collective_id=0, has_side_effects=True, vmem_limit_bytes=60 * MIB
        ),
        name="site",
    )(wave, row_ops, col_ops, count, source, target, energy_row)


def renorm_kernel(
    count, source, target, stepped, cols, root, level, exact, energy,
    out, wave_o, energy_o,
    block_v, cols_v, root_v, out_v, zero_v, exact_v, wave_v, level_v, block_sem, cols_sem, root_sem, out_sem, exact_sem, wave_sem, level_sem,
):
    energy_o[0] = energy[0, 0]

    def needs(k, s):
        pair = (source[k], target[k])
        return [
            pltpu.make_async_copy(
                stepped.at[s, pl.ds(2 * pair[e], 2)], block_v.at[k, s, e], block_sem.at[k, s, e]
            )
            for e in (0, 1)
        ]

    def column_op(k):
        return pltpu.make_async_copy(cols.at[k], cols_v.at[k], cols_sem.at[k])

    def result(k, s):
        return pltpu.make_async_copy(out_v.at[k, s], out.at[k, pl.ds(s * SEC, SEC), :], out_sem.at[k, s])

    def nothing(k, s):
        return pltpu.make_async_copy(zero_v, out.at[k, pl.ds(s * SEC, SEC), :], out_sem.at[k, s])

    roots = [pltpu.make_async_copy(root.at[s], root_v.at[s], root_sem.at[s]) for s in (0, 1)]
    load_level = pltpu.make_async_copy(level, level_v, level_sem)
    load_level.start()
    roots[0].start()
    for one in needs(0, 0):
        one.start()
    column_op(0).start()
    roots[1].start()
    for one in needs(0, 1):
        one.start()
    zero_v[...] = jnp.zeros_like(zero_v)
    load_exact = pltpu.make_async_copy(exact, exact_v, exact_sem)
    load_level.wait()
    roots[0].wait()

    def one_term(k, carry):
        column_op(k).wait()
        for s in (0, 1):
            scale = level_v[s, 0:1, 0:1]
            for one in needs(k, s):
                one.wait()
            if s == 0:

                @pl.when(k + 1 < count[0])
                def ahead():
                    column_op(k + 1).start()
                    for t in (0, 1):
                        for one in needs(k + 1, t):
                            one.start()

                @pl.when(k == 0)
                def others():
                    load_exact.start()
                    for empty in range(1, 4):

                        @pl.when(empty >= count[0])
                        def clear(empty=empty):
                            nothing(empty, 0).start()
                            nothing(empty, 1).start()
            else:

                @pl.when(k == 0)
                def second_root():
                    roots[1].wait()
            halves = []
            for e in (0, 1):
                block = jnp.concatenate([block_v[k, s, e, 0], block_v[k, s, e, 1]], axis=1)
                halves.append((scale * block.astype(F32) + dot(root_v[s], block)).astype(BF16))
            product = dot(halves[0], cols_v[k]).astype(BF16)
            out_v[k, s] = dot_t(product, halves[1]) * SEC ** (-0.5)
            result(k, s).start()
        return carry

    lax.fori_loop(0, count[0], one_term, 0)
    load_exact.wait()
    waves = []
    for s in (0, 1):
        rows = pl.ds(s * SEC, SEC)
        own = exact_v[rows, :]
        wave_v[rows, :] = level_v[s, 0:1, 0:1] * own + dot(root_v[s], own.astype(BF16))
        waves.append(pltpu.make_async_copy(wave_v.at[rows, :], wave_o.at[rows, :], wave_sem.at[s]))
        waves[s].start()
    for one in waves:
        one.wait()
    for k in range(4):
        for s in (0, 1):
            result(k, s).wait()


def renorm(count, source, target, stepped, cols, root, level, exact, energy):
    hbm = pl.BlockSpec(memory_space=pltpu.HBM)
    smem = pl.BlockSpec(memory_space=pltpu.SMEM)
    return pl.pallas_call(
        renorm_kernel,
        out_shape=(
            jax.ShapeDtypeStruct((4, 2 * SEC, SEC), F32),
            jax.ShapeDtypeStruct((2 * SEC, 128), F32),
            jax.ShapeDtypeStruct((1,), F32),
        ),
        in_specs=[smem] * 3 + [hbm] * 5 + [smem],
        out_specs=(hbm, hbm, smem),
        scratch_shapes=[
            pltpu.VMEM((4, 2, 2, 2, SEC, WIDE), BF16),
            pltpu.VMEM((4, SEC, SEC), BF16),
            pltpu.VMEM((2, SEC, SEC), BF16),
            pltpu.VMEM((4, 2, SEC, SEC), F32),
            pltpu.VMEM((SEC, SEC), F32),
            pltpu.VMEM((2 * SEC, 128), F32),
            pltpu.VMEM((2 * SEC, 128), F32),
            pltpu.VMEM((2, 8, 128), F32),
            pltpu.SemaphoreType.DMA((4, 2, 2)),
            pltpu.SemaphoreType.DMA((4,)),
            pltpu.SemaphoreType.DMA((2,)),
            pltpu.SemaphoreType.DMA((4, 2)),
            pltpu.SemaphoreType.DMA(()),
            pltpu.SemaphoreType.DMA((2,)),
            pltpu.SemaphoreType.DMA(()),
        ],
        compiler_params=pltpu.CompilerParams(vmem_limit_bytes=60 * MIB),
        name="renorm",
    )(count, source, target, stepped, cols, root, level, exact, energy)


def on_device(wave_in, row_energy, row_operators, column_operators, term_count, source, target):
    stepped, root, level, exact, energy = site(
        wave_in, row_operators, column_operators, term_count, source, target, row_energy.reshape(8, 128)
    )
    renormalized, wave_next, energy = renorm(
        term_count, source, target, stepped, column_operators, root, level, exact, energy
    )
    return (wave_next, renormalized, energy.reshape(()))


def solution(mesh):
    torus = Mesh(mesh.devices.reshape(4, 4, 2, mesh.shape["sec"]), ("x", "z", "core", "sec"))
    return jax.shard_map(
        on_device,
        mesh=torus,
        in_specs=(
            P("sec", OPS),
            P("sec"),
            P(OPS, "sec", None),
            P(OPS, None, None),
            P(OPS),
            P(OPS),
            P(OPS),
        ),
        out_specs=(P("sec", OPS), P(OPS, "sec", None), P()),
        check_vma=False,
    )
```

```python
import functools

import jax
import jax.numpy as jnp
from jax import lax
from jax.experimental import pallas as pl
from jax.experimental.pallas import tpu as pltpu
from jax.sharding import Mesh
from jax.sharding import PartitionSpec as P

SEC = 512
COLS = 4096
ENTRIES = 4096 * 4096
CHIPS = 16
WIDE = 256
HALF = 256
QUARTER = 128
EIGHTH = 64
CUT = (3,)
MIB = 1 << 20
MESH = pl.DeviceIdType.MESH
OPS = ("x", "z", "core")
F32 = jnp.float32
BF16 = jnp.bfloat16


def turn(place, by):
    return lax.rem(place + (by + 4), 4)


def push(src, dst, send, recv, to):
    return pltpu.make_async_remote_copy(
        src_ref=src, dst_ref=dst, send_sem=send, recv_sem=recv, device_id=to, device_id_type=MESH
    )


def greet(peers):
    barrier = pltpu.get_barrier_semaphore()
    for peer in peers:
        pl.semaphore_signal(barrier, inc=1, device_id=peer, device_id_type=MESH)
    pl.semaphore_wait(barrier, len(peers))


def all_blocks(buf, x, z, send, recv, late=None, cut=(), apart=False):
    names = (("x", "z"), ("z", "x"))
    places = ((x, z), (z, x))
    every = slice(None)

    def block(h, pa, pb):
        return pa * 4 + pb if h == 0 else pb * 4 + pa

    def copy(h, j, pa, pb, part, axis, by, columns=every):
        rows = pl.ds(h * HALF, HALF) if part is None else pl.ds(h * HALF + part * QUARTER, QUARTER)
        ref = buf.at[block(h, pa, pb), rows, columns]
        to = {names[h][axis]: turn(places[h][axis], by)}
        return push(ref, ref, send.at[h, j], recv.at[h, j], to)

    def order(h):
        p = places[h][0]
        return (p, turn(p, -1), turn(p, 1), turn(p, 2))

    sent = []

    def go(*what):
        one = copy(*what)
        one.start()
        sent.append(one)

    def arrived(h, j, pa, pb, part, columns=every):
        copy(h, j, pa, pb, part, 0, 1, columns).wait_recv()

    def across(h, i):
        pa, q = order(h)[i], places[h][1]
        for d in (0, 1):
            for n in (0, 1) if i in cut else (0,):
                part = (d + n) % 2 if i in cut else None
                go(h, 8 + 4 * i + 2 * d + n, pa, q, part, 1, 1 - 2 * d)

    def across_arrived(h, i, d, n):
        part = (d + n) % 2 if i in cut else None
        arrived(h, 8 + 4 * i + 2 * d + n, order(h)[i], turn(places[h][1], 2 * d - 1), part)

    def onward(h, i):
        pa, q = order(h)[i], places[h][1]
        for d in (0, 1):
            across_arrived(h, i, d, 0)
            go(h, 24 + 2 * i + d, pa, turn(q, 2 * d - 1), d, 1, 1 - 2 * d)

    def rest(h, i):
        if i in cut:
            across_arrived(h, i, 0, 1)
            across_arrived(h, i, 1, 1)

    def first(h, columns, j):
        p, q = places[h]
        go(h, j, p, q, None, 0, 1, columns)
        go(h, j + 1, p, q, None, 0, -1, columns)

    if late is None:
        for h in (0, 1):
            first(h, every, 0)
            if apart:
                across(h, 0)
                yield
    else:
        for h in (0, 1):
            first(h, late[0], 0)
        late[2]()
        for h in (0, 1):
            first(h, late[1], 2)
    if not apart:
        for h in (0, 1):
            across(h, 0)
        yield
    for h in (0, 1):
        p, q = places[h]
        for d in (0, 1):
            side = turn(p, 2 * d - 1)
            if late is None:
                arrived(h, d, side, q, None)
            else:
                arrived(h, d, side, q, None, late[0])
                arrived(h, 2 + d, side, q, None, late[1])
            go(h, 4 + d, side, q, d, 0, 1 - 2 * d)
    for h in (0, 1):
        across(h, 1)
        across(h, 2)
    yield
    for h in (0, 1):
        onward(h, 0)
    for h in (0, 1):
        rest(h, 0)
    yield 1
    for h in (0, 1):
        p, q = places[h]
        arrived(h, 4, turn(p, 2), q, 0)
        arrived(h, 5, turn(p, 2), q, 1)
        across(h, 3)
    yield
    for h in (0, 1):
        onward(h, 1)
    yield
    for h in (0, 1):
        onward(h, 2)
    for h in (0, 1):
        rest(h, 1)
        rest(h, 2)
    yield 2

    def last(i):
        for h in (0, 1):
            pa, far = order(h)[i], turn(places[h][1], 2)
            arrived(h, 24 + 2 * i, pa, far, 0)
            arrived(h, 25 + 2 * i, pa, far, 1)

    last(0)
    yield 3
    for h in (0, 1):
        onward(h, 3)
    for h in (0, 1):
        rest(h, 3)
    last(1)
    last(2)
    yield 4
    last(3)
    yield 5
    for one in sent:
        one.wait_send()


def ring_peers(x, z):
    return [{"x": turn(x, 1)}, {"x": turn(x, -1)}, {"z": turn(z, 1)}, {"z": turn(z, -1)}]


def dot(a, b):
    return jnp.dot(a, b, preferred_element_type=F32)


def dot_t(a, b):
    return lax.dot_general(a, b, (((1,), (1,)), ((), ())), preferred_element_type=F32)


def rough(a, b):
    return dot(a.astype(BF16), b.astype(BF16))


class Reduction:
    def __init__(self, bufs, sems, x, z):
        self.part, self.near, self.whole, self.near2, self.whole2, self.total = bufs
        self.send, self.recv, self.mod_send, self.mod_recv, self.send2, self.recv2 = sems
        self.places = ((z, x), (x, z))
        self.sent = []

    def at(self, h, pa, pb):
        return (pb, pa) if h == 0 else (pa, pb)

    def rows(self, w, h, half):
        return pl.ds(w * HALF + h * QUARTER + half * EIGHTH, EIGHTH)

    def both_rows(self, w, h):
        return pl.ds(w * HALF + h * QUARTER, QUARTER)

    def line(self, w, h, pa, half):
        rows = self.rows(w, h, half)
        return self.part.at[:, pa, rows, :] if h == 0 else self.part.at[pa, :, rows, :]

    def order(self, h):
        q = self.places[h][1]
        return (turn(q, 2), turn(q, 1), turn(q, -1), q)

    def peer(self, h, axis, d):
        return {("zx", "xz")[h][axis]: turn(self.places[h][axis], 1 - 2 * d)}

    def go(self, one):
        one.start()
        self.sent.append(one)

    def near_copy(self, w, h, d):
        src = self.line(w, h, turn(self.places[h][0], 2), d)
        return push(src, self.near.at[w, h, d], self.send.at[w, h, d], self.recv.at[w, h, d], self.peer(h, 0, d))

    def plain_copy(self, w, h, d):
        src = self.line(w, h, turn(self.places[h][0], 1 - 2 * d), 1 - d)
        dst = self.whole.at[w, h, d, :, pl.ds((1 - d) * EIGHTH, EIGHTH), :]
        return push(src, dst, self.send.at[w, h, 2 + d], self.recv.at[w, h, 2 + d], self.peer(h, 0, d))

    def added_copy(self, w, h, d, i):
        to = self.order(h)[i]
        src = self.part.at[*self.at(h, turn(self.places[h][0], 1 - 2 * d), to), self.rows(w, h, d), :]
        dst = self.whole.at[w, h, d, to, pl.ds(d * EIGHTH, EIGHTH), :]
        return push(src, dst, self.mod_send.at[w, h, d, i], self.mod_recv.at[w, h, d, i], self.peer(h, 0, d))

    def near2_copy(self, w, h, d):
        p, q = self.places[h]
        src = self.part.at[*self.at(h, p, turn(q, 2)), self.rows(w, h, d), :]
        return push(src, self.near2.at[w, h, d], self.send2.at[w, h, d], self.recv2.at[w, h, d], self.peer(h, 1, d))

    def whole2_copy(self, w, h, d, half):
        p, q = self.places[h]
        j = 2 + 2 * d + half
        src = self.part.at[*self.at(h, p, turn(q, 1 - 2 * d)), self.rows(w, h, half), :]
        dst = self.whole2.at[w, h, d, pl.ds(half * EIGHTH, EIGHTH), :]
        return push(src, dst, self.send2.at[w, h, j], self.recv2.at[w, h, j], self.peer(h, 1, d))

    def begin(self, w):
        for h in (0, 1):
            for d in (0, 1):
                self.go(self.near_copy(w, h, d))
        for h in (0, 1):
            for d in (0, 1):
                self.go(self.plain_copy(w, h, d))

    def add(self, w):
        for h in (0, 1):
            p = self.places[h][0]
            for d in (0, 1):
                self.near_copy(w, h, d).wait_recv()
                for i in range(4):
                    to = self.order(h)[i]
                    spot = (*self.at(h, turn(p, 1 - 2 * d), to), self.rows(w, h, d), slice(None))
                    both = self.part[spot].astype(F32) + self.near[w, h, d, to].astype(F32)
                    self.part[spot] = both.astype(BF16)
                    self.go(self.added_copy(w, h, d, i))

    def second(self, w):
        for h in (0, 1):
            for d in (0, 1):
                self.plain_copy(w, h, d).wait_recv()
        for i in range(4):
            for h in (0, 1):
                p = self.places[h][0]
                for d in (0, 1):
                    self.added_copy(w, h, d, i).wait_recv()
                to = self.order(h)[i]
                spot = (*self.at(h, p, to), self.both_rows(w, h), slice(None))
                done = self.part[spot].astype(F32) + self.whole[w, h, 0, to].astype(F32) + self.whole[w, h, 1, to].astype(F32)
                if i == 3:
                    self.total[self.both_rows(w, h), :] = done
                else:
                    self.part[spot] = done.astype(BF16)
                if i == 0:
                    self.go(self.near2_copy(w, h, 0))
                    self.go(self.near2_copy(w, h, 1))
                if i == 1:
                    self.go(self.whole2_copy(w, h, 0, 1))
                if i == 2:
                    self.go(self.whole2_copy(w, h, 1, 0))

    def add2(self, w):
        for h in (0, 1):
            p, q = self.places[h]
            for d in (0, 1):
                self.near2_copy(w, h, d).wait_recv()
                spot = (*self.at(h, p, turn(q, 1 - 2 * d)), self.rows(w, h, d), slice(None))
                both = self.part[spot].astype(F32) + self.near2[w, h, d].astype(F32)
                self.part[spot] = both.astype(BF16)
                self.go(self.whole2_copy(w, h, d, d))

    def finish(self, w):
        for h in (0, 1):
            for d in (0, 1):
                for half in (0, 1):
                    self.whole2_copy(w, h, d, half).wait_recv()
            here = self.both_rows(w, h)
            self.total[here, :] += self.whole2[w, h, 0].astype(F32) + self.whole2[w, h, 1].astype(F32)

    def close(self):
        for one in self.sent:
            one.wait_send()


def frobenius(a):
    return jnp.sqrt(jnp.sum(a * a, axis=(0, 1), keepdims=True) + 1e-06)


def group_block(group, t, x, z):
    if group == 1:
        dx = (t == 1).astype(jnp.int32) - (t == 2).astype(jnp.int32)
        dz = (t == 3).astype(jnp.int32) - (t == 4).astype(jnp.int32)
    elif group == 2:
        dx, dz = 1 - 2 * lax.rem(t, 2), 1 - 2 * lax.div(t, 2)
    elif group == 3:
        dx, dz = 2 - 2 * t, 2 * t
    elif group == 4:
        dx, dz = jnp.where(t < 2, 1 - 2 * t, 2), jnp.where(t < 2, 2, 5 - 2 * t)
    else:
        dx = dz = 2
    return turn(x, dx) * 4 + turn(z, dz)


GROUP_SIZE = {1: 5, 2: 4, 3: 2, 4: 4, 5: 1}


def site_kernel(
    wave, row_ops, col_ops, count, source, target, energy_row,
    stepped_o, root_o, level_o, exact_o, energy_o,
    wide, row_v, col_v, table, table_in, table_s, order_s, source_s, prefix,
    part, near, whole, near2, whole2, total, stepped, gram, my, mm, mu, mz, roots, level_two, exact, scalars, energy_col,
    wv_send, wv_recv, swap_send, swap_recv,
    rs_send, rs_recv, mod_send, mod_recv, rs2_send, rs2_recv, ag_send, ag_recv, en_send, en_recv, st_send, st_recv, st_own,
    end_send, end_recv, own_sem,
):
    x, z, c, y = lax.axis_index("x"), lax.axis_index("z"), lax.axis_index("core"), lax.axis_index("sec")
    b = x * 4 + z
    sib = {"core": 1 - c}
    mine = pl.ds(pl.multiple_of(c * SEC, SEC), SEC)
    other = pl.ds(pl.multiple_of((1 - c) * SEC, SEC), SEC)
    columns = pl.ds(pl.multiple_of(c * 128, 128), 128)
    other_columns = pl.ds(pl.multiple_of((1 - c) * 128, 128), 128)
    own_slots, sib_slots = pl.ds(0, 4), pl.ds(4, 4)
    own_wave = pltpu.make_async_copy(wave.at[mine, :], wide.at[b, :, columns], own_sem.at[0])
    own_wave.start()
    lane = lax.broadcasted_iota(jnp.int32, (8, 128), 1)
    numbers = jnp.where(lane == 0, count[0], 0)
    for k in range(4):
        numbers = jnp.where(lane == 1 + k, source[k], numbers)
        numbers = jnp.where(lane == 5 + k, target[k], numbers)
    table[...] = numbers
    greet(
        ring_peers(x, z)
        + [sib, {"x": turn(x, 2)}, {"z": turn(z, 2)}, {"sec": turn(y, 1)}, {"sec": turn(y, 2)}, {"sec": turn(y, -1)}]
    )
    swaps = [
        push(wave.at[other, :], wide.at[b, :, columns], swap_send.at[0], swap_recv.at[0], sib),
        push(table, table_in, swap_send.at[1], swap_recv.at[1], sib),
        push(row_ops.at[:, other, :], row_v.at[sib_slots], swap_send.at[2], swap_recv.at[2], sib),
        push(col_ops, col_v.at[sib_slots], swap_send.at[3], swap_recv.at[3], sib),
    ]
    swaps[0].start()
    own_wave.wait()

    def swapped():
        push(wave.at[other, :], wide.at[b, :, other_columns], swap_send.at[0], swap_recv.at[0], sib).wait_recv()

    steps = all_blocks(wide, x, z, wv_send, wv_recv, (columns, other_columns, swapped), CUT)
    next(steps)
    for swap in swaps[1:]:
        swap.start()
    own_rows = pltpu.make_async_copy(row_ops.at[:, mine, :], row_v.at[own_slots], own_sem.at[1])
    own_cols = pltpu.make_async_copy(col_ops, col_v.at[own_slots], own_sem.at[5])
    own_rows.start()
    own_cols.start()
    same = lax.broadcasted_iota(jnp.int32, (128, 128), 0) == lax.broadcasted_iota(jnp.int32, (128, 128), 1)
    for i in range(4):
        spread = jnp.where(same, jnp.broadcast_to(energy_row[pl.ds(c * 4 + i, 1), :], (128, 128)), 0.0)
        energy_col[pl.ds(i * 128, 128), :] = jnp.sum(spread, axis=1, keepdims=True)
    swaps[1].wait_recv()
    to_scalars = pltpu.make_async_copy(table_in, table_s, own_sem.at[6])
    to_scalars.start()
    to_scalars.wait()

    def flag(condition):
        return condition.astype(jnp.int32)

    keys, sources = [], []
    for side in (0, 1):
        live = table_s[0, 0] if side else count[0]
        for k in range(4):
            alive = flag(k < live)
            aim = table_s[0, 5 + k] if side else target[k]
            keys.append(aim * alive + 8 * (1 - alive))
            sources.append(table_s[0, 1 + k] if side else source[k])
    ranks = []
    for i in range(8):
        ahead = [flag(keys[j] <= keys[i]) if j < i else flag(keys[j] < keys[i]) for j in range(8) if j != i]
        ranks.append(sum(ahead))
    for j in range(8):
        order_s[j] = sum(i * flag(ranks[i] == j) for i in range(8))
        source_s[j] = sum(sources[i] * flag(ranks[i] == j) for i in range(8))
    starts = [sum(flag(key < t) for key in keys) for t in range(9)]

    for ready in steps:
        del ready
    swaps[0].wait_send()
    swaps[1].wait_send()
    own_rows.wait()
    own_cols.wait()
    swaps[2].wait()
    swaps[3].wait()

    reduction = Reduction(
        (part, near, whole, near2, whole2, total), (rs_send, rs_recv, mod_send, mod_recv, rs2_send, rs2_recv), x, z
    )
    prefix[0] = jnp.zeros((HALF, SEC), F32)
    for h in (0, 1):
        here = pl.ds(h * HALF, HALF)

        def term(j, carry, here=here):
            slot = order_s[j]
            src = source_s[j] * 2
            rows = row_v[slot, here, :]
            first = dot(rows, wide[src]).astype(BF16)
            second = dot(rows, wide[src + 1]).astype(BF16)
            prefix[j + 1] = prefix[j] + (dot(first, col_v[slot, :WIDE, :]) + dot(second, col_v[slot, WIDE:, :]))
            return carry

        lax.fori_loop(0, 8, term, 0)
        for t in range(8):
            added = (prefix[starts[t + 1]] - prefix[starts[t]]).astype(BF16)
            part[t // 2, 2 * (t % 2), here, :] = added[:, :WIDE]
            part[t // 2, 2 * (t % 2) + 1, here, :] = added[:, WIDE:]
        reduction.begin(h)

    amplitude = wide[b].astype(F32)

    def overlap(i, carry):
        product = part[lax.div(i, 4), lax.rem(i, 4)].astype(F32) * wide[i].astype(F32)
        return carry + jnp.sum(product.reshape(SEC // 8, 8, WIDE), axis=0)

    level = energy_col[...]
    shares = lax.fori_loop(0, CHIPS, overlap, jnp.sum((level * amplitude * amplitude).reshape(SEC // 8, 8, WIDE), axis=0))
    share = jnp.sum(shares, axis=(0, 1), keepdims=True)
    stages = (("sec", y, 4), ("x", x, 4), ("z", z, 4), ("core", c, 2))

    def energy_copies(s):
        name, place, size = stages[s]
        for hop in range(1, size):
            to = {name: lax.rem(place + hop, size)}
            src = lax.rem(place + (size - hop), size)
            yield (
                push(scalars.at[s, place], scalars.at[s, place], en_send.at[s, hop], en_recv.at[s, hop], to),
                push(scalars.at[s, src], scalars.at[s, src], en_send.at[s, hop], en_recv.at[s, hop], to),
            )

    works = (
        lambda: (reduction.add(0), reduction.add(1)),
        lambda: reduction.second(0),
        lambda: reduction.second(1),
        lambda: (reduction.add2(0), reduction.add2(1)),
    )
    for s in range(4):
        place, size = stages[s][1:]
        scalars[s, place] = jnp.broadcast_to(share, (8, 128))
        for out, unused in energy_copies(s):
            out.start()
        works[s]()
        for out, arriving in energy_copies(s):
            arriving.wait_recv()
            out.wait_send()
        share = scalars[s, 0] + scalars[s, 1]
        if size == 4:
            share = (share + scalars[s, 2]) + scalars[s, 3]
        share = share[0:1, 0:1]
    energy = share * (1.0 / ENTRIES)
    energy_o[...] = jnp.broadcast_to(energy, (8, 128))

    steps = all_blocks(stepped, x, z, ag_send, ag_recv, None, CUT, True)
    for h in (0, 1):
        reduction.finish(h)
        here = pl.ds(h * HALF, HALF)
        mild = wide[b, here, :].astype(F32)
        own = mild + 0.5 * (energy * mild - (energy_col[here, :] * mild + total[here, :]))
        stepped[b, here, :] = own.astype(BF16)
        next(steps)
        exact[0, here, :] = own[:, :128]
        exact[1, here, :] = own[:, 128:]
    reduction.close()
    exact_send = push(exact.at[1 - c], exact_o.at[mine, :], end_send.at[0], end_recv.at[0], sib)
    exact_own = pltpu.make_async_copy(exact.at[c], exact_o.at[mine, :], own_sem.at[2])
    exact_send.start()
    exact_own.start()

    def out_block(i):
        return (
            push(stepped.at[i], stepped_o.at[c, i], st_send.at[i], st_recv.at[i], sib),
            pltpu.make_async_copy(stepped.at[i], stepped_o.at[c, i], st_own.at[i]),
        )

    gram[...] = jnp.zeros((SEC, SEC), F32)

    def add_group(group):
        def one_block(t, carry):
            i = group_block(group, t, x, z)
            value = stepped[i]
            for one in out_block(i):
                one.start()
            gram[...] += dot_t(value, value)
            return carry

        lax.fori_loop(0, GROUP_SIZE[group], one_block, 0)

    for ready in steps:
        if ready:
            add_group(ready)

    def root(y_ref, d_ref, again):
        my[...] = 1.5 * y_ref[...] - 0.5 * rough(y_ref[...], y_ref[...])
        mu[...] = 1.5 * my[...] - 0.5 * rough(y_ref[...], my[...])
        d_ref[...] = 0.25 * rough(mu[...], y_ref[...]) - 0.75 * (y_ref[...] + mu[...])
        if again:
            y_ref[...] = 1.5 * my[...] - 0.5 * rough(my[...], mu[...])

    gram_one = gram[...] * (1.0 / COLS)
    scale_one = frobenius(gram_one)
    gram[...] = gram_one / scale_one
    root(gram, mz, True)
    gram_two = 2.25 * gram[...] + rough(mz[...], gram[...])
    scale_two = frobenius(gram_two)
    gram[...] = gram_two / scale_two
    root(gram, mm, False)
    size = jnp.sqrt(scale_one) * jnp.sqrt(scale_two)
    roots[...] = ((2.25 * (mz[...] + mm[...]) + rough(mm[...], mz[...])) / size).astype(BF16)
    level_two[...] = jnp.broadcast_to(2.25 * 2.25 / size, (8, 128))
    root_send = push(roots, root_o.at[c], end_send.at[1], end_recv.at[1], sib)
    root_own = pltpu.make_async_copy(roots, root_o.at[c], own_sem.at[3])
    level_send = push(level_two, level_o.at[c], end_send.at[2], end_recv.at[2], sib)
    level_own = pltpu.make_async_copy(level_two, level_o.at[c], own_sem.at[4])
    level_send.start()
    level_own.start()
    root_send.start()
    root_own.start()

    def block_done(i, carry):
        going, staying = out_block(i)
        going.wait_send()
        staying.wait()
        push(stepped.at[i], stepped_o.at[1 - c, i], st_send.at[i], st_recv.at[i], sib).wait_recv()
        return carry

    lax.fori_loop(0, CHIPS, block_done, 0)
    exact_send.wait_send()
    exact_own.wait()
    push(exact.at[1 - c], exact_o.at[other, :], end_send.at[0], end_recv.at[0], sib).wait_recv()
    root_send.wait_send()
    root_own.wait()
    push(roots, root_o.at[1 - c], end_send.at[1], end_recv.at[1], sib).wait_recv()
    level_send.wait_send()
    level_own.wait()
    push(level_two, level_o.at[1 - c], end_send.at[2], end_recv.at[2], sib).wait_recv()


def site(wave, row_ops, col_ops, count, source, target, energy_row):
    hbm = pl.BlockSpec(memory_space=pltpu.HBM)
    smem = pl.BlockSpec(memory_space=pltpu.SMEM)
    vmem = pl.BlockSpec(memory_space=pltpu.VMEM)
    square = pltpu.VMEM((SEC, SEC), F32)
    blocks = pltpu.VMEM((CHIPS, SEC, WIDE), BF16)
    dma = pltpu.SemaphoreType.DMA
    return pl.pallas_call(
        site_kernel,
        out_shape=(
            jax.ShapeDtypeStruct((2, CHIPS, SEC, WIDE), BF16),
            jax.ShapeDtypeStruct((2, SEC, SEC), BF16),
            jax.ShapeDtypeStruct((2, 8, 128), F32),
            jax.ShapeDtypeStruct((2 * SEC, 128), F32),
            jax.ShapeDtypeStruct((8, 128), F32),
        ),
        in_specs=[hbm] * 3 + [smem] * 3 + [vmem],
        out_specs=(hbm, hbm, hbm, hbm, vmem),
        scratch_shapes=[
            blocks,
            pltpu.VMEM((8, SEC, SEC), BF16),
            pltpu.VMEM((8, SEC, SEC), BF16),
            pltpu.VMEM((8, 128), jnp.int32),
            pltpu.VMEM((8, 128), jnp.int32),
            pltpu.SMEM((8, 128), jnp.int32),
            pltpu.SMEM((8,), jnp.int32),
            pltpu.SMEM((8,), jnp.int32),
            pltpu.VMEM((9, HALF, SEC), F32),
            pltpu.VMEM((4, 4, SEC, WIDE), BF16),
            pltpu.VMEM((2, 2, 2, 4, EIGHTH, WIDE), BF16),
            pltpu.VMEM((2, 2, 2, 4, QUARTER, WIDE), BF16),
            pltpu.VMEM((2, 2, 2, EIGHTH, WIDE), BF16),
            pltpu.VMEM((2, 2, 2, QUARTER, WIDE), BF16),
            pltpu.VMEM((SEC, WIDE), F32),
            blocks,
            square,
            square,
            square,
            square,
            square,
            pltpu.VMEM((SEC, SEC), BF16),
            pltpu.VMEM((8, 128), F32),
            pltpu.VMEM((2, SEC, 128), F32),
            pltpu.VMEM((4, 4, 8, 128), F32),
            pltpu.VMEM((SEC, 1), F32),
            dma((2, 32)),
            dma((2, 32)),
            dma((4,)),
            dma((4,)),
            dma((2, 2, 4)),
            dma((2, 2, 4)),
            dma((2, 2, 2, 4)),
            dma((2, 2, 2, 4)),
            dma((2, 2, 6)),
            dma((2, 2, 6)),
            dma((2, 32)),
            dma((2, 32)),
            dma((4, 4)),
            dma((4, 4)),
            dma((CHIPS,)),
            dma((CHIPS,)),
            dma((CHIPS,)),
            dma((3,)),
            dma((3,)),
            dma((7,)),
        ],
        compiler_params=pltpu.CompilerParams(
            collective_id=0, has_side_effects=True, vmem_limit_bytes=60 * MIB
        ),
        name="site",
    )(wave, row_ops, col_ops, count, source, target, energy_row)


def renorm_kernel(
    count, source, target, stepped, cols, root, level, exact, energy,
    out, wave_o, energy_o,
    block_v, cols_v, root_v, out_v, zero_v, exact_v, wave_v, level_v, block_sem, cols_sem, root_sem, out_sem, exact_sem, wave_sem, level_sem,
):
    energy_o[0] = energy[0, 0]

    def needs(k, s):
        pair = (source[k], target[k])
        return [
            pltpu.make_async_copy(
                stepped.at[s, pl.ds(2 * pair[e], 2)], block_v.at[k, s, e], block_sem.at[k, s, e]
            )
            for e in (0, 1)
        ]

    def column_op(k):
        return pltpu.make_async_copy(cols.at[k], cols_v.at[k], cols_sem.at[k])

    def result(k, s):
        return pltpu.make_async_copy(out_v.at[k, s], out.at[k, pl.ds(s * SEC, SEC), :], out_sem.at[k, s])

    def nothing(k, s):
        return pltpu.make_async_copy(zero_v, out.at[k, pl.ds(s * SEC, SEC), :], out_sem.at[k, s])

    roots = [pltpu.make_async_copy(root.at[s], root_v.at[s], root_sem.at[s]) for s in (0, 1)]
    load_level = pltpu.make_async_copy(level, level_v, level_sem)
    load_level.start()
    roots[0].start()
    for one in needs(0, 0):
        one.start()
    column_op(0).start()
    roots[1].start()
    for one in needs(0, 1):
        one.start()
    zero_v[...] = jnp.zeros_like(zero_v)
    load_exact = pltpu.make_async_copy(exact, exact_v, exact_sem)
    load_level.wait()
    roots[0].wait()

    def one_term(k, carry):
        column_op(k).wait()
        for s in (0, 1):
            scale = level_v[s, 0:1, 0:1]
            for one in needs(k, s):
                one.wait()
            if s == 0:

                @pl.when(k + 1 < count[0])
                def ahead():
                    column_op(k + 1).start()
                    for t in (0, 1):
                        for one in needs(k + 1, t):
                            one.start()

                @pl.when(k == 0)
                def others():
                    load_exact.start()
                    for empty in range(1, 4):

                        @pl.when(empty >= count[0])
                        def clear(empty=empty):
                            nothing(empty, 0).start()
                            nothing(empty, 1).start()
            else:

                @pl.when(k == 0)
                def second_root():
                    roots[1].wait()
            halves = []
            for e in (0, 1):
                block = jnp.concatenate([block_v[k, s, e, 0], block_v[k, s, e, 1]], axis=1)
                halves.append((scale * block.astype(F32) + dot(root_v[s], block)).astype(BF16))
            product = dot(halves[0], cols_v[k]).astype(BF16)
            out_v[k, s] = dot_t(product, halves[1]) * SEC ** (-0.5)
            result(k, s).start()
        return carry

    lax.fori_loop(0, count[0], one_term, 0)
    load_exact.wait()
    waves = []
    for s in (0, 1):
        rows = pl.ds(s * SEC, SEC)
        own = exact_v[rows, :]
        wave_v[rows, :] = level_v[s, 0:1, 0:1] * own + dot(root_v[s], own.astype(BF16))
        waves.append(pltpu.make_async_copy(wave_v.at[rows, :], wave_o.at[rows, :], wave_sem.at[s]))
        waves[s].start()
    for one in waves:
        one.wait()
    for k in range(4):
        for s in (0, 1):
            result(k, s).wait()


def renorm(count, source, target, stepped, cols, root, level, exact, energy):
    hbm = pl.BlockSpec(memory_space=pltpu.HBM)
    smem = pl.BlockSpec(memory_space=pltpu.SMEM)
    return pl.pallas_call(
        renorm_kernel,
        out_shape=(
            jax.ShapeDtypeStruct((4, 2 * SEC, SEC), F32),
            jax.ShapeDtypeStruct((2 * SEC, 128), F32),
            jax.ShapeDtypeStruct((1,), F32),
        ),
        in_specs=[smem] * 3 + [hbm] * 5 + [smem],
        out_specs=(hbm, hbm, smem),
        scratch_shapes=[
            pltpu.VMEM((4, 2, 2, 2, SEC, WIDE), BF16),
            pltpu.VMEM((4, SEC, SEC), BF16),
            pltpu.VMEM((2, SEC, SEC), BF16),
            pltpu.VMEM((4, 2, SEC, SEC), F32),
            pltpu.VMEM((SEC, SEC), F32),
            pltpu.VMEM((2 * SEC, 128), F32),
            pltpu.VMEM((2 * SEC, 128), F32),
            pltpu.VMEM((2, 8, 128), F32),
            pltpu.SemaphoreType.DMA((4, 2, 2)),
            pltpu.SemaphoreType.DMA((4,)),
            pltpu.SemaphoreType.DMA((2,)),
            pltpu.SemaphoreType.DMA((4, 2)),
            pltpu.SemaphoreType.DMA(()),
            pltpu.SemaphoreType.DMA((2,)),
            pltpu.SemaphoreType.DMA(()),
        ],
        compiler_params=pltpu.CompilerParams(vmem_limit_bytes=60 * MIB),
        name="renorm",
    )(count, source, target, stepped, cols, root, level, exact, energy)


def on_device(wave_in, row_energy, row_operators, column_operators, term_count, source, target):
    stepped, root, level, exact, energy = site(
        wave_in, row_operators, column_operators, term_count, source, target, row_energy.reshape(8, 128)
    )
    renormalized, wave_next, energy = renorm(
        term_count, source, target, stepped, column_operators, root, level, exact, energy
    )
    return (wave_next, renormalized, energy.reshape(()))


def solution(mesh):
    torus = Mesh(mesh.devices.reshape(4, 4, 2, mesh.shape["sec"]), ("x", "z", "core", "sec"))
    return jax.shard_map(
        on_device,
        mesh=torus,
        in_specs=(
            P("sec", OPS),
            P("sec"),
            P(OPS, "sec", None),
            P(OPS, None, None),
            P(OPS),
            P(OPS),
            P(OPS),
        ),
        out_specs=(P("sec", OPS), P(OPS, "sec", None), P()),
        check_vma=False,
    )
```

```python
import functools

import jax
import jax.numpy as jnp
from jax import lax
from jax.experimental import pallas as pl
from jax.experimental.pallas import tpu as pltpu
from jax.sharding import Mesh
from jax.sharding import PartitionSpec as P

SEC = 512
COLS = 4096
ENTRIES = 4096 * 4096
CHIPS = 16
WIDE = 256
HALF = 256
QUARTER = 128
EIGHTH = 64
CUT = (3,)
MIB = 1 << 20
MESH = pl.DeviceIdType.MESH
OPS = ("x", "z", "core")
F32 = jnp.float32
BF16 = jnp.bfloat16


def turn(place, by):
    return lax.rem(place + (by + 4), 4)


def push(src, dst, send, recv, to):
    return pltpu.make_async_remote_copy(
        src_ref=src, dst_ref=dst, send_sem=send, recv_sem=recv, device_id=to, device_id_type=MESH
    )


def greet(peers):
    barrier = pltpu.get_barrier_semaphore()
    for peer in peers:
        pl.semaphore_signal(barrier, inc=1, device_id=peer, device_id_type=MESH)
    pl.semaphore_wait(barrier, len(peers))


def all_blocks(buf, x, z, send, recv, late=None, cut=(), apart=False):
    names = (("x", "z"), ("z", "x"))
    places = ((x, z), (z, x))
    every = slice(None)

    def block(h, pa, pb):
        return pa * 4 + pb if h == 0 else pb * 4 + pa

    def copy(h, j, pa, pb, part, axis, by, columns=every):
        rows = pl.ds(h * HALF, HALF) if part is None else pl.ds(h * HALF + part * QUARTER, QUARTER)
        ref = buf.at[block(h, pa, pb), rows, columns]
        to = {names[h][axis]: turn(places[h][axis], by)}
        return push(ref, ref, send.at[h, j], recv.at[h, j], to)

    def order(h):
        p = places[h][0]
        return (p, turn(p, -1), turn(p, 1), turn(p, 2))

    sent = []

    def go(*what):
        one = copy(*what)
        one.start()
        sent.append(one)

    def arrived(h, j, pa, pb, part, columns=every):
        copy(h, j, pa, pb, part, 0, 1, columns).wait_recv()

    def across(h, i):
        pa, q = order(h)[i], places[h][1]
        for d in (0, 1):
            for n in (0, 1) if i in cut else (0,):
                part = (d + n) % 2 if i in cut else None
                go(h, 8 + 4 * i + 2 * d + n, pa, q, part, 1, 1 - 2 * d)

    def across_arrived(h, i, d, n):
        part = (d + n) % 2 if i in cut else None
        arrived(h, 8 + 4 * i + 2 * d + n, order(h)[i], turn(places[h][1], 2 * d - 1), part)

    def onward(h, i):
        pa, q = order(h)[i], places[h][1]
        for d in (0, 1):
            across_arrived(h, i, d, 0)
            go(h, 24 + 2 * i + d, pa, turn(q, 2 * d - 1), d, 1, 1 - 2 * d)

    def rest(h, i):
        if i in cut:
            across_arrived(h, i, 0, 1)
            across_arrived(h, i, 1, 1)

    def first(h, columns, j):
        p, q = places[h]
        go(h, j, p, q, None, 0, 1, columns)
        go(h, j + 1, p, q, None, 0, -1, columns)

    if late is None:
        for h in (0, 1):
            first(h, every, 0)
            if apart:
                across(h, 0)
                yield
    else:
        for h in (0, 1):
            first(h, late[0], 0)
        late[2]()
        for h in (0, 1):
            first(h, late[1], 2)
    if not apart:
        for h in (0, 1):
            across(h, 0)
        yield
    for h in (0, 1):
        p, q = places[h]
        for d in (0, 1):
            side = turn(p, 2 * d - 1)
            if late is None:
                arrived(h, d, side, q, None)
            else:
                arrived(h, d, side, q, None, late[0])
                arrived(h, 2 + d, side, q, None, late[1])
            go(h, 4 + d, side, q, d, 0, 1 - 2 * d)
    for h in (0, 1):
        across(h, 1)
        across(h, 2)
    yield
    def last(i):
        for h in (0, 1):
            pa, far = order(h)[i], turn(places[h][1], 2)
            arrived(h, 24 + 2 * i, pa, far, 0)
            arrived(h, 25 + 2 * i, pa, far, 1)

    for h in (0, 1):
        onward(h, 0)
    for h in (0, 1):
        p, q = places[h]
        arrived(h, 4, turn(p, 2), q, 0)
        arrived(h, 5, turn(p, 2), q, 1)
        across(h, 3)
    for h in (0, 1):
        rest(h, 0)
    for i in (1, 2):
        for h in (0, 1):
            onward(h, i)
    yield 1
    for h in (0, 1):
        onward(h, 3)
    for i in (1, 2, 3):
        for h in (0, 1):
            rest(h, i)
    yield 2
    last(0)
    yield 3
    last(1)
    last(2)
    yield 4
    last(3)
    yield 5
    for one in sent:
        one.wait_send()


def ring_peers(x, z):
    return [{"x": turn(x, 1)}, {"x": turn(x, -1)}, {"z": turn(z, 1)}, {"z": turn(z, -1)}]


def dot(a, b):
    return jnp.dot(a, b, preferred_element_type=F32)


def dot_t(a, b):
    return lax.dot_general(a, b, (((1,), (1,)), ((), ())), preferred_element_type=F32)


def rough(a, b):
    return dot(a.astype(BF16), b.astype(BF16))


class Reduction:
    def __init__(self, bufs, sems, x, z):
        self.part, self.near, self.whole, self.near2, self.whole2, self.total = bufs
        self.send, self.recv, self.mod_send, self.mod_recv, self.send2, self.recv2 = sems
        self.places = ((z, x), (x, z))
        self.sent = []

    def at(self, h, pa, pb):
        return (pb, pa) if h == 0 else (pa, pb)

    def rows(self, w, h, half):
        return pl.ds(w * HALF + h * QUARTER + half * EIGHTH, EIGHTH)

    def both_rows(self, w, h):
        return pl.ds(w * HALF + h * QUARTER, QUARTER)

    def line(self, w, h, pa, half):
        rows = self.rows(w, h, half)
        return self.part.at[:, pa, rows, :] if h == 0 else self.part.at[pa, :, rows, :]

    def order(self, h):
        q = self.places[h][1]
        return (turn(q, 2), turn(q, 1), turn(q, -1), q)

    def peer(self, h, axis, d):
        return {("zx", "xz")[h][axis]: turn(self.places[h][axis], 1 - 2 * d)}

    def go(self, one):
        one.start()
        self.sent.append(one)

    def near_copy(self, w, h, d):
        src = self.line(w, h, turn(self.places[h][0], 2), d)
        return push(src, self.near.at[w, h, d], self.send.at[w, h, d], self.recv.at[w, h, d], self.peer(h, 0, d))

    def plain_copy(self, w, h, d):
        src = self.line(w, h, turn(self.places[h][0], 1 - 2 * d), 1 - d)
        dst = self.whole.at[w, h, d, :, pl.ds((1 - d) * EIGHTH, EIGHTH), :]
        return push(src, dst, self.send.at[w, h, 2 + d], self.recv.at[w, h, 2 + d], self.peer(h, 0, d))

    def added_copy(self, w, h, d, i):
        to = self.order(h)[i]
        src = self.part.at[*self.at(h, turn(self.places[h][0], 1 - 2 * d), to), self.rows(w, h, d), :]
        dst = self.whole.at[w, h, d, to, pl.ds(d * EIGHTH, EIGHTH), :]
        return push(src, dst, self.mod_send.at[w, h, d, i], self.mod_recv.at[w, h, d, i], self.peer(h, 0, d))

    def near2_copy(self, w, h, d):
        p, q = self.places[h]
        src = self.part.at[*self.at(h, p, turn(q, 2)), self.rows(w, h, d), :]
        return push(src, self.near2.at[w, h, d], self.send2.at[w, h, d], self.recv2.at[w, h, d], self.peer(h, 1, d))

    def whole2_copy(self, w, h, d, half):
        p, q = self.places[h]
        j = 2 + 2 * d + half
        src = self.part.at[*self.at(h, p, turn(q, 1 - 2 * d)), self.rows(w, h, half), :]
        dst = self.whole2.at[w, h, d, pl.ds(half * EIGHTH, EIGHTH), :]
        return push(src, dst, self.send2.at[w, h, j], self.recv2.at[w, h, j], self.peer(h, 1, d))

    def begin(self, w):
        for h in (0, 1):
            for d in (0, 1):
                self.go(self.near_copy(w, h, d))
        for h in (0, 1):
            for d in (0, 1):
                self.go(self.plain_copy(w, h, d))

    def add(self, w):
        for h in (0, 1):
            p = self.places[h][0]
            for d in (0, 1):
                self.near_copy(w, h, d).wait_recv()
                for i in range(4):
                    to = self.order(h)[i]
                    spot = (*self.at(h, turn(p, 1 - 2 * d), to), self.rows(w, h, d), slice(None))
                    both = self.part[spot].astype(F32) + self.near[w, h, d, to].astype(F32)
                    self.part[spot] = both.astype(BF16)
                    self.go(self.added_copy(w, h, d, i))

    def second(self, w):
        for h in (0, 1):
            for d in (0, 1):
                self.plain_copy(w, h, d).wait_recv()
        for i in range(4):
            for h in (0, 1):
                p = self.places[h][0]
                for d in (0, 1):
                    self.added_copy(w, h, d, i).wait_recv()
                to = self.order(h)[i]
                spot = (*self.at(h, p, to), self.both_rows(w, h), slice(None))
                done = self.part[spot].astype(F32) + self.whole[w, h, 0, to].astype(F32) + self.whole[w, h, 1, to].astype(F32)
                if i == 3:
                    self.total[self.both_rows(w, h), :] = done
                else:
                    self.part[spot] = done.astype(BF16)
                if i == 0:
                    self.go(self.near2_copy(w, h, 0))
                    self.go(self.near2_copy(w, h, 1))
                if i == 1:
                    self.go(self.whole2_copy(w, h, 0, 1))
                if i == 2:
                    self.go(self.whole2_copy(w, h, 1, 0))

    def add2(self, w):
        for h in (0, 1):
            p, q = self.places[h]
            for d in (0, 1):
                self.near2_copy(w, h, d).wait_recv()
                spot = (*self.at(h, p, turn(q, 1 - 2 * d)), self.rows(w, h, d), slice(None))
                both = self.part[spot].astype(F32) + self.near2[w, h, d].astype(F32)
                self.part[spot] = both.astype(BF16)
                self.go(self.whole2_copy(w, h, d, d))

    def finish(self, w):
        for h in (0, 1):
            for d in (0, 1):
                for half in (0, 1):
                    self.whole2_copy(w, h, d, half).wait_recv()
            here = self.both_rows(w, h)
            self.total[here, :] += self.whole2[w, h, 0].astype(F32) + self.whole2[w, h, 1].astype(F32)

    def close(self):
        for one in self.sent:
            one.wait_send()


def frobenius(a):
    return jnp.sqrt(jnp.sum(a * a, axis=(0, 1), keepdims=True) + 1e-06)


def group_block(group, t, x, z):
    if group == 1:
        dx = (t == 1).astype(jnp.int32) - (t == 2).astype(jnp.int32)
        dz = (t == 3).astype(jnp.int32) - (t == 4).astype(jnp.int32)
    elif group == 2:
        dx, dz = 1 - 2 * lax.rem(t, 2), 1 - 2 * lax.div(t, 2)
    elif group == 3:
        dx, dz = 2 - 2 * t, 2 * t
    elif group == 4:
        dx, dz = jnp.where(t < 2, 1 - 2 * t, 2), jnp.where(t < 2, 2, 5 - 2 * t)
    else:
        dx = dz = 2
    return turn(x, dx) * 4 + turn(z, dz)


GROUP_SIZE = {1: 5, 2: 4, 3: 2, 4: 4, 5: 1}


def site_kernel(
    wave, row_ops, col_ops, count, source, target, energy_row,
    stepped_o, root_o, level_o, exact_o, energy_o,
    wide, row_v, col_v, table, table_in, table_s, order_s, source_s, prefix,
    part, near, whole, near2, whole2, total, stepped, gram, my, mm, mu, mz, small, roots, level_two, exact, scalars, energy_col,
    wv_send, wv_recv, swap_send, swap_recv,
    rs_send, rs_recv, mod_send, mod_recv, rs2_send, rs2_recv, ag_send, ag_recv, en_send, en_recv, st_send, st_recv, st_own,
    end_send, end_recv, root_send, root_recv, own_sem,
):
    x, z, c, y = lax.axis_index("x"), lax.axis_index("z"), lax.axis_index("core"), lax.axis_index("sec")
    b = x * 4 + z
    sib = {"core": 1 - c}
    mine = pl.ds(pl.multiple_of(c * SEC, SEC), SEC)
    other = pl.ds(pl.multiple_of((1 - c) * SEC, SEC), SEC)
    columns = pl.ds(pl.multiple_of(c * 128, 128), 128)
    other_columns = pl.ds(pl.multiple_of((1 - c) * 128, 128), 128)
    own_slots, sib_slots = pl.ds(0, 4), pl.ds(4, 4)
    own_wave = pltpu.make_async_copy(wave.at[mine, :], wide.at[b, :, columns], own_sem.at[0])
    own_wave.start()
    lane = lax.broadcasted_iota(jnp.int32, (8, 128), 1)
    numbers = jnp.where(lane == 0, count[0], 0)
    for k in range(4):
        numbers = jnp.where(lane == 1 + k, source[k], numbers)
        numbers = jnp.where(lane == 5 + k, target[k], numbers)
    table[...] = numbers
    greet(
        ring_peers(x, z)
        + [sib, {"x": turn(x, 2)}, {"z": turn(z, 2)}, {"sec": turn(y, 1)}, {"sec": turn(y, 2)}, {"sec": turn(y, -1)}]
    )
    swaps = [
        push(wave.at[other, :], wide.at[b, :, columns], swap_send.at[0], swap_recv.at[0], sib),
        push(table, table_in, swap_send.at[1], swap_recv.at[1], sib),
        push(row_ops.at[:, other, :], row_v.at[sib_slots], swap_send.at[2], swap_recv.at[2], sib),
        push(col_ops, col_v.at[sib_slots], swap_send.at[3], swap_recv.at[3], sib),
    ]
    swaps[0].start()
    own_wave.wait()

    def swapped():
        push(wave.at[other, :], wide.at[b, :, other_columns], swap_send.at[0], swap_recv.at[0], sib).wait_recv()

    steps = all_blocks(wide, x, z, wv_send, wv_recv, (columns, other_columns, swapped), CUT)
    next(steps)
    for swap in swaps[1:]:
        swap.start()
    own_rows = pltpu.make_async_copy(row_ops.at[:, mine, :], row_v.at[own_slots], own_sem.at[1])
    own_cols = pltpu.make_async_copy(col_ops, col_v.at[own_slots], own_sem.at[5])
    own_rows.start()
    own_cols.start()
    same = lax.broadcasted_iota(jnp.int32, (128, 128), 0) == lax.broadcasted_iota(jnp.int32, (128, 128), 1)
    for i in range(4):
        spread = jnp.where(same, jnp.broadcast_to(energy_row[pl.ds(c * 4 + i, 1), :], (128, 128)), 0.0)
        energy_col[pl.ds(i * 128, 128), :] = jnp.sum(spread, axis=1, keepdims=True)
    swaps[1].wait_recv()
    to_scalars = pltpu.make_async_copy(table_in, table_s, own_sem.at[6])
    to_scalars.start()
    to_scalars.wait()

    def flag(condition):
        return condition.astype(jnp.int32)

    keys, sources = [], []
    for side in (0, 1):
        live = table_s[0, 0] if side else count[0]
        for k in range(4):
            alive = flag(k < live)
            aim = table_s[0, 5 + k] if side else target[k]
            keys.append(aim * alive + 8 * (1 - alive))
            sources.append(table_s[0, 1 + k] if side else source[k])
    ranks = []
    for i in range(8):
        ahead = [flag(keys[j] <= keys[i]) if j < i else flag(keys[j] < keys[i]) for j in range(8) if j != i]
        ranks.append(sum(ahead))
    for j in range(8):
        order_s[j] = sum(i * flag(ranks[i] == j) for i in range(8))
        source_s[j] = sum(sources[i] * flag(ranks[i] == j) for i in range(8))
    starts = [sum(flag(key < t) for key in keys) for t in range(9)]

    for ready in steps:
        del ready
    swaps[0].wait_send()
    swaps[1].wait_send()
    own_rows.wait()
    own_cols.wait()
    swaps[2].wait()
    swaps[3].wait()

    reduction = Reduction(
        (part, near, whole, near2, whole2, total), (rs_send, rs_recv, mod_send, mod_recv, rs2_send, rs2_recv), x, z
    )
    prefix[0] = jnp.zeros((HALF, SEC), F32)
    for h in (0, 1):
        here = pl.ds(h * HALF, HALF)

        def term(j, carry, here=here):
            slot = order_s[j]
            src = source_s[j] * 2
            rows = row_v[slot, here, :]
            first = dot(rows, wide[src]).astype(BF16)
            second = dot(rows, wide[src + 1]).astype(BF16)
            prefix[j + 1] = prefix[j] + (dot(first, col_v[slot, :WIDE, :]) + dot(second, col_v[slot, WIDE:, :]))
            return carry

        lax.fori_loop(0, 8, term, 0)
        for t in range(8):
            added = (prefix[starts[t + 1]] - prefix[starts[t]]).astype(BF16)
            part[t // 2, 2 * (t % 2), here, :] = added[:, :WIDE]
            part[t // 2, 2 * (t % 2) + 1, here, :] = added[:, WIDE:]
        reduction.begin(h)

    amplitude = wide[b].astype(F32)

    def overlap(i, carry):
        product = part[lax.div(i, 4), lax.rem(i, 4)].astype(F32) * wide[i].astype(F32)
        return carry + jnp.sum(product.reshape(SEC // 8, 8, WIDE), axis=0)

    level = energy_col[...]
    shares = lax.fori_loop(0, CHIPS, overlap, jnp.sum((level * amplitude * amplitude).reshape(SEC // 8, 8, WIDE), axis=0))
    share = jnp.sum(shares, axis=(0, 1), keepdims=True)
    stages = (("sec", y, 4), ("x", x, 4), ("z", z, 4), ("core", c, 2))

    def energy_copies(s):
        name, place, size = stages[s]
        for hop in range(1, size):
            to = {name: lax.rem(place + hop, size)}
            src = lax.rem(place + (size - hop), size)
            yield (
                push(scalars.at[s, place], scalars.at[s, place], en_send.at[s, hop], en_recv.at[s, hop], to),
                push(scalars.at[s, src], scalars.at[s, src], en_send.at[s, hop], en_recv.at[s, hop], to),
            )

    works = (
        lambda: (reduction.add(0), reduction.add(1)),
        lambda: reduction.second(0),
        lambda: reduction.second(1),
        lambda: (reduction.add2(0), reduction.add2(1)),
    )
    for s in range(4):
        place, size = stages[s][1:]
        scalars[s, place] = jnp.broadcast_to(share, (8, 128))
        for out, unused in energy_copies(s):
            out.start()
        works[s]()
        for out, arriving in energy_copies(s):
            arriving.wait_recv()
            out.wait_send()
        share = scalars[s, 0] + scalars[s, 1]
        if size == 4:
            share = (share + scalars[s, 2]) + scalars[s, 3]
        share = share[0:1, 0:1]
    energy = share * (1.0 / ENTRIES)
    energy_o[...] = jnp.broadcast_to(energy, (8, 128))

    steps = all_blocks(stepped, x, z, ag_send, ag_recv, None, CUT, True)
    for h in (0, 1):
        reduction.finish(h)
        here = pl.ds(h * HALF, HALF)
        mild = wide[b, here, :].astype(F32)
        own = mild + 0.5 * (energy * mild - (energy_col[here, :] * mild + total[here, :]))
        stepped[b, here, :] = own.astype(BF16)
        next(steps)
        exact[0, here, :] = own[:, :128]
        exact[1, here, :] = own[:, 128:]
    reduction.close()
    exact_send = push(exact.at[1 - c], exact_o.at[mine, :], end_send.at[0], end_recv.at[0], sib)
    exact_own = pltpu.make_async_copy(exact.at[c], exact_o.at[mine, :], own_sem.at[2])
    exact_send.start()
    exact_own.start()

    def out_block(i):
        return (
            push(stepped.at[i], stepped_o.at[c, i], st_send.at[i], st_recv.at[i], sib),
            pltpu.make_async_copy(stepped.at[i], stepped_o.at[c, i], st_own.at[i]),
        )

    gram[...] = jnp.zeros((SEC, SEC), F32)

    def add_group(group):
        def one_block(t, carry):
            i = group_block(group, t, x, z)
            value = stepped[i]
            for one in out_block(i):
                one.start()
            gram[...] += dot_t(value, value)
            return carry

        lax.fori_loop(0, GROUP_SIZE[group], one_block, 0)

    for ready in steps:
        if ready:
            add_group(ready)

    def root(d_ref, again):
        small[0] = gram[...].astype(BF16)
        my[...] = 1.5 * gram[...] - 0.5 * dot(small[0], small[0])
        small[1] = my[...].astype(BF16)
        value = 1.5 * my[...] - 0.5 * dot(small[0], small[1])
        mu[...] = value
        small[2] = value.astype(BF16)
        d_ref[...] = 0.25 * dot(small[2], small[0]) - 0.75 * (gram[...] + mu[...])
        if again:
            gram[...] = 1.5 * my[...] - 0.5 * dot(small[1], small[2])

    squares = jnp.sum(gram[...] * gram[...], axis=(0, 1), keepdims=True)
    scale_one = jnp.sqrt(squares * (1.0 / COLS) * (1.0 / COLS) + 1e-06)
    gram[...] = gram[...] * ((1.0 / COLS) / scale_one)
    root(mz, True)
    gram[...] = 2.25 * gram[...] + rough(mz[...], gram[...])
    scale_two = frobenius(gram[...])
    gram[...] = gram[...] * (1.0 / scale_two)
    root(mm, False)
    size = jnp.sqrt(scale_one) * jnp.sqrt(scale_two)
    over = 1.0 / size
    small[0] = mz[...].astype(BF16)
    root_copies = []
    for h in (0, 1):
        here = pl.ds(h * HALF, HALF)
        both = 2.25 * (mz[here, :] + mm[here, :]) + rough(mm[here, :], small[0])
        roots[here, :] = (both * over).astype(BF16)
        root_copies.append(push(roots.at[here, :], root_o.at[c, here, :], root_send.at[h], root_recv.at[h], sib))
        root_copies[h].start()
    level_two[...] = jnp.broadcast_to(2.25 * 2.25 / size, (8, 128))
    root_own = pltpu.make_async_copy(roots, root_o.at[c], own_sem.at[3])
    level_send = push(level_two, level_o.at[c], end_send.at[2], end_recv.at[2], sib)
    level_own = pltpu.make_async_copy(level_two, level_o.at[c], own_sem.at[4])
    level_send.start()
    level_own.start()
    root_own.start()

    def block_done(i, carry):
        going, staying = out_block(i)
        going.wait_send()
        staying.wait()
        push(stepped.at[i], stepped_o.at[1 - c, i], st_send.at[i], st_recv.at[i], sib).wait_recv()
        return carry

    lax.fori_loop(0, CHIPS, block_done, 0)
    exact_send.wait_send()
    exact_own.wait()
    push(exact.at[1 - c], exact_o.at[other, :], end_send.at[0], end_recv.at[0], sib).wait_recv()
    for one in root_copies:
        one.wait_send()
    root_own.wait()
    for h in (0, 1):
        here = pl.ds(h * HALF, HALF)
        push(roots.at[here, :], root_o.at[1 - c, here, :], root_send.at[h], root_recv.at[h], sib).wait_recv()
    level_send.wait_send()
    level_own.wait()
    push(level_two, level_o.at[1 - c], end_send.at[2], end_recv.at[2], sib).wait_recv()


def site(wave, row_ops, col_ops, count, source, target, energy_row):
    hbm = pl.BlockSpec(memory_space=pltpu.HBM)
    smem = pl.BlockSpec(memory_space=pltpu.SMEM)
    vmem = pl.BlockSpec(memory_space=pltpu.VMEM)
    square = pltpu.VMEM((SEC, SEC), F32)
    blocks = pltpu.VMEM((CHIPS, SEC, WIDE), BF16)
    dma = pltpu.SemaphoreType.DMA
    return pl.pallas_call(
        site_kernel,
        out_shape=(
            jax.ShapeDtypeStruct((2, CHIPS, SEC, WIDE), BF16),
            jax.ShapeDtypeStruct((2, SEC, SEC), BF16),
            jax.ShapeDtypeStruct((2, 8, 128), F32),
            jax.ShapeDtypeStruct((2 * SEC, 128), F32),
            jax.ShapeDtypeStruct((8, 128), F32),
        ),
        in_specs=[hbm] * 3 + [smem] * 3 + [vmem],
        out_specs=(hbm, hbm, hbm, hbm, vmem),
        scratch_shapes=[
            blocks,
            pltpu.VMEM((8, SEC, SEC), BF16),
            pltpu.VMEM((8, SEC, SEC), BF16),
            pltpu.VMEM((8, 128), jnp.int32),
            pltpu.VMEM((8, 128), jnp.int32),
            pltpu.SMEM((8, 128), jnp.int32),
            pltpu.SMEM((8,), jnp.int32),
            pltpu.SMEM((8,), jnp.int32),
            pltpu.VMEM((9, HALF, SEC), F32),
            pltpu.VMEM((4, 4, SEC, WIDE), BF16),
            pltpu.VMEM((2, 2, 2, 4, EIGHTH, WIDE), BF16),
            pltpu.VMEM((2, 2, 2, 4, QUARTER, WIDE), BF16),
            pltpu.VMEM((2, 2, 2, EIGHTH, WIDE), BF16),
            pltpu.VMEM((2, 2, 2, QUARTER, WIDE), BF16),
            pltpu.VMEM((SEC, WIDE), F32),
            blocks,
            square,
            square,
            square,
            square,
            square,
            pltpu.VMEM((3, SEC, SEC), BF16),
            pltpu.VMEM((SEC, SEC), BF16),
            pltpu.VMEM((8, 128), F32),
            pltpu.VMEM((2, SEC, 128), F32),
            pltpu.VMEM((4, 4, 8, 128), F32),
            pltpu.VMEM((SEC, 1), F32),
            dma((2, 32)),
            dma((2, 32)),
            dma((4,)),
            dma((4,)),
            dma((2, 2, 4)),
            dma((2, 2, 4)),
            dma((2, 2, 2, 4)),
            dma((2, 2, 2, 4)),
            dma((2, 2, 6)),
            dma((2, 2, 6)),
            dma((2, 32)),
            dma((2, 32)),
            dma((4, 4)),
            dma((4, 4)),
            dma((CHIPS,)),
            dma((CHIPS,)),
            dma((CHIPS,)),
            dma((3,)),
            dma((3,)),
            dma((2,)),
            dma((2,)),
            dma((7,)),
        ],
        compiler_params=pltpu.CompilerParams(
            collective_id=0, has_side_effects=True, vmem_limit_bytes=60 * MIB
        ),
        name="site",
    )(wave, row_ops, col_ops, count, source, target, energy_row)


def renorm_kernel(
    count, source, target, stepped, cols, root, level, exact, energy,
    out, wave_o, energy_o,
    block_v, cols_v, root_v, out_v, zero_v, exact_v, wave_v, level_v, block_sem, cols_sem, root_sem, out_sem, exact_sem, wave_sem, level_sem,
):
    energy_o[0] = energy[0, 0]

    def needs(k, s):
        pair = (source[k], target[k])
        return [
            pltpu.make_async_copy(
                stepped.at[s, pl.ds(2 * pair[e], 2)], block_v.at[k, s, e], block_sem.at[k, s, e]
            )
            for e in (0, 1)
        ]

    def column_op(k):
        return pltpu.make_async_copy(cols.at[k], cols_v.at[k], cols_sem.at[k])

    def result(k, s):
        return pltpu.make_async_copy(out_v.at[k, s], out.at[k, pl.ds(s * SEC, SEC), :], out_sem.at[k, s])

    def nothing(k, s):
        return pltpu.make_async_copy(zero_v, out.at[k, pl.ds(s * SEC, SEC), :], out_sem.at[k, s])

    roots = [pltpu.make_async_copy(root.at[s], root_v.at[s], root_sem.at[s]) for s in (0, 1)]
    load_level = pltpu.make_async_copy(level, level_v, level_sem)
    load_level.start()
    roots[0].start()
    for one in needs(0, 0):
        one.start()
    column_op(0).start()
    roots[1].start()
    for one in needs(0, 1):
        one.start()
    zero_v[...] = jnp.zeros_like(zero_v)
    load_exact = pltpu.make_async_copy(exact, exact_v, exact_sem)
    load_level.wait()
    roots[0].wait()

    def one_term(k, carry):
        column_op(k).wait()
        for s in (0, 1):
            scale = level_v[s, 0:1, 0:1]
            for one in needs(k, s):
                one.wait()
            if s == 0:

                @pl.when(k + 1 < count[0])
                def ahead():
                    column_op(k + 1).start()
                    for t in (0, 1):
                        for one in needs(k + 1, t):
                            one.start()

                @pl.when(k == 0)
                def others():
                    load_exact.start()
                    for empty in range(1, 4):

                        @pl.when(empty >= count[0])
                        def clear(empty=empty):
                            nothing(empty, 0).start()
                            nothing(empty, 1).start()
            else:

                @pl.when(k == 0)
                def second_root():
                    roots[1].wait()
            halves = []
            for e in (0, 1):
                block = jnp.concatenate([block_v[k, s, e, 0], block_v[k, s, e, 1]], axis=1)
                halves.append((scale * block.astype(F32) + dot(root_v[s], block)).astype(BF16))
            product = dot(halves[0], cols_v[k]).astype(BF16)
            out_v[k, s] = dot_t(product, halves[1]) * SEC ** (-0.5)
            result(k, s).start()
        return carry

    lax.fori_loop(0, count[0], one_term, 0)
    load_exact.wait()
    waves = []
    for s in (0, 1):
        rows = pl.ds(s * SEC, SEC)
        own = exact_v[rows, :]
        wave_v[rows, :] = level_v[s, 0:1, 0:1] * own + dot(root_v[s], own.astype(BF16))
        waves.append(pltpu.make_async_copy(wave_v.at[rows, :], wave_o.at[rows, :], wave_sem.at[s]))
        waves[s].start()
    for one in waves:
        one.wait()
    for k in range(4):
        for s in (0, 1):
            result(k, s).wait()


def renorm(count, source, target, stepped, cols, root, level, exact, energy):
    hbm = pl.BlockSpec(memory_space=pltpu.HBM)
    smem = pl.BlockSpec(memory_space=pltpu.SMEM)
    return pl.pallas_call(
        renorm_kernel,
        out_shape=(
            jax.ShapeDtypeStruct((4, 2 * SEC, SEC), F32),
            jax.ShapeDtypeStruct((2 * SEC, 128), F32),
            jax.ShapeDtypeStruct((1,), F32),
        ),
        in_specs=[smem] * 3 + [hbm] * 5 + [smem],
        out_specs=(hbm, hbm, smem),
        scratch_shapes=[
            pltpu.VMEM((4, 2, 2, 2, SEC, WIDE), BF16),
            pltpu.VMEM((4, SEC, SEC), BF16),
            pltpu.VMEM((2, SEC, SEC), BF16),
            pltpu.VMEM((4, 2, SEC, SEC), F32),
            pltpu.VMEM((SEC, SEC), F32),
            pltpu.VMEM((2 * SEC, 128), F32),
            pltpu.VMEM((2 * SEC, 128), F32),
            pltpu.VMEM((2, 8, 128), F32),
            pltpu.SemaphoreType.DMA((4, 2, 2)),
            pltpu.SemaphoreType.DMA((4,)),
            pltpu.SemaphoreType.DMA((2,)),
            pltpu.SemaphoreType.DMA((4, 2)),
            pltpu.SemaphoreType.DMA(()),
            pltpu.SemaphoreType.DMA((2,)),
            pltpu.SemaphoreType.DMA(()),
        ],
        compiler_params=pltpu.CompilerParams(vmem_limit_bytes=60 * MIB),
        name="renorm",
    )(count, source, target, stepped, cols, root, level, exact, energy)


def on_device(wave_in, row_energy, row_operators, column_operators, term_count, source, target):
    stepped, root, level, exact, energy = site(
        wave_in, row_operators, column_operators, term_count, source, target, row_energy.reshape(8, 128)
    )
    renormalized, wave_next, energy = renorm(
        term_count, source, target, stepped, column_operators, root, level, exact, energy
    )
    return (wave_next, renormalized, energy.reshape(()))


def solution(mesh):
    torus = Mesh(mesh.devices.reshape(4, 4, 2, mesh.shape["sec"]), ("x", "z", "core", "sec"))
    return jax.shard_map(
        on_device,
        mesh=torus,
        in_specs=(
            P("sec", OPS),
            P("sec"),
            P(OPS, "sec", None),
            P(OPS, None, None),
            P(OPS),
            P(OPS),
            P(OPS),
        ),
        out_specs=(P("sec", OPS), P(OPS, "sec", None), P()),
        check_vma=False,
    )
```

```python
import functools

import jax
import jax.numpy as jnp
from jax import lax
from jax.experimental import pallas as pl
from jax.experimental.pallas import tpu as pltpu
from jax.sharding import Mesh
from jax.sharding import PartitionSpec as P

SEC = 512
COLS = 4096
ENTRIES = 4096 * 4096
CHIPS = 16
WIDE = 256
HALF = 256
QUARTER = 128
EIGHTH = 64
CUT = (0, 1, 2, 3)
MIB = 1 << 20
MESH = pl.DeviceIdType.MESH
OPS = ("x", "z", "core")
F32 = jnp.float32
BF16 = jnp.bfloat16


def turn(place, by):
    return lax.rem(place + (by + 4), 4)


def push(src, dst, send, recv, to):
    return pltpu.make_async_remote_copy(
        src_ref=src, dst_ref=dst, send_sem=send, recv_sem=recv, device_id=to, device_id_type=MESH
    )


def greet(peers):
    barrier = pltpu.get_barrier_semaphore()
    for peer in peers:
        pl.semaphore_signal(barrier, inc=1, device_id=peer, device_id_type=MESH)
    pl.semaphore_wait(barrier, len(peers))


def all_blocks(buf, x, z, send, recv, late=None, cut=(), apart=False):
    names = (("x", "z"), ("z", "x"))
    places = ((x, z), (z, x))
    every = slice(None)

    def block(h, pa, pb):
        return pa * 4 + pb if h == 0 else pb * 4 + pa

    def copy(h, j, pa, pb, part, axis, by, columns=every):
        rows = pl.ds(h * HALF, HALF) if part is None else pl.ds(h * HALF + part * QUARTER, QUARTER)
        ref = buf.at[block(h, pa, pb), rows, columns]
        to = {names[h][axis]: turn(places[h][axis], by)}
        return push(ref, ref, send.at[h, j], recv.at[h, j], to)

    def order(h):
        p = places[h][0]
        return (p, turn(p, -1), turn(p, 1), turn(p, 2))

    sent = []

    def go(*what):
        one = copy(*what)
        one.start()
        sent.append(one)

    def arrived(h, j, pa, pb, part, columns=every):
        copy(h, j, pa, pb, part, 0, 1, columns).wait_recv()

    def across(h, i):
        pa, q = order(h)[i], places[h][1]
        for d in (0, 1):
            for n in (0, 1) if i in cut else (0,):
                part = (d + n) % 2 if i in cut else None
                go(h, 8 + 4 * i + 2 * d + n, pa, q, part, 1, 1 - 2 * d)

    def across_arrived(h, i, d, n):
        part = (d + n) % 2 if i in cut else None
        arrived(h, 8 + 4 * i + 2 * d + n, order(h)[i], turn(places[h][1], 2 * d - 1), part)

    def onward(h, i):
        pa, q = order(h)[i], places[h][1]
        for d in (0, 1):
            across_arrived(h, i, d, 0)
            go(h, 24 + 2 * i + d, pa, turn(q, 2 * d - 1), d, 1, 1 - 2 * d)

    def rest(h, i):
        if i in cut:
            across_arrived(h, i, 0, 1)
            across_arrived(h, i, 1, 1)

    def first(h, columns, j):
        p, q = places[h]
        go(h, j, p, q, None, 0, 1, columns)
        go(h, j + 1, p, q, None, 0, -1, columns)

    if late is None:
        for h in (0, 1):
            first(h, every, 0)
            if apart:
                across(h, 0)
                yield
    else:
        for h in (0, 1):
            first(h, late[0], 0)
        late[2]()
        for h in (0, 1):
            first(h, late[1], 2)
    if not apart:
        for h in (0, 1):
            across(h, 0)
        yield
    for h in (0, 1):
        p, q = places[h]
        for d in (0, 1):
            side = turn(p, 2 * d - 1)
            if late is None:
                arrived(h, d, side, q, None)
            else:
                arrived(h, d, side, q, None, late[0])
                arrived(h, 2 + d, side, q, None, late[1])
            go(h, 4 + d, side, q, d, 0, 1 - 2 * d)
    for h in (0, 1):
        across(h, 1)
        across(h, 2)
    yield
    def last(i):
        for h in (0, 1):
            pa, far = order(h)[i], turn(places[h][1], 2)
            arrived(h, 24 + 2 * i, pa, far, 0)
            arrived(h, 25 + 2 * i, pa, far, 1)

    for h in (0, 1):
        onward(h, 0)
    for h in (0, 1):
        p, q = places[h]
        arrived(h, 4, turn(p, 2), q, 0)
        arrived(h, 5, turn(p, 2), q, 1)
        across(h, 3)
    for h in (0, 1):
        rest(h, 0)
    for i in (1, 2):
        for h in (0, 1):
            onward(h, i)
    yield 1
    for h in (0, 1):
        onward(h, 3)
    for i in (1, 2, 3):
        for h in (0, 1):
            rest(h, i)
    yield 2
    last(0)
    yield 3
    last(1)
    last(2)
    yield 4
    last(3)
    yield 5
    for one in sent:
        one.wait_send()


def ring_peers(x, z):
    return [{"x": turn(x, 1)}, {"x": turn(x, -1)}, {"z": turn(z, 1)}, {"z": turn(z, -1)}]


def dot(a, b):
    return jnp.dot(a, b, preferred_element_type=F32)


def dot_t(a, b):
    return lax.dot_general(a, b, (((1,), (1,)), ((), ())), preferred_element_type=F32)


def rough(a, b):
    return dot(a.astype(BF16), b.astype(BF16))


class Reduction:
    def __init__(self, bufs, sems, x, z):
        self.part, self.near, self.whole, self.near2, self.whole2, self.total = bufs
        self.send, self.recv, self.mod_send, self.mod_recv, self.send2, self.recv2 = sems
        self.places = ((z, x), (x, z))
        self.sent = []

    def at(self, h, pa, pb):
        return (pb, pa) if h == 0 else (pa, pb)

    def rows(self, w, h, half):
        return pl.ds(w * HALF + h * QUARTER + half * EIGHTH, EIGHTH)

    def both_rows(self, w, h):
        return pl.ds(w * HALF + h * QUARTER, QUARTER)

    def line(self, w, h, pa, half):
        rows = self.rows(w, h, half)
        return self.part.at[:, pa, rows, :] if h == 0 else self.part.at[pa, :, rows, :]

    def order(self, h):
        q = self.places[h][1]
        return (turn(q, 2), turn(q, 1), turn(q, -1), q)

    def peer(self, h, axis, d):
        return {("zx", "xz")[h][axis]: turn(self.places[h][axis], 1 - 2 * d)}

    def go(self, one):
        one.start()
        self.sent.append(one)

    def near_copy(self, w, h, d):
        src = self.line(w, h, turn(self.places[h][0], 2), d)
        return push(src, self.near.at[w, h, d], self.send.at[w, h, d], self.recv.at[w, h, d], self.peer(h, 0, d))

    def plain_copy(self, w, h, d):
        src = self.line(w, h, turn(self.places[h][0], 1 - 2 * d), 1 - d)
        dst = self.whole.at[w, h, d, :, pl.ds((1 - d) * EIGHTH, EIGHTH), :]
        return push(src, dst, self.send.at[w, h, 2 + d], self.recv.at[w, h, 2 + d], self.peer(h, 0, d))

    def added_copy(self, w, h, d, i):
        to = self.order(h)[i]
        src = self.part.at[*self.at(h, turn(self.places[h][0], 1 - 2 * d), to), self.rows(w, h, d), :]
        dst = self.whole.at[w, h, d, to, pl.ds(d * EIGHTH, EIGHTH), :]
        return push(src, dst, self.mod_send.at[w, h, d, i], self.mod_recv.at[w, h, d, i], self.peer(h, 0, d))

    def near2_copy(self, w, h, d):
        p, q = self.places[h]
        src = self.part.at[*self.at(h, p, turn(q, 2)), self.rows(w, h, d), :]
        return push(src, self.near2.at[w, h, d], self.send2.at[w, h, d], self.recv2.at[w, h, d], self.peer(h, 1, d))

    def whole2_copy(self, w, h, d, half):
        p, q = self.places[h]
        j = 2 + 2 * d + half
        src = self.part.at[*self.at(h, p, turn(q, 1 - 2 * d)), self.rows(w, h, half), :]
        dst = self.whole2.at[w, h, d, pl.ds(half * EIGHTH, EIGHTH), :]
        return push(src, dst, self.send2.at[w, h, j], self.recv2.at[w, h, j], self.peer(h, 1, d))

    def begin(self, w):
        for h in (0, 1):
            for d in (0, 1):
                self.go(self.near_copy(w, h, d))
        for h in (0, 1):
            for d in (0, 1):
                self.go(self.plain_copy(w, h, d))

    def add(self, w):
        for h in (0, 1):
            p = self.places[h][0]
            for d in (0, 1):
                self.near_copy(w, h, d).wait_recv()
                for i in range(4):
                    to = self.order(h)[i]
                    spot = (*self.at(h, turn(p, 1 - 2 * d), to), self.rows(w, h, d), slice(None))
                    both = self.part[spot].astype(F32) + self.near[w, h, d, to].astype(F32)
                    self.part[spot] = both.astype(BF16)
                    self.go(self.added_copy(w, h, d, i))

    def second(self, w):
        for h in (0, 1):
            for d in (0, 1):
                self.plain_copy(w, h, d).wait_recv()
        for i in range(4):
            for h in (0, 1):
                p = self.places[h][0]
                for d in (0, 1):
                    self.added_copy(w, h, d, i).wait_recv()
                to = self.order(h)[i]
                spot = (*self.at(h, p, to), self.both_rows(w, h), slice(None))
                done = self.part[spot].astype(F32) + self.whole[w, h, 0, to].astype(F32) + self.whole[w, h, 1, to].astype(F32)
                if i == 3:
                    self.total[self.both_rows(w, h), :] = done
                else:
                    self.part[spot] = done.astype(BF16)
                if i == 0:
                    self.go(self.near2_copy(w, h, 0))
                    self.go(self.near2_copy(w, h, 1))
                if i == 1:
                    self.go(self.whole2_copy(w, h, 0, 1))
                if i == 2:
                    self.go(self.whole2_copy(w, h, 1, 0))

    def add2(self, w):
        for h in (0, 1):
            p, q = self.places[h]
            for d in (0, 1):
                self.near2_copy(w, h, d).wait_recv()
                spot = (*self.at(h, p, turn(q, 1 - 2 * d)), self.rows(w, h, d), slice(None))
                both = self.part[spot].astype(F32) + self.near2[w, h, d].astype(F32)
                self.part[spot] = both.astype(BF16)
                self.go(self.whole2_copy(w, h, d, d))

    def finish(self, w):
        for h in (0, 1):
            for d in (0, 1):
                for half in (0, 1):
                    self.whole2_copy(w, h, d, half).wait_recv()
            here = self.both_rows(w, h)
            self.total[here, :] += self.whole2[w, h, 0].astype(F32) + self.whole2[w, h, 1].astype(F32)

    def close(self):
        for one in self.sent:
            one.wait_send()


def frobenius(a):
    return jnp.sqrt(jnp.sum(a * a, axis=(0, 1), keepdims=True) + 1e-06)


def group_block(group, t, x, z):
    if group == 1:
        dx = (t == 1).astype(jnp.int32) - (t == 2).astype(jnp.int32)
        dz = (t == 3).astype(jnp.int32) - (t == 4).astype(jnp.int32)
    elif group == 2:
        dx, dz = 1 - 2 * lax.rem(t, 2), 1 - 2 * lax.div(t, 2)
    elif group == 3:
        dx, dz = 2 - 2 * t, 2 * t
    elif group == 4:
        dx, dz = jnp.where(t < 2, 1 - 2 * t, 2), jnp.where(t < 2, 2, 5 - 2 * t)
    else:
        dx = dz = 2
    return turn(x, dx) * 4 + turn(z, dz)


GROUP_SIZE = {1: 5, 2: 4, 3: 2, 4: 4, 5: 1}


def site_kernel(
    wave, row_ops, col_ops, count, source, target, energy_row,
    stepped_o, root_o, level_o, exact_o, energy_o,
    wide, row_v, col_v, table, table_in, table_s, order_s, source_s, prefix,
    part, near, whole, near2, whole2, total, stepped, gram, my, mm, mu, mz, small, roots, level_two, exact, scalars, energy_col,
    wv_send, wv_recv, swap_send, swap_recv,
    rs_send, rs_recv, mod_send, mod_recv, rs2_send, rs2_recv, ag_send, ag_recv, en_send, en_recv, st_send, st_recv, st_own,
    end_send, end_recv, root_send, root_recv, own_sem,
):
    x, z, c, y = lax.axis_index("x"), lax.axis_index("z"), lax.axis_index("core"), lax.axis_index("sec")
    b = x * 4 + z
    sib = {"core": 1 - c}
    mine = pl.ds(pl.multiple_of(c * SEC, SEC), SEC)
    other = pl.ds(pl.multiple_of((1 - c) * SEC, SEC), SEC)
    columns = pl.ds(pl.multiple_of(c * 128, 128), 128)
    other_columns = pl.ds(pl.multiple_of((1 - c) * 128, 128), 128)
    own_slots, sib_slots = pl.ds(0, 4), pl.ds(4, 4)
    own_wave = pltpu.make_async_copy(wave.at[mine, :], wide.at[b, :, columns], own_sem.at[0])
    own_wave.start()
    lane = lax.broadcasted_iota(jnp.int32, (8, 128), 1)
    numbers = jnp.where(lane == 0, count[0], 0)
    for k in range(4):
        numbers = jnp.where(lane == 1 + k, source[k], numbers)
        numbers = jnp.where(lane == 5 + k, target[k], numbers)
    table[...] = numbers
    greet(
        ring_peers(x, z)
        + [sib, {"x": turn(x, 2)}, {"z": turn(z, 2)}, {"sec": turn(y, 1)}, {"sec": turn(y, 2)}, {"sec": turn(y, -1)}]
    )
    swaps = [
        push(wave.at[other, :], wide.at[b, :, columns], swap_send.at[0], swap_recv.at[0], sib),
        push(table, table_in, swap_send.at[1], swap_recv.at[1], sib),
        push(row_ops.at[:, other, :], row_v.at[sib_slots], swap_send.at[2], swap_recv.at[2], sib),
        push(col_ops, col_v.at[sib_slots], swap_send.at[3], swap_recv.at[3], sib),
    ]
    swaps[0].start()
    own_wave.wait()

    def swapped():
        push(wave.at[other, :], wide.at[b, :, other_columns], swap_send.at[0], swap_recv.at[0], sib).wait_recv()

    steps = all_blocks(wide, x, z, wv_send, wv_recv, (columns, other_columns, swapped), CUT)
    next(steps)
    for swap in swaps[1:]:
        swap.start()
    own_rows = pltpu.make_async_copy(row_ops.at[:, mine, :], row_v.at[own_slots], own_sem.at[1])
    own_cols = pltpu.make_async_copy(col_ops, col_v.at[own_slots], own_sem.at[5])
    own_rows.start()
    own_cols.start()
    same = lax.broadcasted_iota(jnp.int32, (128, 128), 0) == lax.broadcasted_iota(jnp.int32, (128, 128), 1)
    for i in range(4):
        spread = jnp.where(same, jnp.broadcast_to(energy_row[pl.ds(c * 4 + i, 1), :], (128, 128)), 0.0)
        energy_col[pl.ds(i * 128, 128), :] = jnp.sum(spread, axis=1, keepdims=True)
    swaps[1].wait_recv()
    to_scalars = pltpu.make_async_copy(table_in, table_s, own_sem.at[6])
    to_scalars.start()
    to_scalars.wait()

    def flag(condition):
        return condition.astype(jnp.int32)

    keys, sources = [], []
    for side in (0, 1):
        live = table_s[0, 0] if side else count[0]
        for k in range(4):
            alive = flag(k < live)
            aim = table_s[0, 5 + k] if side else target[k]
            keys.append(aim * alive + 8 * (1 - alive))
            sources.append(table_s[0, 1 + k] if side else source[k])
    ranks = []
    for i in range(8):
        ahead = [flag(keys[j] <= keys[i]) if j < i else flag(keys[j] < keys[i]) for j in range(8) if j != i]
        ranks.append(sum(ahead))
    for j in range(8):
        order_s[j] = sum(i * flag(ranks[i] == j) for i in range(8))
        source_s[j] = sum(sources[i] * flag(ranks[i] == j) for i in range(8))
    starts = [sum(flag(key < t) for key in keys) for t in range(9)]

    for ready in steps:
        del ready
    swaps[0].wait_send()
    swaps[1].wait_send()
    own_rows.wait()
    own_cols.wait()
    swaps[2].wait()
    swaps[3].wait()

    reduction = Reduction(
        (part, near, whole, near2, whole2, total), (rs_send, rs_recv, mod_send, mod_recv, rs2_send, rs2_recv), x, z
    )
    prefix[0] = jnp.zeros((HALF, SEC), F32)
    for h in (0, 1):
        here = pl.ds(h * HALF, HALF)

        def term(j, carry, here=here):
            slot = order_s[j]
            src = source_s[j] * 2
            rows = row_v[slot, here, :]
            first = dot(rows, wide[src]).astype(BF16)
            second = dot(rows, wide[src + 1]).astype(BF16)
            prefix[j + 1] = prefix[j] + (dot(first, col_v[slot, :WIDE, :]) + dot(second, col_v[slot, WIDE:, :]))
            return carry

        lax.fori_loop(0, 8, term, 0)
        for t in range(8):
            added = (prefix[starts[t + 1]] - prefix[starts[t]]).astype(BF16)
            part[t // 2, 2 * (t % 2), here, :] = added[:, :WIDE]
            part[t // 2, 2 * (t % 2) + 1, here, :] = added[:, WIDE:]
        reduction.begin(h)

    amplitude = wide[b].astype(F32)

    def overlap(i, carry):
        product = part[lax.div(i, 4), lax.rem(i, 4)].astype(F32) * wide[i].astype(F32)
        return carry + jnp.sum(product.reshape(SEC // 8, 8, WIDE), axis=0)

    level = energy_col[...]
    shares = lax.fori_loop(0, CHIPS, overlap, jnp.sum((level * amplitude * amplitude).reshape(SEC // 8, 8, WIDE), axis=0))
    share = jnp.sum(shares, axis=(0, 1), keepdims=True)
    stages = (("sec", y, 4), ("x", x, 4), ("z", z, 4), ("core", c, 2))

    def energy_copies(s):
        name, place, size = stages[s]
        for hop in range(1, size):
            to = {name: lax.rem(place + hop, size)}
            src = lax.rem(place + (size - hop), size)
            yield (
                push(scalars.at[s, place], scalars.at[s, place], en_send.at[s, hop], en_recv.at[s, hop], to),
                push(scalars.at[s, src], scalars.at[s, src], en_send.at[s, hop], en_recv.at[s, hop], to),
            )

    works = (
        lambda: (reduction.add(0), reduction.add(1)),
        lambda: reduction.second(0),
        lambda: reduction.second(1),
        lambda: (reduction.add2(0), reduction.add2(1)),
    )
    for s in range(4):
        place, size = stages[s][1:]
        scalars[s, place] = jnp.broadcast_to(share, (8, 128))
        for out, unused in energy_copies(s):
            out.start()
        works[s]()
        for out, arriving in energy_copies(s):
            arriving.wait_recv()
            out.wait_send()
        share = scalars[s, 0] + scalars[s, 1]
        if size == 4:
            share = (share + scalars[s, 2]) + scalars[s, 3]
        share = share[0:1, 0:1]
    energy = share * (1.0 / ENTRIES)
    energy_o[...] = jnp.broadcast_to(energy, (8, 128))

    steps = all_blocks(stepped, x, z, ag_send, ag_recv, None, CUT, True)
    for h in (0, 1):
        reduction.finish(h)
        here = pl.ds(h * HALF, HALF)
        mild = wide[b, here, :].astype(F32)
        own = mild + 0.5 * (energy * mild - (energy_col[here, :] * mild + total[here, :]))
        stepped[b, here, :] = own.astype(BF16)
        next(steps)
        exact[0, here, :] = own[:, :128]
        exact[1, here, :] = own[:, 128:]
    reduction.close()
    exact_send = push(exact.at[1 - c], exact_o.at[mine, :], end_send.at[0], end_recv.at[0], sib)
    exact_own = pltpu.make_async_copy(exact.at[c], exact_o.at[mine, :], own_sem.at[2])
    exact_send.start()
    exact_own.start()

    def out_block(i):
        return (
            push(stepped.at[i], stepped_o.at[c, i], st_send.at[i], st_recv.at[i], sib),
            pltpu.make_async_copy(stepped.at[i], stepped_o.at[c, i], st_own.at[i]),
        )

    gram[...] = jnp.zeros((SEC, SEC), F32)

    def add_group(group):
        def one_block(t, carry):
            i = group_block(group, t, x, z)
            value = stepped[i]
            for one in out_block(i):
                one.start()
            gram[...] += dot_t(value, value)
            return carry

        lax.fori_loop(0, GROUP_SIZE[group], one_block, 0)

    for ready in steps:
        if ready:
            add_group(ready)

    def root(d_ref, again):
        small[0] = gram[...].astype(BF16)
        my[...] = 1.5 * gram[...] - 0.5 * dot(small[0], small[0])
        small[1] = my[...].astype(BF16)
        value = 1.5 * my[...] - 0.5 * dot(small[0], small[1])
        mu[...] = value
        small[2] = value.astype(BF16)
        d_ref[...] = 0.25 * dot(small[2], small[0]) - 0.75 * (gram[...] + mu[...])
        if again:
            gram[...] = 1.5 * my[...] - 0.5 * dot(small[1], small[2])

    squares = jnp.sum(gram[...] * gram[...], axis=(0, 1), keepdims=True)
    scale_one = jnp.sqrt(squares * (1.0 / COLS) * (1.0 / COLS) + 1e-06)
    gram[...] = gram[...] * ((1.0 / COLS) / scale_one)
    root(mz, True)
    gram[...] = 2.25 * gram[...] + rough(mz[...], gram[...])
    scale_two = frobenius(gram[...])
    gram[...] = gram[...] * (1.0 / scale_two)
    root(mm, False)
    size = jnp.sqrt(scale_one) * jnp.sqrt(scale_two)
    over = 1.0 / size
    small[0] = mz[...].astype(BF16)
    root_copies = []
    for h in (0, 1):
        here = pl.ds(h * HALF, HALF)
        both = 2.25 * (mz[here, :] + mm[here, :]) + rough(mm[here, :], small[0])
        roots[here, :] = (both * over).astype(BF16)
        root_copies.append(push(roots.at[here, :], root_o.at[c, here, :], root_send.at[h], root_recv.at[h], sib))
        root_copies[h].start()
    level_two[...] = jnp.broadcast_to(2.25 * 2.25 / size, (8, 128))
    root_own = pltpu.make_async_copy(roots, root_o.at[c], own_sem.at[3])
    level_send = push(level_two, level_o.at[c], end_send.at[2], end_recv.at[2], sib)
    level_own = pltpu.make_async_copy(level_two, level_o.at[c], own_sem.at[4])
    level_send.start()
    level_own.start()
    root_own.start()

    def block_done(i, carry):
        going, staying = out_block(i)
        going.wait_send()
        staying.wait()
        push(stepped.at[i], stepped_o.at[1 - c, i], st_send.at[i], st_recv.at[i], sib).wait_recv()
        return carry

    lax.fori_loop(0, CHIPS, block_done, 0)
    exact_send.wait_send()
    exact_own.wait()
    push(exact.at[1 - c], exact_o.at[other, :], end_send.at[0], end_recv.at[0], sib).wait_recv()
    for one in root_copies:
        one.wait_send()
    root_own.wait()
    for h in (0, 1):
        here = pl.ds(h * HALF, HALF)
        push(roots.at[here, :], root_o.at[1 - c, here, :], root_send.at[h], root_recv.at[h], sib).wait_recv()
    level_send.wait_send()
    level_own.wait()
    push(level_two, level_o.at[1 - c], end_send.at[2], end_recv.at[2], sib).wait_recv()


def site(wave, row_ops, col_ops, count, source, target, energy_row):
    hbm = pl.BlockSpec(memory_space=pltpu.HBM)
    smem = pl.BlockSpec(memory_space=pltpu.SMEM)
    vmem = pl.BlockSpec(memory_space=pltpu.VMEM)
    square = pltpu.VMEM((SEC, SEC), F32)
    blocks = pltpu.VMEM((CHIPS, SEC, WIDE), BF16)
    dma = pltpu.SemaphoreType.DMA
    return pl.pallas_call(
        site_kernel,
        out_shape=(
            jax.ShapeDtypeStruct((2, CHIPS, SEC, WIDE), BF16),
            jax.ShapeDtypeStruct((2, SEC, SEC), BF16),
            jax.ShapeDtypeStruct((2, 8, 128), F32),
            jax.ShapeDtypeStruct((2 * SEC, 128), F32),
            jax.ShapeDtypeStruct((8, 128), F32),
        ),
        in_specs=[hbm] * 3 + [smem] * 3 + [vmem],
        out_specs=(hbm, hbm, hbm, hbm, vmem),
        scratch_shapes=[
            blocks,
            pltpu.VMEM((8, SEC, SEC), BF16),
            pltpu.VMEM((8, SEC, SEC), BF16),
            pltpu.VMEM((8, 128), jnp.int32),
            pltpu.VMEM((8, 128), jnp.int32),
            pltpu.SMEM((8, 128), jnp.int32),
            pltpu.SMEM((8,), jnp.int32),
            pltpu.SMEM((8,), jnp.int32),
            pltpu.VMEM((9, HALF, SEC), F32),
            pltpu.VMEM((4, 4, SEC, WIDE), BF16),
            pltpu.VMEM((2, 2, 2, 4, EIGHTH, WIDE), BF16),
            pltpu.VMEM((2, 2, 2, 4, QUARTER, WIDE), BF16),
            pltpu.VMEM((2, 2, 2, EIGHTH, WIDE), BF16),
            pltpu.VMEM((2, 2, 2, QUARTER, WIDE), BF16),
            pltpu.VMEM((SEC, WIDE), F32),
            blocks,
            square,
            square,
            square,
            square,
            square,
            pltpu.VMEM((3, SEC, SEC), BF16),
            pltpu.VMEM((SEC, SEC), BF16),
            pltpu.VMEM((8, 128), F32),
            pltpu.VMEM((2, SEC, 128), F32),
            pltpu.VMEM((4, 4, 8, 128), F32),
            pltpu.VMEM((SEC, 1), F32),
            dma((2, 32)),
            dma((2, 32)),
            dma((4,)),
            dma((4,)),
            dma((2, 2, 4)),
            dma((2, 2, 4)),
            dma((2, 2, 2, 4)),
            dma((2, 2, 2, 4)),
            dma((2, 2, 6)),
            dma((2, 2, 6)),
            dma((2, 32)),
            dma((2, 32)),
            dma((4, 4)),
            dma((4, 4)),
            dma((CHIPS,)),
            dma((CHIPS,)),
            dma((CHIPS,)),
            dma((3,)),
            dma((3,)),
            dma((2,)),
            dma((2,)),
            dma((7,)),
        ],
        compiler_params=pltpu.CompilerParams(
            collective_id=0, has_side_effects=True, vmem_limit_bytes=60 * MIB
        ),
        name="site",
    )(wave, row_ops, col_ops, count, source, target, energy_row)


def renorm_kernel(
    count, source, target, stepped, cols, root, level, exact, energy,
    out, wave_o, energy_o,
    block_v, cols_v, root_v, out_v, zero_v, exact_v, wave_v, level_v, block_sem, cols_sem, root_sem, out_sem, exact_sem, wave_sem, level_sem,
):
    energy_o[0] = energy[0, 0]

    def needs(k, s):
        pair = (source[k], target[k])
        return [
            pltpu.make_async_copy(
                stepped.at[s, pl.ds(2 * pair[e], 2)], block_v.at[k, s, e], block_sem.at[k, s, e]
            )
            for e in (0, 1)
        ]

    def column_op(k):
        return pltpu.make_async_copy(cols.at[k], cols_v.at[k], cols_sem.at[k])

    def result(k, s):
        return pltpu.make_async_copy(out_v.at[k, s], out.at[k, pl.ds(s * SEC, SEC), :], out_sem.at[k, s])

    def nothing(k, s):
        return pltpu.make_async_copy(zero_v, out.at[k, pl.ds(s * SEC, SEC), :], out_sem.at[k, s])

    roots = [pltpu.make_async_copy(root.at[s], root_v.at[s], root_sem.at[s]) for s in (0, 1)]
    load_level = pltpu.make_async_copy(level, level_v, level_sem)
    load_level.start()
    roots[0].start()
    for one in needs(0, 0):
        one.start()
    column_op(0).start()
    roots[1].start()
    for one in needs(0, 1):
        one.start()
    zero_v[...] = jnp.zeros_like(zero_v)
    load_exact = pltpu.make_async_copy(exact, exact_v, exact_sem)
    load_level.wait()
    roots[0].wait()

    def one_term(k, carry):
        column_op(k).wait()
        for s in (0, 1):
            scale = level_v[s, 0:1, 0:1]
            for one in needs(k, s):
                one.wait()
            if s == 0:

                @pl.when(k + 1 < count[0])
                def ahead():
                    column_op(k + 1).start()
                    for t in (0, 1):
                        for one in needs(k + 1, t):
                            one.start()

                @pl.when(k == 0)
                def others():
                    load_exact.start()
                    for empty in range(1, 4):

                        @pl.when(empty >= count[0])
                        def clear(empty=empty):
                            nothing(empty, 0).start()
                            nothing(empty, 1).start()
            else:

                @pl.when(k == 0)
                def second_root():
                    roots[1].wait()
            halves = []
            for e in (0, 1):
                block = jnp.concatenate([block_v[k, s, e, 0], block_v[k, s, e, 1]], axis=1)
                halves.append((scale * block.astype(F32) + dot(root_v[s], block)).astype(BF16))
            product = dot(halves[0], cols_v[k]).astype(BF16)
            out_v[k, s] = dot_t(product, halves[1]) * SEC ** (-0.5)
            result(k, s).start()
        return carry

    lax.fori_loop(0, count[0], one_term, 0)
    load_exact.wait()
    waves = []
    for s in (0, 1):
        rows = pl.ds(s * SEC, SEC)
        own = exact_v[rows, :]
        wave_v[rows, :] = level_v[s, 0:1, 0:1] * own + dot(root_v[s], own.astype(BF16))
        waves.append(pltpu.make_async_copy(wave_v.at[rows, :], wave_o.at[rows, :], wave_sem.at[s]))
        waves[s].start()
    for one in waves:
        one.wait()
    for k in range(4):
        for s in (0, 1):
            result(k, s).wait()


def renorm(count, source, target, stepped, cols, root, level, exact, energy):
    hbm = pl.BlockSpec(memory_space=pltpu.HBM)
    smem = pl.BlockSpec(memory_space=pltpu.SMEM)
    return pl.pallas_call(
        renorm_kernel,
        out_shape=(
            jax.ShapeDtypeStruct((4, 2 * SEC, SEC), F32),
            jax.ShapeDtypeStruct((2 * SEC, 128), F32),
            jax.ShapeDtypeStruct((1,), F32),
        ),
        in_specs=[smem] * 3 + [hbm] * 5 + [smem],
        out_specs=(hbm, hbm, smem),
        scratch_shapes=[
            pltpu.VMEM((4, 2, 2, 2, SEC, WIDE), BF16),
            pltpu.VMEM((4, SEC, SEC), BF16),
            pltpu.VMEM((2, SEC, SEC), BF16),
            pltpu.VMEM((4, 2, SEC, SEC), F32),
            pltpu.VMEM((SEC, SEC), F32),
            pltpu.VMEM((2 * SEC, 128), F32),
            pltpu.VMEM((2 * SEC, 128), F32),
            pltpu.VMEM((2, 8, 128), F32),
            pltpu.SemaphoreType.DMA((4, 2, 2)),
            pltpu.SemaphoreType.DMA((4,)),
            pltpu.SemaphoreType.DMA((2,)),
            pltpu.SemaphoreType.DMA((4, 2)),
            pltpu.SemaphoreType.DMA(()),
            pltpu.SemaphoreType.DMA((2,)),
            pltpu.SemaphoreType.DMA(()),
        ],
        compiler_params=pltpu.CompilerParams(vmem_limit_bytes=60 * MIB),
        name="renorm",
    )(count, source, target, stepped, cols, root, level, exact, energy)


def on_device(wave_in, row_energy, row_operators, column_operators, term_count, source, target):
    stepped, root, level, exact, energy = site(
        wave_in, row_operators, column_operators, term_count, source, target, row_energy.reshape(8, 128)
    )
    renormalized, wave_next, energy = renorm(
        term_count, source, target, stepped, column_operators, root, level, exact, energy
    )
    return (wave_next, renormalized, energy.reshape(()))


def solution(mesh):
    torus = Mesh(mesh.devices.reshape(4, 4, 2, mesh.shape["sec"]), ("x", "z", "core", "sec"))
    return jax.shard_map(
        on_device,
        mesh=torus,
        in_specs=(
            P("sec", OPS),
            P("sec"),
            P(OPS, "sec", None),
            P(OPS, None, None),
            P(OPS),
            P(OPS),
            P(OPS),
        ),
        out_specs=(P("sec", OPS), P(OPS, "sec", None), P()),
        check_vma=False,
    )
```
